128 devices in a mesh: dp: 32 (over z, y, core), table: 4 (over x).
Axes of the slice: x: 4, y: 4, z: 4, core: 2. Of those that a mesh axis runs over, the one named last changes fastest.
Arguments:
- table: bfloat16 [524288, 512], P(('dp', 'table')), may hold values from -12 to 12
- item_ids: int32 [32768], P(('dp', 'table')), may hold values from 0 to 524287, as said below
- negatives: int32 [128, 512], P('dp', 'table'), may hold values from 0 to 524287, as said below
- lengths: int32 [32, 4], P('dp'), may hold values from 1 to 512, 1024 in all within a row
- w_in: bfloat16 [4, 512, 512], P(None, None, 'table'), may hold values from -0.25 to 0.25
- w_out: bfloat16 [512, 512], P('table'), may hold values from -0.25 to 0.25
Outputs:
- grad_table: float32 [524288, 512], P(('dp', 'table'))
- grad_w_in: float32 [4, 512, 512], P(None, None, 'table')
- grad_w_out: float32 [512, 512], P('table')
The draws below stay inside these ranges and needn't reach their ends.
Inputs may be any that keep to these rules, and one draw needn't show every extreme that they name: `item_ids`: item i is row i % 4096 of the rows held by device i // 4096 in dp+table order. Of the 256 history ids of one device (aligned blocks of the list), at most 4 are held by any one device; in every block some device holds exactly 4, and one device, drawn from the seed, does so in every block. `negatives`: of the 512 negative ids on one device, at most 8 are held by any one device; in every device's shard some device holds exactly 8, the same one for all shards.
All inputs are finite; a program needn't handle non-finite values.
Results may differ from the reference program's by a relative error of at most 0.029.
Values may be sent and summed in bfloat16 or wider, within the bound.
A program may use at most 128 MiB of HBM per device.

```python
import math
import jax
import jax.numpy as jnp
import numpy as np
from jax import lax

D = 512
DH = 128
NEG = 512
ITEMS_DEV = 4096
TOK_DEV = 1024
USERS_DP = 4
HD = 512
OWNERS = 128
ITEMS = 524288
MOST = 512
CAPH = 4
CAPN = 8
N_DP = 32
N_TABLE = 4


def owned_ids(key, blocks, rows, bound, favored):

    def one_block(block_key):
        key_a, key_b, key_c = jax.random.split(block_key, 3)
        spread = jax.random.permutation(key_a, (OWNERS - 1) * bound)[:rows - bound].astype(jnp.int32)
        others = spread // bound
        others = others + (others >= favored).astype(jnp.int32)
        holders = jnp.concatenate([jnp.full((bound,), favored, jnp.int32), others])
        holders = jax.random.permutation(key_b, holders).astype(jnp.int32)
        local = jax.random.randint(key_c, (rows,), 0, ITEMS_DEV, jnp.int32)
        return holders * ITEMS_DEV + local
    return jax.vmap(one_block)(jax.random.split(key, blocks))


def draw_item_ids(key, part):
    key = jax.random.fold_in(key, 11)
    favored = jax.random.randint(jax.random.fold_in(key, 1), (), 0, OWNERS, jnp.int32)
    blocks = owned_ids(jax.random.fold_in(key, 2), OWNERS, TOK_DEV // N_TABLE, CAPH, favored)
    return blocks.reshape(-1).astype(jnp.int32)


def draw_negatives(key, part):
    key = jax.random.fold_in(key, 23)
    favored = jax.random.randint(jax.random.fold_in(key, 1), (), 0, OWNERS, jnp.int32)
    blocks = owned_ids(jax.random.fold_in(key, 2), OWNERS, USERS_DP * NEG // N_TABLE, CAPN, favored)
    shaped = blocks.reshape(N_DP, N_TABLE, USERS_DP, NEG // N_TABLE)
    return jnp.transpose(shaped, (0, 2, 1, 3)).reshape(N_DP * USERS_DP, NEG).astype(jnp.int32)


def draw_table(key, part):
    key = jax.random.fold_in(key, 5)
    key_a, key_b = jax.random.split(key, 2)
    base = jnp.clip(jax.random.normal(key_a, (ITEMS, D), jnp.float32), -6.0, 6.0)
    scale = jnp.exp(jax.random.uniform(key_b, (ITEMS, 1), jnp.float32, -0.69, 0.69))
    return jnp.clip(base * scale, -12.0, 12.0).astype(jnp.bfloat16)


def steps_of(rng, dims, cuts, smallest, high):
    def one(axis_at, blocks):
        heights = jax.random.uniform(jax.random.fold_in(jax.random.fold_in(rng, 6), axis_at), (blocks,), jnp.float32, smallest / len(cuts), high / len(cuts))
        return jnp.repeat(jnp.exp(heights), dims[axis_at] // blocks).reshape((-1,) + (1,) * (len(dims) - axis_at - 1))

    factor_of = one(*cuts[0])
    for cut in cuts[1:]:
        factor_of = factor_of * one(*cut)
    return factor_of


def profile(number_of, total, limit, skew):
    weights = [(1 << 20) // math.isqrt(standing ** skew) + 1 for standing in range(2, number_of + 1)]
    rest, counts = total - limit - (number_of - 1), [1] * (number_of - 1)
    while rest > 0:
        movable = [i for i in range(number_of - 1) if counts[i] < limit]
        pool, left = sum([weights[i] for i in movable]), rest
        for i in movable:
            more = min(limit - counts[i], max(1, left * weights[i] // pool), rest)
            counts[i] = counts[i] + more
            rest = rest - more
    return np.array([limit] + counts)


def ragged_sizes(stream_key, number_of, total, reach, slope):
    if number_of == 2:
        one = jax.random.randint(stream_key, (), max(1, total - reach), min(reach, total - 1) + 1)
        return jnp.stack([one, total - one])
    tallies = jnp.asarray(profile(number_of, total, reach, slope), jnp.int32)
    couples = (number_of - 1) // 2
    donor, sink = tallies[1:1 + 2 * couples:2], tallies[2:2 + 2 * couples:2]
    margin = jnp.minimum(donor - 1, reach - sink)
    moved = jax.random.randint(jax.random.fold_in(stream_key, 1), (couples,), 0, 1 << 20) % (margin + 1)
    tallies = tallies.at[1:1 + 2 * couples:2].set(donor - moved).at[2:2 + 2 * couples:2].set(sink + moved)
    return tallies[jax.random.permutation(jax.random.fold_in(stream_key, 2), number_of)]


def scatter_about(key, shape, scale, most, cuts=(), kind=jnp.bfloat16):
    level = steps_of(key, shape, cuts, -0.22, 0.18) if cuts else 1.0
    drawn = jax.random.normal(key, shape, jnp.float32) * scale * level
    return jnp.minimum(jnp.maximum(drawn, -most), most).astype(kind)


def setup_inputs(seed: int = 0) -> dict:
    splits = jax.random.split(jax.random.key(seed), 7)
    return {
        "table": draw_table(jax.random.fold_in(splits[6], 71), 0),
        "item_ids": draw_item_ids(jax.random.fold_in(splits[6], 71), 0),
        "negatives": draw_negatives(jax.random.fold_in(splits[6], 71), 0),
        "lengths": jax.vmap(lambda own: ragged_sizes(own, USERS_DP, TOK_DEV, MOST, 2))(jax.random.split(splits[3], N_DP)).reshape((N_DP, USERS_DP)).astype(jnp.int32),
        "w_in": scatter_about(splits[4], (4, D, HD), D ** -0.5, 0.25, ((2, 4),)),
        "w_out": scatter_about(splits[5], (HD, D), HD ** -0.5, 0.25, ((0, 4),)),
    }


epsilon = 1e-06
sharpness = 20.0

def layer_norm(values):
    center = values - lax.optimization_barrier(jnp.mean(values, axis=-1, keepdims=True))
    spread = lax.optimization_barrier(jnp.mean(center * center, axis=-1, keepdims=True))
    return center * lax.rsqrt(spread + epsilon)

def unit_rows(values):
    return values * lax.rsqrt(lax.optimization_barrier(jnp.sum(values * values, axis=-1, keepdims=True)) + epsilon)

def segments(user_lengths, count):
    ends = jnp.cumsum(user_lengths).astype(jnp.int32)
    places = jnp.arange(count, dtype=jnp.int32)
    segment = lax.optimization_barrier(jnp.sum((places[:, None] >= ends[None, :]).astype(jnp.int32), axis=1)).astype(jnp.int32)
    belongs = segment[:, None] == jnp.arange(user_lengths.shape[0], dtype=jnp.int32)[None, :]
    row_len = lax.optimization_barrier(jnp.sum(jnp.where(belongs, user_lengths[None, :].astype(jnp.float32), jnp.float32(0.0)), axis=1))
    return (segment, row_len)

def branch(emb_f, w_in_f, w_out_f, segment, row_len):
    count = emb_f.shape[0]
    normed = layer_norm(emb_f).astype(jnp.bfloat16)
    w_in_b = w_in_f.astype(jnp.bfloat16)
    proj = jax.nn.silu(jnp.einsum('td,jde->jte', normed.astype(jnp.float32), w_in_b.astype(jnp.float32))).astype(jnp.bfloat16)
    heads = proj.shape[2] // DH
    shaped = proj.reshape(4, count, heads, DH)
    gate_u, value, query, keys = (shaped[0], shaped[1], shaped[2], shaped[3])
    scores = jnp.einsum('qhd,khd->hqk', query.astype(jnp.float32), keys.astype(jnp.float32)) * DH ** (-0.5)
    places = jnp.arange(count, dtype=jnp.int32)
    visible = (segment[:, None] == segment[None, :]) & (places[None, :] <= places[:, None])
    weights = jnp.where(visible[None], jax.nn.silu(scores) / row_len[None, :, None], jnp.float32(0.0)).astype(jnp.bfloat16)
    mixed = jnp.einsum('hqk,khd->qhd', weights.astype(jnp.float32), value.astype(jnp.float32))
    gated = (layer_norm(mixed) * gate_u.astype(jnp.float32)).reshape(count, heads * DH).astype(jnp.bfloat16)
    return jnp.dot(gated, w_out_f.astype(jnp.bfloat16), preferred_element_type=jnp.float32)

def sampled_loss(y_rows, emb_f, neg_f, row_start, segment, col_user):
    rows = y_rows.shape[0]
    width = emb_f.shape[1]
    y_unit = unit_rows(y_rows).astype(jnp.bfloat16)
    e_unit = unit_rows(emb_f).astype(jnp.bfloat16)
    padded = jnp.concatenate([e_unit, jnp.zeros((1, width), jnp.bfloat16)], axis=0)
    following = lax.dynamic_slice_in_dim(padded, row_start + 1, rows, 0)
    seg_pad = jnp.concatenate([segment, jnp.full((1,), -1, jnp.int32)], axis=0)
    seg_next = lax.dynamic_slice_in_dim(seg_pad, row_start + 1, rows, 0)
    seg_here = lax.dynamic_slice_in_dim(segment, row_start, rows, 0)
    valid = seg_next == seg_here
    positive = sharpness * lax.optimization_barrier(jnp.sum(y_unit.astype(jnp.float32) * following.astype(jnp.float32), axis=-1))
    n_unit = unit_rows(neg_f).astype(jnp.bfloat16)
    negative = sharpness * lax.dot_general(y_unit, n_unit, (((1,), (1,)), ((), ())), preferred_element_type=jnp.float32)
    own = seg_here[:, None] == col_user[None, :]
    total = jnp.exp(positive) + lax.optimization_barrier(jnp.sum(jnp.where(own, jnp.exp(negative), jnp.float32(0.0)), axis=-1))
    return jnp.sum(jnp.where(valid, jnp.log(total) - positive, jnp.float32(0.0)))

def reference(table, item_ids, negatives, lengths, w_in, w_out):
    emb = jnp.take(table, item_ids, axis=0).astype(jnp.float32)
    neg = jnp.take(table, negatives.reshape(-1), axis=0).astype(jnp.float32)
    col_user = (jnp.arange(USERS_DP * NEG, dtype=jnp.int32) // NEG).astype(jnp.int32)

    def group_loss(emb_g, neg_g, len_g, w_in_f, w_out_f):
        segment, row_len = segments(len_g, TOK_DEV)
        out = emb_g + branch(emb_g, w_in_f, w_out_f, segment, row_len)
        return sampled_loss(out, emb_g, neg_g, jnp.zeros((), jnp.int32), segment, col_user)
    saved = jax.checkpoint(group_loss)

    def whole(emb_f, neg_f, w_in_f, w_out_f):

        def advance(carry, piece):
            return (carry + saved(piece[0], piece[1], piece[2], w_in_f, w_out_f), None)
        pieces = (emb_f.reshape(N_DP, TOK_DEV, D), neg_f.reshape(N_DP, USERS_DP * NEG, D), lengths)
        total, _ = lax.scan(advance, jnp.zeros((), jnp.float32), pieces)
        return total
    loss_sum, pullback = jax.vjp(whole, emb, neg, w_in.astype(jnp.float32), w_out.astype(jnp.float32))
    d_emb, d_neg, d_win, d_wout = pullback(jnp.ones((), jnp.float32))
    grad_table = jnp.zeros((ITEMS, D), jnp.float32).at[item_ids].add(d_emb).at[negatives.reshape(-1)].add(d_neg)
    return (grad_table, d_win, d_wout)
```

```python
import functools
import jax
import jax.numpy as jnp
from jax import lax
from jax.experimental import pallas as pl
from jax.experimental.pallas import tpu as pltpu
from jax.sharding import PartitionSpec as P

DH = 128
D = 512
CAP_H = 4
CAP_N = 8
OWNERS = 128
N_DP = 32
N_TABLE = 4
ROWS = 4096
BF = jnp.bfloat16
F32 = jnp.float32
MESH = pl.DeviceIdType.MESH

epsilon = 1e-06
sharpness = 20.0


def iota(shape, dim):
    return lax.broadcasted_iota(jnp.int32, shape, dim)


def one_zero(mask):
    return jnp.where(mask, 1.0, 0.0).astype(BF)


def mm(a, b):
    return lax.dot_general(a, b, (((1,), (0,)), ((), ())), preferred_element_type=F32)


def mm_nt(a, b):
    return lax.dot_general(a, b, (((1,), (1,)), ((), ())), preferred_element_type=F32)


def mm_tn(a, b):
    return lax.dot_general(a, b, (((0,), (0,)), ((), ())), preferred_element_type=F32)


def position():
    dp = lax.axis_index("dp")
    tx = lax.axis_index("table")
    return dp, tx


def partner(dp, tx, step):
    dx = lax.rem(step, 4)
    dc = lax.rem(lax.div(step, 4), 2)
    dy = lax.rem(lax.div(step, 8), 4)
    dz = lax.div(step, 32)
    c = lax.rem(lax.rem(dp, 2) + dc, 2)
    y = lax.rem(lax.rem(lax.div(dp, 2), 4) + dy, 4)
    z = lax.rem(lax.div(dp, 8) + dz, 4)
    x = lax.rem(tx + dx, 4)
    return z * 8 + y * 2 + c, x


def greet_all(barrier, dp, tx):
    def one(i, carry):
        pd, px = partner(dp, tx, i)
        pl.semaphore_signal(barrier, inc=1, device_id=(pd, px), device_id_type=MESH)
        return carry

    lax.fori_loop(1, OWNERS, one, 0)


def spread_all(src, dst, chunk, send_sem, recv_sem, dp, tx):
    me = dp * 4 + tx

    def one(i, carry):
        pd, px = partner(dp, tx, lax.rem(i * 37, OWNERS))
        pltpu.make_async_remote_copy(
            src_ref=src.at[pl.ds(pl.multiple_of((pd * 4 + px) * chunk, chunk), chunk)],
            dst_ref=dst.at[pl.ds(pl.multiple_of(me * chunk, chunk), chunk)],
            send_sem=send_sem,
            recv_sem=recv_sem,
            device_id=(pd, px),
            device_id_type=MESH,
        ).start()
        return carry

    lax.fori_loop(1, OWNERS, one, 0)
    own = pl.ds(pl.multiple_of(me * chunk, chunk), chunk)
    dst[own] = src[own]


def wait_rows(ref, count, sem):
    pltpu.make_async_copy(ref.at[pl.ds(0, count)], ref.at[pl.ds(0, count)], sem).wait()


class Ring:
    def __init__(self, dp, tx, send_sems, recv_sems):
        self.dp = dp
        self.tx = tx
        self.right = lax.rem(tx + 1, 4)
        self.left = lax.rem(tx + 3, 4)
        self.far = lax.rem(tx + 2, 4)
        self.send_sems = send_sems
        self.recv_sems = recv_sems

    def copy(self, src, dst, slot, to):
        return pltpu.make_async_remote_copy(
            src_ref=src,
            dst_ref=dst,
            send_sem=self.send_sems.at[slot],
            recv_sem=self.recv_sems.at[slot],
            device_id=(self.dp, to),
            device_id_type=MESH,
        )


class Gather:
    def __init__(self, ring, buf, block):
        h = block // 2
        r = ring

        def part(t, half):
            return buf.at[pl.ds(pl.multiple_of(t * block + half * h, h), h)]

        self.first = [
            r.copy(part(r.tx, 0), part(r.tx, 0), 0, r.right),
            r.copy(part(r.tx, 1), part(r.tx, 1), 1, r.left),
            r.copy(part(r.tx, 1), part(r.tx, 1), 2, r.right),
            r.copy(part(r.tx, 0), part(r.tx, 0), 3, r.left),
        ]
        self.second = [
            r.copy(part(r.left, 0), part(r.left, 0), 4, r.right),
            r.copy(part(r.right, 1), part(r.right, 1), 5, r.left),
        ]

    def start(self):
        for c in self.first:
            c.start()

    def forward(self):
        for c, d in zip(self.first[:2], self.second):
            c.wait_recv()
            d.start()

    def finish(self):
        for c in self.first[2:] + self.second:
            c.wait_recv()
        for c in self.first + self.second:
            c.wait_send()


class Scatter:
    def __init__(self, ring, part, land, onward, block):
        h = block // 2
        r = ring
        self.h = h
        self.ring = r
        self.part = part
        self.land = land
        self.onward = onward
        self.block = block

        self.first = [
            r.copy(self.at(r.far, 0), self.slot(0), 0, r.right),
            r.copy(self.at(r.far, 1), self.slot(1), 1, r.left),
            r.copy(self.at(r.right, 1), self.slot(2), 2, r.right),
            r.copy(self.at(r.left, 0), self.slot(3), 3, r.left),
        ]
        self.second = [
            r.copy(onward.at[pl.ds(0, h)], self.slot(4), 4, r.right),
            r.copy(onward.at[pl.ds(h, h)], self.slot(5), 5, r.left),
        ]

    def at(self, t, half):
        return self.part.at[self.span(t, half)]

    def span(self, t, half):
        return pl.ds(pl.multiple_of(t * self.block + half * self.h, self.h), self.h)

    def slot(self, i):
        return self.land.at[pl.ds(i * self.h, self.h)]

    def start(self):
        for c in self.first:
            c.start()

    def forward(self):
        h = self.h
        for i, t in enumerate((self.ring.right, self.ring.left)):
            self.first[i].wait_recv()
            self.onward[i * h : (i + 1) * h] = (
                self.land[i * h : (i + 1) * h].astype(F32) + self.part[self.span(t, i)].astype(F32)
            ).astype(BF)
            self.second[i].start()

    def finish(self):
        h = self.h
        for c in self.first[2:] + self.second:
            c.wait_recv()
        for c in self.first + self.second:
            c.wait_send()

        def got(i):
            return self.land[i * h : (i + 1) * h].astype(F32)

        return got(3) + got(4), got(2) + got(5)


def slots_of(ids):
    n = ids.shape[1]
    holder = lax.shift_right_logical(ids, 12)
    hits = iota((OWNERS, n), 0) == holder
    earlier = one_zero(iota((n, n), 0) < iota((n, n), 1))
    hits_b = one_zero(hits)
    before = jnp.sum(jnp.where(hits, mm(hits_b, earlier), 0.0), axis=0, keepdims=True)
    return holder, hits_b, before.astype(jnp.int32)


def wanted_rows(ids, hits_b, before, offset):
    n = ids.shape[1]
    marked = (ids & (ROWS - 1)) + 1
    chosen = iota((OWNERS, n), 0) == before + offset
    high = jnp.where(chosen, lax.shift_right_logical(marked, 6).astype(F32), 0.0).astype(BF)
    low = jnp.where(chosen, (marked & 63).astype(F32), 0.0).astype(BF)
    return 64.0 * mm_nt(hits_b, high) + mm_nt(hits_b, low)


def as_column(row):
    n = row.shape[1]
    wide = jnp.broadcast_to(row.astype(F32), (128, n))
    return jnp.transpose(wide)[:, 0:1].astype(jnp.int32)


def neg_row(negs_ref):
    return jnp.concatenate([negs_ref[u : u + 1, :] for u in range(4)], axis=1)


def part_mask(rows, width, per, parts):
    which = lax.rem(iota((rows, width), 0), 16) // per
    return [one_zero(which == c) for c in range(parts)]


def pick_parts(values, per, width):
    which = lax.div(lax.rem(iota((values.shape[0], width), 0), 16), per)
    out = values[:, 0:width]
    for c in range(1, values.shape[1] // width):
        out = jnp.where(which == c, values[:, c * width : (c + 1) * width], out)
    return out


def gather_rows(table, ids_col, out_ref, at):
    step = 512

    def one(i, total):
        base = pl.multiple_of(i * step, step)
        pick = one_zero(ids_col == iota((512, step), 1) + i * step)
        return total + mm(pick, table[pl.ds(base, step), :])

    total = lax.fori_loop(0, ROWS // step, one, jnp.zeros((512, D), F32))
    out_ref[at : at + 512, :] = total.astype(BF)


def spread_chunks(rows_ref, chunks_ref, at, cap):
    width = cap * 32
    block = 128 // cap
    many = block * 16
    r, q = iota((many, 128), 0), iota((many, 128), 1)
    fold = one_zero(
        (lax.rem(q, block) == lax.div(r, 16)) & (lax.div(q, block) == lax.rem(r, cap))
    )
    for b in range(cap):
        rows = jnp.concatenate(
            [
                rows_ref[at + k * 128 + b * block : at + k * 128 + (b + 1) * block, :]
                for k in range(cap)
            ],
            axis=0,
        )
        chunks_ref[b * many : (b + 1) * many, :] = pick_parts(mm(fold, rows), cap, width).astype(BF)


def unfold(chunks, per, parts):
    rows, width = chunks.shape
    masks = part_mask(rows, width, per, parts)
    return jnp.concatenate([chunks * m for m in masks], axis=1)


def take_slots(chunks_ref, slot_col, cap):
    n = slot_col.shape[0]
    total = jnp.zeros((n, D), F32)
    step = 512
    for i in range(OWNERS * 16 // step):
        r = iota((n, step), 1) + i * step
        key = lax.div(r, 16) * cap + lax.rem(r, cap)
        total = total + mm(
            one_zero(slot_col == key),
            unfold(chunks_ref[i * step : (i + 1) * step, :], cap, 16 // cap),
        )
    return total.astype(BF)


def put_slots(rows, slot_row, chunks_ref, cap):
    n = slot_row.shape[1]
    step = 512
    for i in range(OWNERS * 16 // step):
        r = iota((step, n), 0) + i * step
        key = lax.div(r, 16) * cap + lax.rem(r, cap)
        chunks_ref[i * step : (i + 1) * step, :] = pick_parts(
            mm(one_zero(slot_row == key), rows), cap, cap * 32
        ).astype(BF)


def fetch_kernel(
    ids_ref,
    negs_ref,
    table_hbm,
    emb_ref,
    neg_ref,
    arrived_ref,
    table_ref,
    request_ref,
    picked_ref,
    hist_out,
    neg_out,
    hist_in,
    neg_in,
    table_sem,
    all_send,
    all_recv,
    hist_ss,
    hist_rs,
    neg_ss,
    neg_rs,
):
    dp, tx = position()
    barrier = pltpu.get_barrier_semaphore()
    greet_all(barrier, dp, tx)
    load = pltpu.make_async_copy(table_hbm, table_ref, table_sem)
    load.start()

    ids, negs = ids_ref[...], neg_row(negs_ref)
    holder_h, hits_h, before_h = slots_of(ids)
    holder_n, hits_n, before_n = slots_of(negs)
    wanted = wanted_rows(ids, hits_h, before_h, 0) + wanted_rows(negs, hits_n, before_n, CAP_H)
    request_ref[:, 0, :] = wanted.astype(jnp.int32) - 1
    slot_h = as_column(holder_h * CAP_H + before_h)
    slot_n = as_column(holder_n * CAP_N + before_n)

    pl.semaphore_wait(barrier, OWNERS - 1)
    spread_all(request_ref, arrived_ref, 1, all_send.at[0], all_recv.at[0], dp, tx)
    load.wait()
    wait_rows(arrived_ref, OWNERS - 1, all_recv.at[0])

    arrived = arrived_ref[:, 0, :]
    columns = [arrived[:, k : k + 1] for k in range(CAP_H + CAP_N)]
    gather_rows(table_ref, jnp.concatenate(columns[0:4], axis=0), picked_ref, 0)
    spread_chunks(picked_ref, hist_out, 0, CAP_H)
    spread_all(hist_out, hist_in, 16, all_send.at[1], all_recv.at[1], dp, tx)
    gather_rows(table_ref, jnp.concatenate(columns[4:8], axis=0), picked_ref, 512)
    gather_rows(table_ref, jnp.concatenate(columns[8:12], axis=0), picked_ref, 1024)
    spread_chunks(picked_ref, neg_out, 512, CAP_N)
    spread_all(neg_out, neg_in, 16, all_send.at[2], all_recv.at[2], dp, tx)

    wait_rows(hist_in, (OWNERS - 1) * 16, all_recv.at[1])
    emb_ref[pl.ds(pl.multiple_of(tx * 256, 256), 256), :] = take_slots(hist_in, slot_h, CAP_H)
    hist = Gather(Ring(dp, tx, hist_ss, hist_rs), emb_ref, 256)
    hist.start()
    hist.forward()
    wait_rows(neg_in, (OWNERS - 1) * 16, all_recv.at[2])
    neg_ref[pl.ds(pl.multiple_of(tx * 512, 512), 512), :] = take_slots(neg_in, slot_n, CAP_N)
    negs_all = Gather(Ring(dp, tx, neg_ss, neg_rs), neg_ref, 512)
    negs_all.start()
    negs_all.forward()
    hist.finish()
    negs_all.finish()
    wait_rows(request_ref, OWNERS - 1, all_send.at[0])
    wait_rows(hist_out, (OWNERS - 1) * 16, all_send.at[1])
    wait_rows(neg_out, (OWNERS - 1) * 16, all_send.at[2])


VM = pl.BlockSpec(memory_space=pltpu.VMEM)
HB = pl.BlockSpec(memory_space=pl.ANY)


def fetch(ids, negs, table):
    sem = pltpu.SemaphoreType.DMA
    return pl.pallas_call(
        fetch_kernel,
        out_shape=[
            jax.ShapeDtypeStruct((1024, D), BF),
            jax.ShapeDtypeStruct((2048, D), BF),
            jax.ShapeDtypeStruct((OWNERS, 1, 128), jnp.int32),
        ],
        in_specs=[VM, VM, HB],
        out_specs=[VM, VM, VM],
        scratch_shapes=[
            pltpu.VMEM((ROWS, D), BF),
            pltpu.VMEM((OWNERS, 1, 128), jnp.int32),
            pltpu.VMEM((12 * OWNERS, D), BF),
            pltpu.VMEM((OWNERS * 16, 128), BF),
            pltpu.VMEM((OWNERS * 16, 256), BF),
            pltpu.VMEM((OWNERS * 16, 128), BF),
            pltpu.VMEM((OWNERS * 16, 256), BF),
            sem,
            sem((3,)),
            sem((3,)),
            sem((6,)),
            sem((6,)),
            sem((6,)),
            sem((6,)),
        ],
        compiler_params=pltpu.CompilerParams(
            collective_id=0, has_side_effects=True, vmem_limit_bytes=48 * 1024 * 1024
        ),
        name="fetch_rows",
    )(ids, negs, table)


def greet_dp(dp, tx, step):
    pd, _ = partner(dp, tx, step * 4)
    return pd


def return_kernel(
    ids_ref,
    negs_ref,
    emb_part,
    neg_part,
    weight_ref,
    hist_in,
    neg_in,
    weight_sum,
    hist_out,
    neg_out,
    emb_land,
    emb_on,
    neg_land,
    neg_on,
    weight_in,
    weight_mine,
    all_send,
    all_recv,
    emb_ss,
    emb_rs,
    neg_ss,
    neg_rs,
):
    dp, tx = position()
    barrier = pltpu.get_barrier_semaphore()
    greet_all(barrier, dp, tx)
    ids, negs = ids_ref[...], neg_row(negs_ref)
    holder_h, _, before_h = slots_of(ids)
    holder_n, _, before_n = slots_of(negs)
    slot_h = holder_h * CAP_H + before_h
    slot_n = holder_n * CAP_N + before_n
    pl.semaphore_wait(barrier, OWNERS - 1)

    neg_sum = Scatter(Ring(dp, tx, neg_ss, neg_rs), neg_part, neg_land, neg_on, 512)
    emb_sum = Scatter(Ring(dp, tx, emb_ss, emb_rs), emb_part, emb_land, emb_on, 256)
    emb_sum.start()
    neg_sum.start()

    piece = 80

    def out_piece(i, carry):
        pd = greet_dp(dp, tx, i)
        pltpu.make_async_remote_copy(
            src_ref=weight_ref.at[pl.ds(pl.multiple_of(pd * piece, 16), piece)],
            dst_ref=weight_in.at[pl.ds(pl.multiple_of(dp * piece, 16), piece)],
            send_sem=all_send.at[2],
            recv_sem=all_recv.at[2],
            device_id=(pd, tx),
            device_id_type=MESH,
        ).start()
        return carry

    emb_sum.forward()
    neg_sum.forward()
    lax.fori_loop(1, N_DP, out_piece, 0)
    own = pl.ds(pl.multiple_of(dp * piece, 16), piece)
    weight_in[own] = weight_ref[own]

    def block_sum(total, part_ref, block):
        first, second = total.finish()
        mine = part_ref[pl.ds(pl.multiple_of(tx * block, block), block), :].astype(F32)
        return (mine + jnp.concatenate([first, second], axis=0)).astype(BF)

    d_hist = block_sum(emb_sum, emb_part, 256)
    put_slots(d_hist, slot_h, hist_out, CAP_H)
    spread_all(hist_out, hist_in, 16, all_send.at[0], all_recv.at[0], dp, tx)
    d_neg = block_sum(neg_sum, neg_part, 512)
    put_slots(d_neg, slot_n, neg_out, CAP_N)
    spread_all(neg_out, neg_in, 16, all_send.at[1], all_recv.at[1], dp, tx)

    wait_rows(weight_in, (N_DP - 1) * piece, all_recv.at[2])
    total = weight_in[0:piece, :].astype(F32)
    for i in range(1, N_DP):
        total = total + weight_in[i * piece : (i + 1) * piece, :].astype(F32)
    weight_mine[...] = total.astype(BF)
    weight_sum[own] = total.astype(BF)

    def back_piece(i, carry):
        pd = greet_dp(dp, tx, i)
        pltpu.make_async_remote_copy(
            src_ref=weight_mine,
            dst_ref=weight_sum.at[pl.ds(pl.multiple_of(dp * piece, 16), piece)],
            send_sem=all_send.at[3],
            recv_sem=all_recv.at[3],
            device_id=(pd, tx),
            device_id_type=MESH,
        ).start()
        return carry

    lax.fori_loop(1, N_DP, back_piece, 0)
    wait_rows(hist_in, (OWNERS - 1) * 16, all_recv.at[0])
    wait_rows(neg_in, (OWNERS - 1) * 16, all_recv.at[1])
    wait_rows(weight_sum, (N_DP - 1) * piece, all_recv.at[3])
    wait_rows(hist_out, (OWNERS - 1) * 16, all_send.at[0])
    wait_rows(neg_out, (OWNERS - 1) * 16, all_send.at[1])
    wait_rows(weight_in, (N_DP - 1) * piece, all_send.at[2])
    wait_rows(weight_in, (N_DP - 1) * piece, all_send.at[3])


def give_back(ids, negs, emb_part, neg_part, weight):
    sem = pltpu.SemaphoreType.DMA
    return pl.pallas_call(
        return_kernel,
        out_shape=[
            jax.ShapeDtypeStruct((OWNERS * 16, 128), BF),
            jax.ShapeDtypeStruct((OWNERS * 16, 256), BF),
            jax.ShapeDtypeStruct((2560, 128), BF),
        ],
        in_specs=[VM] * 5,
        out_specs=[VM] * 3,
        scratch_shapes=[
            pltpu.VMEM((OWNERS * 16, 128), BF),
            pltpu.VMEM((OWNERS * 16, 256), BF),
            pltpu.VMEM((6 * 128, D), BF),
            pltpu.VMEM((2 * 128, D), BF),
            pltpu.VMEM((6 * 256, D), BF),
            pltpu.VMEM((2 * 256, D), BF),
            pltpu.VMEM((2560, 128), BF),
            pltpu.VMEM((80, 128), BF),
            sem((4,)),
            sem((4,)),
            sem((6,)),
            sem((6,)),
            sem((6,)),
            sem((6,)),
        ],
        compiler_params=pltpu.CompilerParams(
            collective_id=1, has_side_effects=True, vmem_limit_bytes=48 * 1024 * 1024
        ),
        name="return_rows",
    )(ids, negs, emb_part, neg_part, weight)


def gather_chunks(chunks_ref, rows_ref, at, cap):
    block = 128 // cap
    many = block * 16
    q, r = iota((128, many), 0), iota((128, many), 1)
    fold = one_zero(
        (lax.rem(q, block) == lax.div(r, 16)) & (lax.div(q, block) == lax.rem(r, cap))
    )
    for b in range(cap):
        wide = unfold(chunks_ref[b * many : (b + 1) * many, :], cap, 16 // cap)
        rows = mm(fold, wide).astype(BF)
        for k in range(cap):
            rows_ref[at + k * 128 + b * block : at + k * 128 + (b + 1) * block, :] = rows[
                k * block : (k + 1) * block
            ]


def add_kernel(arrived_ref, hist_ref, neg_ref, out_ref, rows_ref, ids_ref):
    tile = out_ref.shape[0]
    step = pl.program_id(0)

    @pl.when(step == 0)
    def _():
        gather_chunks(hist_ref, rows_ref, 0, CAP_H)
        gather_chunks(neg_ref, rows_ref, 512, CAP_N)
        ids_ref[...] = jnp.transpose(arrived_ref[:, 0, :].astype(F32)).astype(jnp.int32)

    total = jnp.zeros((tile, D), F32)
    for k in range(0, CAP_H + CAP_N, 4):
        row = jnp.concatenate([ids_ref[k + j : k + j + 1, :] for j in range(4)], axis=1)
        put = one_zero(row == iota((tile, 512), 0) + step * tile)
        total = total + mm(put, rows_ref[k * 128 : (k + 4) * 128, :])
    out_ref[...] = total


def add_rows(arrived, hist_in, neg_in):
    tile = 512
    return pl.pallas_call(
        add_kernel,
        out_shape=jax.ShapeDtypeStruct((ROWS, D), F32),
        grid=(ROWS // tile,),
        in_specs=[VM] * 3,
        out_specs=pl.BlockSpec((tile, D), lambda i: (i, 0)),
        scratch_shapes=[
            pltpu.VMEM((12 * OWNERS, D), BF),
            pltpu.VMEM((128, 128), jnp.int32),
        ],
        compiler_params=pltpu.CompilerParams(vmem_limit_bytes=32 * 1024 * 1024),
        name="add_rows",
    )(arrived, hist_in, neg_in)


def layer_norm(values):
    center = values - jnp.mean(values, axis=-1, keepdims=True)
    spread = jnp.mean(center * center, axis=-1, keepdims=True)
    return center * lax.rsqrt(spread + epsilon)


def unit_rows(values):
    return values * lax.rsqrt(jnp.sum(values * values, axis=-1, keepdims=True) + epsilon)


def segments(user_lengths, count):
    ends = jnp.cumsum(user_lengths)
    places = jnp.arange(count, dtype=jnp.int32)
    segment = jnp.sum((places[:, None] >= ends[None, :]).astype(jnp.int32), axis=1)
    belongs = segment[:, None] == jnp.arange(user_lengths.shape[0], dtype=jnp.int32)[None, :]
    row_len = jnp.sum(jnp.where(belongs, user_lengths[None, :].astype(jnp.float32), 0.0), axis=1)
    return (segment, row_len)


def branch(emb_f, w_in_f, w_out_f, segment, row_len):
    count = emb_f.shape[0]
    normed = layer_norm(emb_f).astype(jnp.bfloat16)
    w_in_b = w_in_f.astype(jnp.bfloat16)
    proj = jax.nn.silu(
        jnp.einsum("td,jde->jte", normed, w_in_b, preferred_element_type=jnp.float32)
    ).astype(jnp.bfloat16)
    heads = proj.shape[2] // DH
    shaped = proj.reshape(4, count, heads, DH)
    gate_u, value, query, keys = (shaped[0], shaped[1], shaped[2], shaped[3])
    scores = jnp.einsum("qhd,khd->hqk", query, keys, preferred_element_type=jnp.float32) * DH ** (
        -0.5
    )
    places = jnp.arange(count, dtype=jnp.int32)
    visible = (segment[:, None] == segment[None, :]) & (places[None, :] <= places[:, None])
    weights = jnp.where(visible[None], jax.nn.silu(scores) / row_len[None, :, None], 0.0).astype(
        jnp.bfloat16
    )
    mixed = jnp.einsum("hqk,khd->qhd", weights, value, preferred_element_type=jnp.float32)
    gated = (
        (layer_norm(mixed) * gate_u.astype(jnp.float32))
        .reshape(count, heads * DH)
        .astype(jnp.bfloat16)
    )
    return jnp.dot(gated, w_out_f.astype(jnp.bfloat16), preferred_element_type=jnp.float32)


def sampled_loss(y_rows, emb_f, neg_f, row_start, segment, col_user):
    rows = y_rows.shape[0]
    width = emb_f.shape[1]
    y_unit = unit_rows(y_rows).astype(jnp.bfloat16)
    e_unit = unit_rows(emb_f).astype(jnp.bfloat16)
    padded = jnp.concatenate([e_unit, jnp.zeros((1, width), jnp.bfloat16)], axis=0)
    following = lax.dynamic_slice_in_dim(padded, row_start + 1, rows, 0)
    seg_pad = jnp.concatenate([segment, jnp.full((1,), -1, jnp.int32)], axis=0)
    seg_next = lax.dynamic_slice_in_dim(seg_pad, row_start + 1, rows, 0)
    seg_here = lax.dynamic_slice_in_dim(segment, row_start, rows, 0)
    valid = seg_next == seg_here
    positive = sharpness * jnp.sum(
        y_unit.astype(jnp.float32) * following.astype(jnp.float32), axis=-1
    )
    n_unit = unit_rows(neg_f).astype(jnp.bfloat16)
    negative = sharpness * lax.dot_general(
        y_unit, n_unit, (((1,), (1,)), ((), ())), preferred_element_type=jnp.float32
    )
    own = seg_here[:, None] == col_user[None, :]
    total = jnp.exp(positive) + jnp.sum(jnp.where(own, jnp.exp(negative), 0.0), axis=-1)
    return jnp.sum(jnp.where(valid, jnp.log(total) - positive, 0.0))


def on_device(table, item_ids, negatives, lengths, w_in, w_out):
    neg_ids = negatives.reshape(-1)
    hist_count = item_ids.shape[0]
    neg_count = neg_ids.shape[0]
    table_count = lax.axis_size("table")
    ids_row = item_ids.reshape(1, hist_count)
    emb_all, neg_all, arrived = fetch(ids_row, negatives, table)
    count = emb_all.shape[0]
    segment, row_len = segments(lengths[0], count)
    my_index = lax.axis_index("table")
    row_start = my_index * hist_count
    per_user = negatives.shape[1]
    col_user = jnp.arange(table_count * neg_count, dtype=jnp.int32) % neg_count // per_user
    emb_f = emb_all.astype(jnp.float32)
    neg_f = neg_all.astype(jnp.float32)

    def heads_term(emb_in, w_in_f, w_out_f):
        return branch(emb_in, w_in_f, w_out_f, segment, row_len)

    partial_out, heads_pullback = jax.vjp(
        heads_term, emb_f, w_in.astype(jnp.float32), w_out.astype(jnp.float32)
    )
    y_share = lax.psum_scatter(
        partial_out.astype(jnp.bfloat16), "table", scatter_dimension=0, tiled=True
    ).astype(jnp.float32)
    y_rows = y_share + lax.dynamic_slice_in_dim(emb_f, row_start, hist_count, 0)

    def quarter_loss(y_in, emb_in, neg_in):
        return sampled_loss(y_in, emb_in, neg_in, row_start, segment, col_user)

    loss_part, loss_pullback = jax.vjp(quarter_loss, y_rows, emb_f, neg_f)
    d_rows, d_emb_loss, d_neg = loss_pullback(jnp.ones((), jnp.float32))
    d_out = lax.all_gather(d_rows.astype(jnp.bfloat16), "table", axis=0, tiled=True).astype(
        d_rows.dtype
    )
    d_emb_heads, d_win, d_wout = heads_pullback(d_out)
    residual = lax.dynamic_update_slice_in_dim(jnp.zeros_like(emb_f), d_rows, row_start, 0)
    d_emb = d_emb_heads + d_emb_loss + residual
    weight = jnp.concatenate(
        [
            d_win.astype(BF).reshape(2048, 128),
            d_wout.astype(BF).reshape(128, 4, 128).transpose(1, 0, 2).reshape(512, 128),
        ],
        axis=0,
    )
    hist_in, neg_in, weight_sum = give_back(
        ids_row, negatives, d_emb.astype(BF), d_neg.astype(BF), weight
    )
    grad_w_in = weight_sum[:2048].reshape(4, 512, 128).astype(F32)
    grad_w_out = (
        weight_sum[2048:].reshape(4, 128, 128).transpose(1, 0, 2).reshape(128, 512).astype(F32)
    )
    grad_table = add_rows(arrived, hist_in, neg_in)
    return (grad_table, grad_w_in, grad_w_out)


def solution(mesh):
    placed = (
        P(("dp", "table"), None),
        P(("dp", "table")),
        P("dp", "table"),
        P("dp", None),
        P(None, None, "table"),
        P("table", None),
    )
    return jax.shard_map(
        on_device,
        mesh=mesh,
        in_specs=placed,
        out_specs=(P(("dp", "table"), None), P(None, None, "table"), P("table", None)),
        check_vma=False,
    )
```

```python
import functools
import jax
import jax.numpy as jnp
from jax import lax
from jax.experimental import pallas as pl
from jax.experimental.pallas import tpu as pltpu
from jax.sharding import PartitionSpec as P

DH = 128
D = 512
CAP_H = 4
CAP_N = 8
OWNERS = 128
N_DP = 32
N_TABLE = 4
ROWS = 4096
BF = jnp.bfloat16
F32 = jnp.float32
MESH = pl.DeviceIdType.MESH

epsilon = 1e-06
sharpness = 20.0


def iota(shape, dim):
    return lax.broadcasted_iota(jnp.int32, shape, dim)


def one_zero(mask):
    return jnp.where(mask, 1.0, 0.0).astype(BF)


def mm(a, b):
    return lax.dot_general(a, b, (((1,), (0,)), ((), ())), preferred_element_type=F32)


def mm_nt(a, b):
    return lax.dot_general(a, b, (((1,), (1,)), ((), ())), preferred_element_type=F32)


def mm_tn(a, b):
    return lax.dot_general(a, b, (((0,), (0,)), ((), ())), preferred_element_type=F32)


def position():
    dp = lax.axis_index("dp")
    tx = lax.axis_index("table")
    return dp, tx


def partner(dp, tx, step):
    dx = lax.rem(step, 4)
    dc = lax.rem(lax.div(step, 4), 2)
    dy = lax.rem(lax.div(step, 8), 4)
    dz = lax.div(step, 32)
    c = lax.rem(lax.rem(dp, 2) + dc, 2)
    y = lax.rem(lax.rem(lax.div(dp, 2), 4) + dy, 4)
    z = lax.rem(lax.div(dp, 8) + dz, 4)
    x = lax.rem(tx + dx, 4)
    return z * 8 + y * 2 + c, x


def greet_all(barrier, dp, tx):
    def one(i, carry):
        pd, px = partner(dp, tx, i)
        pl.semaphore_signal(barrier, inc=1, device_id=(pd, px), device_id_type=MESH)
        return carry

    lax.fori_loop(1, OWNERS, one, 0)


def spread_all(src, dst, chunk, send_sem, recv_sem, dp, tx):
    me = dp * 4 + tx

    def one(i, carry):
        pd, px = partner(dp, tx, lax.rem(i * 37, OWNERS))
        pltpu.make_async_remote_copy(
            src_ref=src.at[pl.ds(pl.multiple_of((pd * 4 + px) * chunk, chunk), chunk)],
            dst_ref=dst.at[pl.ds(pl.multiple_of(me * chunk, chunk), chunk)],
            send_sem=send_sem,
            recv_sem=recv_sem,
            device_id=(pd, px),
            device_id_type=MESH,
        ).start()
        return carry

    lax.fori_loop(1, OWNERS, one, 0)
    own = pl.ds(pl.multiple_of(me * chunk, chunk), chunk)
    dst[own] = src[own]


def wait_rows(ref, count, sem):
    pltpu.make_async_copy(ref.at[pl.ds(0, count)], ref.at[pl.ds(0, count)], sem).wait()


class Ring:
    def __init__(self, dp, tx, send_sems, recv_sems):
        self.dp = dp
        self.tx = tx
        self.right = lax.rem(tx + 1, 4)
        self.left = lax.rem(tx + 3, 4)
        self.far = lax.rem(tx + 2, 4)
        self.send_sems = send_sems
        self.recv_sems = recv_sems

    def copy(self, src, dst, slot, to):
        return pltpu.make_async_remote_copy(
            src_ref=src,
            dst_ref=dst,
            send_sem=self.send_sems.at[slot],
            recv_sem=self.recv_sems.at[slot],
            device_id=(self.dp, to),
            device_id_type=MESH,
        )


class Gather:
    def __init__(self, ring, buf, block):
        h = block // 2
        r = ring

        def part(t, half):
            return buf.at[pl.ds(pl.multiple_of(t * block + half * h, h), h)]

        self.first = [
            r.copy(part(r.tx, 0), part(r.tx, 0), 0, r.right),
            r.copy(part(r.tx, 1), part(r.tx, 1), 1, r.left),
            r.copy(part(r.tx, 1), part(r.tx, 1), 2, r.right),
            r.copy(part(r.tx, 0), part(r.tx, 0), 3, r.left),
        ]
        self.second = [
            r.copy(part(r.left, 0), part(r.left, 0), 4, r.right),
            r.copy(part(r.right, 1), part(r.right, 1), 5, r.left),
        ]

    def start(self):
        for c in self.first:
            c.start()

    def forward(self):
        for c, d in zip(self.first[:2], self.second):
            c.wait_recv()
            d.start()

    def finish(self):
        for c in self.first[2:] + self.second:
            c.wait_recv()
        for c in self.first + self.second:
            c.wait_send()


class Scatter:
    def __init__(self, ring, part, land, onward, block):
        h = block // 2
        r = ring
        self.h = h
        self.ring = r
        self.part = part
        self.land = land
        self.onward = onward
        self.block = block

        self.first = [
            r.copy(self.at(r.far, 0), self.slot(0), 0, r.right),
            r.copy(self.at(r.far, 1), self.slot(1), 1, r.left),
            r.copy(self.at(r.right, 1), self.slot(2), 2, r.right),
            r.copy(self.at(r.left, 0), self.slot(3), 3, r.left),
        ]
        self.second = [
            r.copy(onward.at[pl.ds(0, h)], self.slot(4), 4, r.right),
            r.copy(onward.at[pl.ds(h, h)], self.slot(5), 5, r.left),
        ]

    def at(self, t, half):
        return self.part.at[self.span(t, half)]

    def span(self, t, half):
        return pl.ds(pl.multiple_of(t * self.block + half * self.h, self.h), self.h)

    def slot(self, i):
        return self.land.at[pl.ds(i * self.h, self.h)]

    def start(self):
        for c in self.first:
            c.start()

    def forward(self):
        h = self.h
        for i, t in enumerate((self.ring.right, self.ring.left)):
            self.first[i].wait_recv()
            self.onward[i * h : (i + 1) * h] = (
                self.land[i * h : (i + 1) * h].astype(F32) + self.part[self.span(t, i)].astype(F32)
            ).astype(BF)
            self.second[i].start()

    def finish(self):
        h = self.h
        for c in self.first[2:] + self.second:
            c.wait_recv()
        for c in self.first + self.second:
            c.wait_send()

        def got(i):
            return self.land[i * h : (i + 1) * h].astype(F32)

        return got(3) + got(4), got(2) + got(5)


def slots_of(ids):
    n = ids.shape[1]
    holder = lax.shift_right_logical(ids, 12)
    hits = iota((OWNERS, n), 0) == holder
    earlier = one_zero(iota((n, n), 0) < iota((n, n), 1))
    hits_b = one_zero(hits)
    before = jnp.sum(jnp.where(hits, mm(hits_b, earlier), 0.0), axis=0, keepdims=True)
    return holder, hits_b, before.astype(jnp.int32)


def wanted_rows(ids, hits_b, before, offset):
    n = ids.shape[1]
    marked = (ids & (ROWS - 1)) + 1
    chosen = iota((OWNERS, n), 0) == before + offset
    high = jnp.where(chosen, lax.shift_right_logical(marked, 6).astype(F32), 0.0).astype(BF)
    low = jnp.where(chosen, (marked & 63).astype(F32), 0.0).astype(BF)
    return 64.0 * mm_nt(hits_b, high) + mm_nt(hits_b, low)


def as_column(row):
    n = row.shape[1]
    wide = jnp.broadcast_to(row.astype(F32), (128, n))
    return jnp.transpose(wide)[:, 0:1].astype(jnp.int32)


def neg_row(negs_ref):
    return jnp.concatenate([negs_ref[u : u + 1, :] for u in range(4)], axis=1)


def part_mask(rows, width, per, parts):
    which = lax.rem(iota((rows, width), 0), 16) // per
    return [one_zero(which == c) for c in range(parts)]


def pick_parts(values, per, width):
    which = lax.div(lax.rem(iota((values.shape[0], width), 0), 16), per)
    out = values[:, 0:width]
    for c in range(1, values.shape[1] // width):
        out = jnp.where(which == c, values[:, c * width : (c + 1) * width], out)
    return out


def gather_rows(table, ids_col, out_ref, at):
    step = 512

    def one(i, total):
        base = pl.multiple_of(i * step, step)
        pick = one_zero(ids_col == iota((512, step), 1) + i * step)
        return total + mm(pick, table[pl.ds(base, step), :])

    total = lax.fori_loop(0, ROWS // step, one, jnp.zeros((512, D), F32))
    out_ref[at : at + 512, :] = total.astype(BF)


def spread_chunks(rows_ref, chunks_ref, at, cap):
    width = cap * 32
    block = 128 // cap
    many = block * 16
    r, q = iota((many, 128), 0), iota((many, 128), 1)
    fold = one_zero(
        (lax.rem(q, block) == lax.div(r, 16)) & (lax.div(q, block) == lax.rem(r, cap))
    )
    for b in range(cap):
        rows = jnp.concatenate(
            [
                rows_ref[at + k * 128 + b * block : at + k * 128 + (b + 1) * block, :]
                for k in range(cap)
            ],
            axis=0,
        )
        chunks_ref[b * many : (b + 1) * many, :] = pick_parts(mm(fold, rows), cap, width).astype(BF)


def unfold(chunks, per, parts):
    rows, width = chunks.shape
    masks = part_mask(rows, width, per, parts)
    return jnp.concatenate([chunks * m for m in masks], axis=1)


def take_slots(chunks_ref, slot_col, cap):
    n = slot_col.shape[0]
    total = jnp.zeros((n, D), F32)
    step = 512
    for i in range(OWNERS * 16 // step):
        r = iota((n, step), 1) + i * step
        key = lax.div(r, 16) * cap + lax.rem(r, cap)
        total = total + mm(
            one_zero(slot_col == key),
            unfold(chunks_ref[i * step : (i + 1) * step, :], cap, 16 // cap),
        )
    return total.astype(BF)


def put_slots(rows, slot_row, chunks_ref, cap):
    n = slot_row.shape[1]
    step = 512
    for i in range(OWNERS * 16 // step):
        r = iota((step, n), 0) + i * step
        key = lax.div(r, 16) * cap + lax.rem(r, cap)
        chunks_ref[i * step : (i + 1) * step, :] = pick_parts(
            mm(one_zero(slot_row == key), rows), cap, cap * 32
        ).astype(BF)


def row_sum(values):
    return jnp.sum(values, axis=-1, keepdims=True)


def row_mean(values):
    return jnp.mean(values, axis=-1, keepdims=True)


def normal(values):
    center = values - row_mean(values)
    factor = lax.rsqrt(row_mean(center * center) + epsilon)
    return center * factor, factor


def normal_back(grad, normed, factor):
    return factor * (grad - row_mean(grad) - normed * row_mean(grad * normed))


def unit_factor(values):
    return lax.rsqrt(row_sum(values * values) + epsilon)


def unit_back(grad, values, factor):
    return factor * (grad - values * (factor * factor * row_sum(grad * values)))


class Users:
    def __init__(self, lengths_ref):
        self.lengths = [lengths_ref[0, u] for u in range(4)]
        self.ends = []
        end = 0
        for length in self.lengths:
            end = end + length
            self.ends.append(end)

    def segment(self, t):
        return sum(jnp.where(t >= end, 1, 0) for end in self.ends)

    def start(self, t):
        return sum(jnp.where(t >= e, n, 0) for e, n in zip(self.ends, self.lengths))

    def length(self, t):
        out = jnp.where(t >= 0, self.lengths[0], 0)
        for u in range(1, 4):
            out = jnp.where(t >= self.ends[u - 1], self.lengths[u], out)
        return out


VM = pl.BlockSpec(memory_space=pltpu.VMEM)
HB = pl.BlockSpec(memory_space=pl.ANY)
SM = pl.BlockSpec(memory_space=pltpu.SMEM)
Q = 256
KEYS = 768
SCALE = DH**-0.5
PIECE = 80


def layer_kernel(
    ids_ref,
    negs_ref,
    lengths_ref,
    table_hbm,
    w_in_hbm,
    w_out_hbm,
    arrived_ref,
    hist_back,
    neg_back,
    weight_sum,
    table_ref,
    request_ref,
    picked_ref,
    hist_out,
    neg_out,
    hist_in,
    neg_in,
    w_in_ref,
    w_out_ref,
    emb_ref,
    unit_ref,
    normed_ref,
    proj_ref,
    slope_ref,
    weights_ref,
    dweights_ref,
    mixed_ref,
    factor_ref,
    gated_ref,
    part_ref,
    out_land,
    out_on,
    share_ref,
    dout_ref,
    dneg_ref,
    demb_ref,
    neg_land,
    neg_on,
    emb_land,
    emb_on,
    rest_ref,
    dgate_ref,
    dvalue_ref,
    dquery_ref,
    dkey_ref,
    dpre_ref,
    dwout_ref,
    weight_ref,
    weight_in,
    weight_mine,
    load_sems,
    all_send,
    all_recv,
    ring_send,
    ring_recv,
):
    dp, tx = position()
    barrier = pltpu.get_barrier_semaphore()
    greet_all(barrier, dp, tx)
    loads = [pltpu.make_async_copy(table_hbm, table_ref, load_sems.at[0])]
    for j in range(4):
        loads.append(
            pltpu.make_async_copy(
                w_in_hbm.at[j], w_in_ref.at[:, j * DH : (j + 1) * DH], load_sems.at[1 + j]
            )
        )
    loads.append(pltpu.make_async_copy(w_out_hbm, w_out_ref, load_sems.at[5]))
    for load in loads:
        load.start()

    def ring(i):
        return Ring(dp, tx, ring_send.at[i], ring_recv.at[i])

    right, left, far = ring(0).right, ring(0).left, ring(0).far

    def rows_of(b, n=Q):
        return pl.ds(pl.multiple_of(b * n, n), n)

    ids, negs = ids_ref[...], neg_row(negs_ref)
    holder_h, hits_h, before_h = slots_of(ids)
    holder_n, hits_n, before_n = slots_of(negs)
    wanted = wanted_rows(ids, hits_h, before_h, 0) + wanted_rows(negs, hits_n, before_n, CAP_H)
    request_ref[:, 0, :] = wanted.astype(jnp.int32) - 1
    slot_h = holder_h * CAP_H + before_h
    slot_n = holder_n * CAP_N + before_n
    slot_h_col, slot_n_col = as_column(slot_h), as_column(slot_n)
    users = Users(lengths_ref)

    pl.semaphore_wait(barrier, OWNERS - 1)
    spread_all(request_ref, arrived_ref, 1, all_send.at[0], all_recv.at[0], dp, tx)
    for load in loads:
        load.wait()
    wait_rows(arrived_ref, OWNERS - 1, all_recv.at[0])

    arrived = arrived_ref[:, 0, :]
    columns = [arrived[:, k : k + 1] for k in range(CAP_H + CAP_N)]
    gather_rows(table_ref, jnp.concatenate(columns[0:4], axis=0), picked_ref, 0)
    spread_chunks(picked_ref, hist_out, 0, CAP_H)
    spread_all(hist_out, hist_in, 16, all_send.at[1], all_recv.at[1], dp, tx)
    gather_rows(table_ref, jnp.concatenate(columns[4:8], axis=0), picked_ref, 512)
    gather_rows(table_ref, jnp.concatenate(columns[8:12], axis=0), picked_ref, 1024)
    spread_chunks(picked_ref, neg_out, 512, CAP_N)
    spread_all(neg_out, neg_in, 16, all_send.at[2], all_recv.at[2], dp, tx)

    wait_rows(hist_in, (OWNERS - 1) * 16, all_recv.at[1])
    emb_ref[rows_of(tx), :] = take_slots(hist_in, slot_h_col, CAP_H)
    hist = Gather(ring(0), emb_ref, Q)
    hist.start()

    def project(b):
        at = rows_of(b)
        normed = normal(emb_ref[at, :].astype(F32))[0].astype(BF)
        normed_ref[at, :] = normed
        pre = mm(normed, w_in_ref[...])
        gate = lax.logistic(pre)
        proj_ref[at, :] = (pre * gate).astype(BF)
        slope_ref[at, :] = gate * (1.0 + pre * (1.0 - gate))

    project(tx)
    hist.forward()
    for c in hist.first[2:]:
        c.wait_recv()
    project(left)
    project(right)
    for c in hist.second:
        c.wait_recv()
    project(far)

    wait_rows(neg_in, (OWNERS - 1) * 16, all_recv.at[2])
    neg_f = take_slots(neg_in, slot_n_col, CAP_N).astype(F32)
    neg_factor = unit_factor(neg_f)
    unit_ref[rows_of(tx, 512), :] = (neg_f * neg_factor).astype(BF)
    units = Gather(ring(1), unit_ref, 512)
    units.start()

    def keys_of(b):
        return pl.ds(pl.multiple_of(lax.div(b, 3) * Q, Q), KEYS)

    def attend(b):
        at, kr = rows_of(b), keys_of(b)
        scores = mm_nt(proj_ref[at, 256:384], proj_ref[kr, 384:512]) * SCALE
        t = iota((Q, 1), 0) + b * Q
        s = iota((Q, KEYS), 1) + lax.div(b, 3) * Q
        seen = (s <= t) & (s >= users.start(t))
        share = 1.0 / users.length(t).astype(F32)
        gate = lax.logistic(scores)
        weights = jnp.where(seen, scores * gate * share, 0.0).astype(BF)
        weights_ref[at, :] = weights
        dweights_ref[at, :] = jnp.where(
            seen, gate * (1.0 + scores * (1.0 - gate)) * (share * SCALE), 0.0
        )
        mixed, factor = normal(mm(weights, proj_ref[kr, 128:256]))
        mixed_ref[at, :] = mixed
        factor_ref[at, :] = jnp.broadcast_to(factor, (Q, DH))
        gated = (mixed * proj_ref[at, 0:128].astype(F32)).astype(BF)
        gated_ref[at, :] = gated
        part_ref[at, :] = mm(gated, w_out_ref[...]).astype(BF)

    out_sum = Scatter(ring(2), part_ref, out_land, out_on, Q)
    attend(far)
    out_sum.first[0].start()
    out_sum.first[1].start()
    attend(right)
    out_sum.first[2].start()
    attend(left)
    out_sum.first[3].start()
    units.forward()
    out_sum.forward()
    attend(tx)
    emb_f = emb_ref[rows_of(tx), :].astype(F32)
    first, second = out_sum.finish()
    y = emb_f + part_ref[rows_of(tx), :].astype(F32) + jnp.concatenate([first, second], axis=0)

    y_factor = unit_factor(y)
    y_unit = (y * y_factor).astype(BF)
    last = iota((Q, 1), 0) == Q - 1
    follow = jnp.where(
        last,
        emb_ref[rows_of(right), :].astype(F32)[0:1, :],
        pltpu.roll(emb_f, Q - 1, 0),
    )
    follow_factor = unit_factor(follow)
    follow_unit = (follow * follow_factor).astype(BF).astype(F32)
    y_unit_f = y_unit.astype(F32)
    t = iota((Q, 1), 0) + tx * Q
    segment = users.segment(t)
    valid = users.segment(t + 1) == segment
    grown_pos = jnp.exp(sharpness * row_sum(y_unit_f * follow_unit))
    total = grown_pos
    mine = [jnp.where(segment == u, 1.0, 0.0) for u in range(4)]
    units.finish()
    for c in range(4):
        grown = jnp.exp(sharpness * mm_nt(y_unit, unit_ref[c * 512 : (c + 1) * 512, :]))
        grown = jnp.concatenate(
            [grown[:, u * 128 : (u + 1) * 128] * mine[u] for u in range(4)], axis=1
        )
        total = total + row_sum(grown)
        share_ref[c] = grown
    scaled = jnp.where(valid, sharpness / total, 0.0)
    d_pos = jnp.where(valid, sharpness * (grown_pos / total - 1.0), 0.0)
    d_unit = d_pos * follow_unit
    for c in range(4):
        d_unit = d_unit + mm(
            (share_ref[c] * scaled).astype(BF), unit_ref[c * 512 : (c + 1) * 512, :]
        )
    d_rows = unit_back(d_unit, y, y_factor)
    dout_ref[rows_of(tx), :] = d_rows.astype(BF)
    douts = Gather(ring(3), dout_ref, Q)
    douts.start()
    neg_sum = Scatter(ring(4), dneg_ref, neg_land, neg_on, 512)

    def neg_grads(b):
        dneg_ref[rows_of(b, 512), :] = mm_tn((share_ref[b] * scaled).astype(BF), y_unit).astype(BF)

    neg_grads(far)
    d_follow = unit_back(d_pos * y_unit_f, follow, follow_factor)
    rest_ref[0:Q, :] = d_rows + jnp.where(t == tx * Q, 0.0, pltpu.roll(d_follow, 1, 0))
    rest_ref[Q : Q + 8, :] = jnp.where(iota((8, 1), 0) == 0, d_follow[Q - 1 : Q, :], 0.0)
    douts.forward()
    neg_sum.first[0].start()
    neg_sum.first[1].start()
    neg_grads(right)
    neg_sum.first[2].start()
    neg_grads(left)
    neg_sum.first[3].start()
    neg_grads(tx)

    dkey_ref[...] = jnp.zeros_like(dkey_ref)
    dvalue_ref[...] = jnp.zeros_like(dvalue_ref)
    dwout_ref[...] = jnp.zeros_like(dwout_ref)

    def attend_back(b):
        at, kr = rows_of(b), keys_of(b)
        d_out = dout_ref[at, :]
        d_gated = mm_nt(d_out, w_out_ref[...]).astype(BF).astype(F32)
        dwout_ref[...] += mm_tn(gated_ref[at, :], d_out)
        mixed = mixed_ref[at, :]
        dgate_ref[at, :] = (d_gated * mixed).astype(BF)
        d_mixed = normal_back(
            d_gated * proj_ref[at, 0:128].astype(F32), mixed, factor_ref[at, :][:, 0:1]
        ).astype(BF)
        d_scores = (mm_nt(d_mixed, proj_ref[kr, 128:256]) * dweights_ref[at, :]).astype(BF)
        dquery_ref[at, :] = mm(d_scores, proj_ref[kr, 384:512]).astype(BF)
        dkey_ref[kr, :] += mm_tn(d_scores, proj_ref[at, 256:384])
        dvalue_ref[kr, :] += mm_tn(weights_ref[at, :], d_mixed)

    attend_back(tx)
    for c in douts.first[2:]:
        c.wait_recv()
    attend_back(left)
    attend_back(right)
    neg_sum.forward()
    for c in douts.second:
        c.wait_recv()
    attend_back(far)

    def project_back(b):
        at = rows_of(b)
        d_proj = jnp.concatenate(
            [
                dgate_ref[at, :].astype(F32),
                dvalue_ref[at, :].astype(BF).astype(F32),
                dquery_ref[at, :].astype(F32),
                dkey_ref[at, :].astype(BF).astype(F32),
            ],
            axis=1,
        )
        d_pre = (d_proj * slope_ref[at, :]).astype(BF)
        dpre_ref[at, :] = d_pre
        normed, factor = normal(emb_ref[at, :].astype(F32))
        return normal_back(mm_nt(d_pre, w_in_ref[...]).astype(BF).astype(F32), normed, factor)

    emb_sum = Scatter(ring(5), demb_ref, emb_land, emb_on, Q)
    demb_ref[rows_of(far), :] = project_back(far).astype(BF)
    emb_sum.first[0].start()
    emb_sum.first[1].start()
    d_right = project_back(right)
    demb_ref[rows_of(right), :] = (
        d_right + jnp.where(iota((Q, 1), 0) == 0, rest_ref[Q : Q + 1, :], 0.0)
    ).astype(BF)
    emb_sum.first[2].start()
    demb_ref[rows_of(left), :] = project_back(left).astype(BF)
    emb_sum.first[3].start()
    rest_ref[0:Q, :] += project_back(tx)
    emb_sum.forward()

    d_win = mm_tn(normed_ref[...], dpre_ref[...]).astype(BF)
    for j in range(4):
        weight_ref[j * D : (j + 1) * D, :] = d_win[:, j * DH : (j + 1) * DH]
        weight_ref[2048 + j * DH : 2048 + (j + 1) * DH, :] = dwout_ref[
            :, j * DH : (j + 1) * DH
        ].astype(BF)
    own = pl.ds(pl.multiple_of(dp * PIECE, 16), PIECE)

    def out_piece(i, carry):
        pd, _ = partner(dp, tx, i * 4)
        pltpu.make_async_remote_copy(
            src_ref=weight_ref.at[pl.ds(pl.multiple_of(pd * PIECE, 16), PIECE)],
            dst_ref=weight_in.at[own],
            send_sem=all_send.at[5],
            recv_sem=all_recv.at[5],
            device_id=(pd, tx),
            device_id_type=MESH,
        ).start()
        return carry

    def back_piece(i, carry):
        pd, _ = partner(dp, tx, i * 4)
        pltpu.make_async_remote_copy(
            src_ref=weight_mine,
            dst_ref=weight_sum.at[own],
            send_sem=all_send.at[6],
            recv_sem=all_recv.at[6],
            device_id=(pd, tx),
            device_id_type=MESH,
        ).start()
        return carry

    first, second = emb_sum.finish()
    d_hist = rest_ref[0:Q, :] + jnp.concatenate([first, second], axis=0)
    wait_rows(hist_out, (OWNERS - 1) * 16, all_send.at[1])
    put_slots(d_hist.astype(BF), slot_h, hist_out, CAP_H)
    spread_all(hist_out, hist_back, 16, all_send.at[3], all_recv.at[3], dp, tx)

    first, second = neg_sum.finish()
    d_neg = dneg_ref[rows_of(tx, 512), :].astype(F32) + jnp.concatenate([first, second], axis=0)
    wait_rows(neg_out, (OWNERS - 1) * 16, all_send.at[2])
    put_slots(unit_back(d_neg, neg_f, neg_factor).astype(BF), slot_n, neg_out, CAP_N)
    spread_all(neg_out, neg_back, 16, all_send.at[4], all_recv.at[4], dp, tx)

    lax.fori_loop(1, N_DP, out_piece, 0)
    weight_in[own] = weight_ref[own]
    wait_rows(weight_in, (N_DP - 1) * PIECE, all_recv.at[5])
    total = weight_in[0:PIECE, :].astype(F32)
    for i in range(1, N_DP):
        total = total + weight_in[i * PIECE : (i + 1) * PIECE, :].astype(F32)
    weight_mine[...] = total.astype(BF)
    weight_sum[own] = total.astype(BF)
    lax.fori_loop(1, N_DP, back_piece, 0)

    wait_rows(hist_back, (OWNERS - 1) * 16, all_recv.at[3])
    wait_rows(neg_back, (OWNERS - 1) * 16, all_recv.at[4])
    wait_rows(weight_sum, (N_DP - 1) * PIECE, all_recv.at[6])
    for c in hist.first + hist.second + douts.first + douts.second:
        c.wait_send()
    wait_rows(request_ref, OWNERS - 1, all_send.at[0])
    wait_rows(hist_out, (OWNERS - 1) * 16, all_send.at[3])
    wait_rows(neg_out, (OWNERS - 1) * 16, all_send.at[4])
    wait_rows(weight_in, (N_DP - 1) * PIECE, all_send.at[5])
    wait_rows(weight_in, (N_DP - 1) * PIECE, all_send.at[6])


def layer(ids, negs, lengths, table, w_in, w_out):
    sem = pltpu.SemaphoreType.DMA
    vm = pltpu.VMEM
    return pl.pallas_call(
        layer_kernel,
        out_shape=[
            jax.ShapeDtypeStruct((OWNERS, 1, 128), jnp.int32),
            jax.ShapeDtypeStruct((OWNERS * 16, 128), BF),
            jax.ShapeDtypeStruct((OWNERS * 16, 256), BF),
            jax.ShapeDtypeStruct((2560, 128), BF),
        ],
        in_specs=[VM, VM, SM, HB, HB, HB],
        out_specs=[VM] * 4,
        scratch_shapes=[
            vm((ROWS, D), BF),
            vm((OWNERS, 1, 128), jnp.int32),
            vm((12 * OWNERS, D), BF),
            vm((OWNERS * 16, 128), BF),
            vm((OWNERS * 16, 256), BF),
            vm((OWNERS * 16, 128), BF),
            vm((OWNERS * 16, 256), BF),
            vm((D, D), BF),
            vm((DH, D), BF),
            vm((1024, D), BF),
            vm((2048, D), BF),
            vm((1024, D), BF),
            vm((1024, D), BF),
            vm((1024, D), F32),
            vm((1024, KEYS), BF),
            vm((1024, KEYS), F32),
            vm((1024, DH), F32),
            vm((1024, DH), F32),
            vm((1024, DH), BF),
            vm((1024, D), BF),
            vm((6 * 128, D), BF),
            vm((2 * 128, D), BF),
            vm((4, Q, 512), F32),
            vm((1024, D), BF),
            vm((2048, D), BF),
            vm((1024, D), BF),
            vm((6 * 256, D), BF),
            vm((2 * 256, D), BF),
            vm((6 * 128, D), BF),
            vm((2 * 128, D), BF),
            vm((Q + 8, D), F32),
            vm((1024, DH), BF),
            vm((1024, DH), F32),
            vm((1024, DH), BF),
            vm((1024, DH), F32),
            vm((1024, D), BF),
            vm((DH, D), F32),
            vm((2560, 128), BF),
            vm((2560, 128), BF),
            vm((PIECE, 128), BF),
            sem((6,)),
            sem((7,)),
            sem((7,)),
            sem((6, 6)),
            sem((6, 6)),
        ],
        compiler_params=pltpu.CompilerParams(
            collective_id=0, has_side_effects=True, vmem_limit_bytes=56 * 1024 * 1024
        ),
        name="layer",
    )(ids, negs, lengths, table, w_in, w_out)


def gather_chunks(chunks_ref, rows_ref, at, cap):
    block = 128 // cap
    many = block * 16
    q, r = iota((128, many), 0), iota((128, many), 1)
    fold = one_zero(
        (lax.rem(q, block) == lax.div(r, 16)) & (lax.div(q, block) == lax.rem(r, cap))
    )
    for b in range(cap):
        wide = unfold(chunks_ref[b * many : (b + 1) * many, :], cap, 16 // cap)
        rows = mm(fold, wide).astype(BF)
        for k in range(cap):
            rows_ref[at + k * 128 + b * block : at + k * 128 + (b + 1) * block, :] = rows[
                k * block : (k + 1) * block
            ]


def add_kernel(arrived_ref, hist_ref, neg_ref, out_ref, rows_ref, ids_ref):
    tile = out_ref.shape[0]
    step = pl.program_id(0)

    @pl.when(step == 0)
    def _():
        gather_chunks(hist_ref, rows_ref, 0, CAP_H)
        gather_chunks(neg_ref, rows_ref, 512, CAP_N)
        ids_ref[...] = jnp.transpose(arrived_ref[:, 0, :].astype(F32)).astype(jnp.int32)

    total = jnp.zeros((tile, D), F32)
    for k in range(0, CAP_H + CAP_N, 4):
        row = jnp.concatenate([ids_ref[k + j : k + j + 1, :] for j in range(4)], axis=1)
        put = one_zero(row == iota((tile, 512), 0) + step * tile)
        total = total + mm(put, rows_ref[k * 128 : (k + 4) * 128, :])
    out_ref[...] = total


def add_rows(arrived, hist_in, neg_in):
    tile = 512
    return pl.pallas_call(
        add_kernel,
        out_shape=jax.ShapeDtypeStruct((ROWS, D), F32),
        grid=(ROWS // tile,),
        in_specs=[VM] * 3,
        out_specs=pl.BlockSpec((tile, D), lambda i: (i, 0)),
        scratch_shapes=[
            pltpu.VMEM((12 * OWNERS, D), BF),
            pltpu.VMEM((128, 128), jnp.int32),
        ],
        compiler_params=pltpu.CompilerParams(vmem_limit_bytes=32 * 1024 * 1024),
        name="add_rows",
    )(arrived, hist_in, neg_in)


def on_device(table, item_ids, negatives, lengths, w_in, w_out):
    arrived, hist_back, neg_back, weight_sum = layer(
        item_ids.reshape(1, -1), negatives, lengths, table, w_in, w_out
    )
    grad_w_in = weight_sum[:2048].reshape(4, D, DH).astype(F32)
    grad_w_out = weight_sum[2048:].reshape(4, DH, DH).transpose(1, 0, 2).reshape(DH, D).astype(F32)
    grad_table = add_rows(arrived, hist_back, neg_back)
    return (grad_table, grad_w_in, grad_w_out)


def solution(mesh):
    placed = (
        P(("dp", "table"), None),
        P(("dp", "table")),
        P("dp", "table"),
        P("dp", None),
        P(None, None, "table"),
        P("table", None),
    )
    return jax.shard_map(
        on_device,
        mesh=mesh,
        in_specs=placed,
        out_specs=(P(("dp", "table"), None), P(None, None, "table"), P("table", None)),
        check_vma=False,
    )
```

```python
import functools
import jax
import jax.numpy as jnp
from jax import lax
from jax.experimental import pallas as pl
from jax.experimental.pallas import tpu as pltpu
from jax.sharding import PartitionSpec as P

DH = 128
D = 512
CAP_H = 4
CAP_N = 8
OWNERS = 128
N_DP = 32
N_TABLE = 4
ROWS = 4096
BF = jnp.bfloat16
F32 = jnp.float32
MESH = pl.DeviceIdType.MESH

epsilon = 1e-06
sharpness = 20.0


def iota(shape, dim):
    return lax.broadcasted_iota(jnp.int32, shape, dim)


def one_zero(mask):
    return jnp.where(mask, 1.0, 0.0).astype(BF)


def mm(a, b):
    return lax.dot_general(a, b, (((1,), (0,)), ((), ())), preferred_element_type=F32)


def mm_nt(a, b):
    return lax.dot_general(a, b, (((1,), (1,)), ((), ())), preferred_element_type=F32)


def mm_tn(a, b):
    return lax.dot_general(a, b, (((0,), (0,)), ((), ())), preferred_element_type=F32)


def position():
    dp = lax.axis_index("dp")
    tx = lax.axis_index("table")
    return dp, tx


def coordinates(dp, tx):
    z, y, c = lax.div(dp, 8), lax.rem(lax.div(dp, 2), 4), lax.rem(dp, 2)
    near = [(core, lax.rem(tx + dx, 4)) for core in (1 - c, c) for dx in range(4)]
    return z, y, near[4:] + near[:4]


def plane_base(z, y, step):
    return lax.rem(z + lax.div(step, 4), 4) * 8 + lax.rem(y + lax.rem(step, 4), 4) * 2


def each_partner(dp, tx, do):
    z, y, near = coordinates(dp, tx)

    def one(i, carry):
        base = plane_base(z, y, lax.rem(i * 7, 16))
        for core, x in near:
            do(base + core, x)
        return carry

    lax.fori_loop(1, 16, one, 0)
    for core, x in near[1:]:
        do(z * 8 + y * 2 + core, x)


def each_dp(dp, tx, do):
    z, y, near = coordinates(dp, tx)
    mine, other = near[0][0], near[4][0]

    def one(i, carry):
        base = plane_base(z, y, lax.rem(i * 7, 16))
        do(base + mine)
        do(base + other)
        return carry

    lax.fori_loop(1, 16, one, 0)
    do(z * 8 + y * 2 + other)


def signal(sem, dp, x):
    pl.semaphore_signal(sem, inc=1, device_id=(dp, x), device_id_type=MESH)


def greet_planes(barrier, dp, tx):
    z, y, near = coordinates(dp, tx)
    for core, x in near[1:]:
        signal(barrier, z * 8 + y * 2 + core, x)
    core, x = near[0]
    for i in range(1, 16):
        signal(barrier, plane_base(z, y, i) + core, x)


def greet_again(sem, dp, tx):
    z, y, near = coordinates(dp, tx)
    for core, x in near[1:]:
        signal(sem, z * 8 + y * 2 + core, x)


def spread_all(src, dst, chunk, send_sem, recv_sem, dp, tx):
    me = dp * 4 + tx
    land = pl.ds(pl.multiple_of(me * chunk, chunk), chunk)

    def one(pd, px):
        pltpu.make_async_remote_copy(
            src_ref=src.at[pl.ds(pl.multiple_of((pd * 4 + px) * chunk, chunk), chunk)],
            dst_ref=dst.at[land],
            send_sem=send_sem,
            recv_sem=recv_sem,
            device_id=(pd, px),
            device_id_type=MESH,
        ).start()

    each_partner(dp, tx, one)
    dst[land] = src[land]


def wait_rows(ref, count, sem):
    pltpu.make_async_copy(ref.at[pl.ds(0, count)], ref.at[pl.ds(0, count)], sem).wait()


class Ring:
    def __init__(self, dp, tx, send_sems, recv_sems):
        self.dp = dp
        self.tx = tx
        self.right = lax.rem(tx + 1, 4)
        self.left = lax.rem(tx + 3, 4)
        self.far = lax.rem(tx + 2, 4)
        self.send_sems = send_sems
        self.recv_sems = recv_sems

    def copy(self, src, dst, slot, to):
        return pltpu.make_async_remote_copy(
            src_ref=src,
            dst_ref=dst,
            send_sem=self.send_sems.at[slot],
            recv_sem=self.recv_sems.at[slot],
            device_id=(self.dp, to),
            device_id_type=MESH,
        )


class Gather:
    def __init__(self, ring, buf, block):
        h = block // 2
        r = ring

        def part(t, half):
            return buf.at[pl.ds(pl.multiple_of(t * block + half * h, h), h)]

        self.first = [
            r.copy(part(r.tx, 0), part(r.tx, 0), 0, r.right),
            r.copy(part(r.tx, 1), part(r.tx, 1), 1, r.left),
            r.copy(part(r.tx, 1), part(r.tx, 1), 2, r.right),
            r.copy(part(r.tx, 0), part(r.tx, 0), 3, r.left),
        ]
        self.second = [
            r.copy(part(r.left, 0), part(r.left, 0), 4, r.right),
            r.copy(part(r.right, 1), part(r.right, 1), 5, r.left),
        ]

    def start(self):
        for c in self.first:
            c.start()

    def forward(self):
        for c, d in zip(self.first[:2], self.second):
            c.wait_recv()
            d.start()

    def finish(self):
        for c in self.first[2:] + self.second:
            c.wait_recv()
        for c in self.first + self.second:
            c.wait_send()


class Scatter:
    def __init__(self, ring, part, land, onward, block):
        h = block // 2
        r = ring
        self.h = h
        self.ring = r
        self.part = part
        self.land = land
        self.onward = onward
        self.block = block

        self.first = [
            r.copy(self.at(r.far, 0), self.slot(0), 0, r.right),
            r.copy(self.at(r.far, 1), self.slot(1), 1, r.left),
            r.copy(self.at(r.right, 1), self.slot(2), 2, r.right),
            r.copy(self.at(r.left, 0), self.slot(3), 3, r.left),
        ]
        self.second = [
            r.copy(onward.at[pl.ds(0, h)], self.slot(4), 4, r.right),
            r.copy(onward.at[pl.ds(h, h)], self.slot(5), 5, r.left),
        ]

    def at(self, t, half):
        return self.part.at[self.span(t, half)]

    def span(self, t, half):
        return pl.ds(pl.multiple_of(t * self.block + half * self.h, self.h), self.h)

    def slot(self, i):
        return self.land.at[pl.ds(i * self.h, self.h)]

    def start(self):
        for c in self.first:
            c.start()

    def forward(self):
        h = self.h
        for i, t in enumerate((self.ring.right, self.ring.left)):
            self.first[i].wait_recv()
            self.onward[i * h : (i + 1) * h] = (
                self.land[i * h : (i + 1) * h].astype(F32) + self.part[self.span(t, i)].astype(F32)
            ).astype(BF)
            self.second[i].start()

    def finish(self):
        h = self.h
        for c in self.first[2:] + self.second:
            c.wait_recv()
        for c in self.first + self.second:
            c.wait_send()

        def got(i):
            return self.land[i * h : (i + 1) * h].astype(F32)

        return got(3) + got(4), got(2) + got(5)


def slots_of(ids):
    n = ids.shape[1]
    holder = lax.shift_right_logical(ids, 12)
    hits = iota((OWNERS, n), 0) == holder
    earlier = one_zero(iota((n, n), 0) < iota((n, n), 1))
    hits_b = one_zero(hits)
    before = jnp.sum(jnp.where(hits, mm(hits_b, earlier), 0.0), axis=0, keepdims=True)
    return holder, hits_b, before.astype(jnp.int32)


def wanted_rows(ids, hits_b, before, offset):
    n = ids.shape[1]
    marked = (ids & (ROWS - 1)) + 1
    chosen = iota((OWNERS, n), 0) == before + offset
    high = jnp.where(chosen, lax.shift_right_logical(marked, 6).astype(F32), 0.0).astype(BF)
    low = jnp.where(chosen, (marked & 63).astype(F32), 0.0).astype(BF)
    return 64.0 * mm_nt(hits_b, high) + mm_nt(hits_b, low)


def as_column(row):
    n = row.shape[1]
    wide = jnp.broadcast_to(row.astype(F32), (128, n))
    return jnp.transpose(wide)[:, 0:1].astype(jnp.int32)


def neg_row(negs_ref):
    return jnp.concatenate([negs_ref[u : u + 1, :] for u in range(4)], axis=1)


def part_mask(rows, width, per, parts):
    which = lax.rem(iota((rows, width), 0), 16) // per
    return [one_zero(which == c) for c in range(parts)]


def pick_parts(values, per, width):
    which = lax.div(lax.rem(iota((values.shape[0], width), 0), 16), per)
    out = values[:, 0:width]
    for c in range(1, values.shape[1] // width):
        out = jnp.where(which == c, values[:, c * width : (c + 1) * width], out)
    return out


def gather_rows(table, ids_col, out_ref, at):
    step = 512

    def one(i, total):
        base = pl.multiple_of(i * step, step)
        pick = one_zero(ids_col == iota((512, step), 1) + i * step)
        return total + mm(pick, table[pl.ds(base, step), :])

    total = lax.fori_loop(0, ROWS // step, one, jnp.zeros((512, D), F32))
    out_ref[at : at + 512, :] = total.astype(BF)


def spread_chunks(rows_ref, chunks_ref, at, cap):
    width = cap * 32
    block = 128 // cap
    many = block * 16
    r, q = iota((many, 128), 0), iota((many, 128), 1)
    fold = one_zero(
        (lax.rem(q, block) == lax.div(r, 16)) & (lax.div(q, block) == lax.rem(r, cap))
    )
    for b in range(cap):
        rows = jnp.concatenate(
            [
                rows_ref[at + k * 128 + b * block : at + k * 128 + (b + 1) * block, :]
                for k in range(cap)
            ],
            axis=0,
        )
        chunks_ref[b * many : (b + 1) * many, :] = pick_parts(mm(fold, rows), cap, width).astype(BF)


def unfold(chunks, per, parts):
    rows, width = chunks.shape
    masks = part_mask(rows, width, per, parts)
    return jnp.concatenate([chunks * m for m in masks], axis=1)


def take_slots(chunks_ref, slot_col, cap):
    n = slot_col.shape[0]
    total = jnp.zeros((n, D), F32)
    step = 512
    for i in range(OWNERS * 16 // step):
        r = iota((n, step), 1) + i * step
        key = lax.div(r, 16) * cap + lax.rem(r, cap)
        total = total + mm(
            one_zero(slot_col == key),
            unfold(chunks_ref[i * step : (i + 1) * step, :], cap, 16 // cap),
        )
    return total.astype(BF)


def put_slots(rows, slot_row, chunks_ref, cap):
    n = slot_row.shape[1]
    step = 512
    for i in range(OWNERS * 16 // step):
        r = iota((step, n), 0) + i * step
        key = lax.div(r, 16) * cap + lax.rem(r, cap)
        chunks_ref[i * step : (i + 1) * step, :] = pick_parts(
            mm(one_zero(slot_row == key), rows), cap, cap * 32
        ).astype(BF)


def row_sum(values):
    return jnp.sum(values, axis=-1, keepdims=True)


def row_mean(values):
    return jnp.mean(values, axis=-1, keepdims=True)


def normal(values):
    center = values - row_mean(values)
    factor = lax.rsqrt(row_mean(center * center) + epsilon)
    return center * factor, factor


def normal_back(grad, normed, factor):
    return factor * (grad - row_mean(grad) - normed * row_mean(grad * normed))


def unit_factor(values):
    return lax.rsqrt(row_sum(values * values) + epsilon)


def unit_back(grad, values, factor):
    return factor * (grad - values * (factor * factor * row_sum(grad * values)))


class Users:
    def __init__(self, lengths_ref):
        self.lengths = [lengths_ref[0, u] for u in range(4)]
        self.ends = []
        end = 0
        for length in self.lengths:
            end = end + length
            self.ends.append(end)

    def segment(self, t):
        return sum(jnp.where(t >= end, 1, 0) for end in self.ends)

    def start(self, t):
        return sum(jnp.where(t >= e, n, 0) for e, n in zip(self.ends, self.lengths))

    def length(self, t):
        out = jnp.where(t >= 0, self.lengths[0], 0)
        for u in range(1, 4):
            out = jnp.where(t >= self.ends[u - 1], self.lengths[u], out)
        return out


VM = pl.BlockSpec(memory_space=pltpu.VMEM)
HB = pl.BlockSpec(memory_space=pl.ANY)
SM = pl.BlockSpec(memory_space=pltpu.SMEM)
Q = 256
KEYS = 768
SCALE = DH**-0.5
PIECE = 80


def layer_kernel(
    ids_ref,
    negs_ref,
    lengths_ref,
    table_hbm,
    w_in_hbm,
    w_out_hbm,
    ids_out,
    rows_out,
    weight_out,
    table_ref,
    request_ref,
    arrived_ref,
    arrived_t_ref,
    hist_back,
    neg_back,
    picked_ref,
    hist_out,
    neg_out,
    hist_in,
    neg_in,
    w_in_ref,
    w_out_ref,
    emb_ref,
    unit_ref,
    normed_ref,
    proj_ref,
    slope_ref,
    weights_ref,
    dweights_ref,
    mixed_ref,
    factor_ref,
    gated_ref,
    part_ref,
    out_land,
    out_on,
    share_ref,
    dout_ref,
    dneg_ref,
    demb_ref,
    neg_land,
    neg_on,
    emb_land,
    emb_on,
    rest_ref,
    dgate_ref,
    dvalue_ref,
    dquery_ref,
    dkey_ref,
    dpre_ref,
    dwout_ref,
    weight_ref,
    weight_in,
    weight_mine,
    weight_sum,
    met_sem,
    load_sems,
    all_send,
    all_recv,
    ring_send,
    ring_recv,
):
    dp, tx = position()
    barrier = pltpu.get_barrier_semaphore()
    greet_planes(barrier, dp, tx)
    loads = [pltpu.make_async_copy(table_hbm, table_ref, load_sems.at[0])]
    for j in range(4):
        loads.append(
            pltpu.make_async_copy(
                w_in_hbm.at[j], w_in_ref.at[:, j * DH : (j + 1) * DH], load_sems.at[1 + j]
            )
        )
    loads.append(pltpu.make_async_copy(w_out_hbm, w_out_ref, load_sems.at[5]))
    for load in loads:
        load.start()

    def ring(i):
        return Ring(dp, tx, ring_send.at[i], ring_recv.at[i])

    right, left, far = ring(0).right, ring(0).left, ring(0).far

    def rows_of(b, n=Q):
        return pl.ds(pl.multiple_of(b * n, n), n)

    ids, negs = ids_ref[...], neg_row(negs_ref)
    holder_h, hits_h, before_h = slots_of(ids)
    holder_n, hits_n, before_n = slots_of(negs)
    wanted = wanted_rows(ids, hits_h, before_h, 0) + wanted_rows(negs, hits_n, before_n, CAP_H)
    pl.semaphore_wait(barrier, 22)
    greet_again(met_sem, dp, tx)
    request_ref[:, 0, :] = wanted.astype(jnp.int32) - 1
    slot_h = holder_h * CAP_H + before_h
    slot_n = holder_n * CAP_N + before_n
    slot_h_col, slot_n_col = as_column(slot_h), as_column(slot_n)
    users = Users(lengths_ref)

    pl.semaphore_wait(met_sem, 7)
    spread_all(request_ref, arrived_ref, 1, all_send.at[0], all_recv.at[0], dp, tx)
    for load in loads:
        load.wait()
    wait_rows(arrived_ref, OWNERS - 1, all_recv.at[0])

    arrived = arrived_ref[:, 0, :]
    columns = [arrived[:, k : k + 1] for k in range(CAP_H + CAP_N)]
    gather_rows(table_ref, jnp.concatenate(columns[0:4], axis=0), picked_ref, 0)
    spread_chunks(picked_ref, hist_out, 0, CAP_H)
    spread_all(hist_out, hist_in, 16, all_send.at[1], all_recv.at[1], dp, tx)
    gather_rows(table_ref, jnp.concatenate(columns[4:8], axis=0), picked_ref, 512)
    gather_rows(table_ref, jnp.concatenate(columns[8:12], axis=0), picked_ref, 1024)
    spread_chunks(picked_ref, neg_out, 512, CAP_N)
    spread_all(neg_out, neg_in, 16, all_send.at[2], all_recv.at[2], dp, tx)

    wait_rows(hist_in, (OWNERS - 1) * 16, all_recv.at[1])
    emb_ref[rows_of(tx), :] = take_slots(hist_in, slot_h_col, CAP_H)
    hist = Gather(ring(0), emb_ref, Q)
    hist.start()

    def project(b):
        at = rows_of(b)
        normed = normal(emb_ref[at, :].astype(F32))[0].astype(BF)
        normed_ref[at, :] = normed
        pre = mm(normed, w_in_ref[...])
        gate = lax.logistic(pre)
        proj_ref[at, :] = (pre * gate).astype(BF)
        slope_ref[at, :] = gate * (1.0 + pre * (1.0 - gate))

    project(tx)
    hist.forward()
    for c in hist.first[2:]:
        c.wait_recv()
    project(left)
    project(right)
    for c in hist.second:
        c.wait_recv()
    project(far)

    arrived_t_ref[...] = jnp.transpose(arrived.astype(F32)).astype(jnp.int32)

    wait_rows(neg_in, (OWNERS - 1) * 16, all_recv.at[2])
    neg_f = take_slots(neg_in, slot_n_col, CAP_N).astype(F32)
    neg_factor = unit_factor(neg_f)
    unit_ref[rows_of(tx, 512), :] = (neg_f * neg_factor).astype(BF)
    units = Gather(ring(1), unit_ref, 512)
    units.start()

    def keys_of(b):
        return pl.ds(pl.multiple_of(lax.div(b, 3) * Q, Q), KEYS)

    def attend(b):
        at, kr = rows_of(b), keys_of(b)
        scores = mm_nt(proj_ref[at, 256:384], proj_ref[kr, 384:512]) * SCALE
        t = iota((Q, 1), 0) + b * Q
        s = iota((Q, KEYS), 1) + lax.div(b, 3) * Q
        seen = (s <= t) & (s >= users.start(t))
        share = 1.0 / users.length(t).astype(F32)
        gate = lax.logistic(scores)
        weights = jnp.where(seen, scores * gate * share, 0.0).astype(BF)
        weights_ref[at, :] = weights
        dweights_ref[at, :] = jnp.where(
            seen, gate * (1.0 + scores * (1.0 - gate)) * (share * SCALE), 0.0
        )
        mixed, factor = normal(mm(weights, proj_ref[kr, 128:256]))
        mixed_ref[at, :] = mixed
        factor_ref[at, :] = jnp.broadcast_to(factor, (Q, DH))
        gated = (mixed * proj_ref[at, 0:128].astype(F32)).astype(BF)
        gated_ref[at, :] = gated
        part_ref[at, :] = mm(gated, w_out_ref[...]).astype(BF)

    out_sum = Scatter(ring(2), part_ref, out_land, out_on, Q)
    attend(far)
    out_sum.first[0].start()
    out_sum.first[1].start()
    attend(right)
    out_sum.first[2].start()
    attend(left)
    out_sum.first[3].start()
    units.forward()
    out_sum.forward()
    attend(tx)
    emb_f = emb_ref[rows_of(tx), :].astype(F32)
    first, second = out_sum.finish()
    y = emb_f + part_ref[rows_of(tx), :].astype(F32) + jnp.concatenate([first, second], axis=0)

    y_factor = unit_factor(y)
    y_unit = (y * y_factor).astype(BF)
    last = iota((Q, 1), 0) == Q - 1
    follow = jnp.where(
        last,
        emb_ref[rows_of(right), :].astype(F32)[0:1, :],
        pltpu.roll(emb_f, Q - 1, 0),
    )
    follow_factor = unit_factor(follow)
    follow_unit = (follow * follow_factor).astype(BF).astype(F32)
    y_unit_f = y_unit.astype(F32)
    t = iota((Q, 1), 0) + tx * Q
    segment = users.segment(t)
    valid = users.segment(t + 1) == segment
    grown_pos = jnp.exp(sharpness * row_sum(y_unit_f * follow_unit))
    total = grown_pos
    mine = [jnp.where(segment == u, 1.0, 0.0) for u in range(4)]
    units.finish()
    for c in range(4):
        grown = jnp.exp(sharpness * mm_nt(y_unit, unit_ref[c * 512 : (c + 1) * 512, :]))
        grown = jnp.concatenate(
            [grown[:, u * 128 : (u + 1) * 128] * mine[u] for u in range(4)], axis=1
        )
        total = total + row_sum(grown)
        share_ref[c] = grown
    scaled = jnp.where(valid, sharpness / total, 0.0)
    d_pos = jnp.where(valid, sharpness * (grown_pos / total - 1.0), 0.0)
    d_unit = d_pos * follow_unit
    for c in range(4):
        d_unit = d_unit + mm(
            (share_ref[c] * scaled).astype(BF), unit_ref[c * 512 : (c + 1) * 512, :]
        )
    d_rows = unit_back(d_unit, y, y_factor)
    dout_ref[rows_of(tx), :] = d_rows.astype(BF)
    douts = Gather(ring(3), dout_ref, Q)
    douts.start()
    neg_sum = Scatter(ring(4), dneg_ref, neg_land, neg_on, 512)

    def neg_grads(b):
        dneg_ref[rows_of(b, 512), :] = mm_tn((share_ref[b] * scaled).astype(BF), y_unit).astype(BF)

    neg_grads(far)
    d_follow = unit_back(d_pos * y_unit_f, follow, follow_factor)
    rest_ref[0:Q, :] = d_rows + jnp.where(t == tx * Q, 0.0, pltpu.roll(d_follow, 1, 0))
    rest_ref[Q : Q + 8, :] = jnp.where(iota((8, 1), 0) == 0, d_follow[Q - 1 : Q, :], 0.0)
    douts.forward()
    neg_sum.first[0].start()
    neg_sum.first[1].start()
    neg_grads(right)
    neg_sum.first[2].start()
    neg_grads(left)
    neg_sum.first[3].start()
    neg_grads(tx)

    dkey_ref[...] = jnp.zeros_like(dkey_ref)
    dvalue_ref[...] = jnp.zeros_like(dvalue_ref)
    dwout_ref[...] = jnp.zeros_like(dwout_ref)

    def attend_back(b):
        at, kr = rows_of(b), keys_of(b)
        d_out = dout_ref[at, :]
        d_gated = mm_nt(d_out, w_out_ref[...]).astype(BF).astype(F32)
        dwout_ref[...] += mm_tn(gated_ref[at, :], d_out)
        mixed = mixed_ref[at, :]
        dgate_ref[at, :] = (d_gated * mixed).astype(BF)
        d_mixed = normal_back(
            d_gated * proj_ref[at, 0:128].astype(F32), mixed, factor_ref[at, :][:, 0:1]
        ).astype(BF)
        d_scores = (mm_nt(d_mixed, proj_ref[kr, 128:256]) * dweights_ref[at, :]).astype(BF)
        dquery_ref[at, :] = mm(d_scores, proj_ref[kr, 384:512]).astype(BF)
        dkey_ref[kr, :] += mm_tn(d_scores, proj_ref[at, 256:384])
        dvalue_ref[kr, :] += mm_tn(weights_ref[at, :], d_mixed)

    attend_back(tx)
    for c in douts.first[2:]:
        c.wait_recv()
    attend_back(left)
    attend_back(right)
    neg_sum.forward()
    for c in douts.second:
        c.wait_recv()
    attend_back(far)

    def project_back(b):
        at = rows_of(b)
        d_proj = jnp.concatenate(
            [
                dgate_ref[at, :].astype(F32),
                dvalue_ref[at, :].astype(BF).astype(F32),
                dquery_ref[at, :].astype(F32),
                dkey_ref[at, :].astype(BF).astype(F32),
            ],
            axis=1,
        )
        d_pre = (d_proj * slope_ref[at, :]).astype(BF)
        dpre_ref[at, :] = d_pre
        normed, factor = normal(emb_ref[at, :].astype(F32))
        return normal_back(mm_nt(d_pre, w_in_ref[...]).astype(BF).astype(F32), normed, factor)

    emb_sum = Scatter(ring(5), demb_ref, emb_land, emb_on, Q)
    demb_ref[rows_of(far), :] = project_back(far).astype(BF)
    emb_sum.first[0].start()
    emb_sum.first[1].start()
    d_right = project_back(right)
    demb_ref[rows_of(right), :] = (
        d_right + jnp.where(iota((Q, 1), 0) == 0, rest_ref[Q : Q + 1, :], 0.0)
    ).astype(BF)
    emb_sum.first[2].start()
    demb_ref[rows_of(left), :] = project_back(left).astype(BF)
    emb_sum.first[3].start()
    rest_ref[0:Q, :] += project_back(tx)
    emb_sum.forward()

    d_win = mm_tn(normed_ref[...], dpre_ref[...]).astype(BF)
    for j in range(4):
        weight_ref[j * D : (j + 1) * D, :] = d_win[:, j * DH : (j + 1) * DH]
        weight_ref[2048 + j * DH : 2048 + (j + 1) * DH, :] = dwout_ref[
            :, j * DH : (j + 1) * DH
        ].astype(BF)
    own = pl.ds(pl.multiple_of(dp * PIECE, 16), PIECE)

    def out_piece(pd):
        pltpu.make_async_remote_copy(
            src_ref=weight_ref.at[pl.ds(pl.multiple_of(pd * PIECE, 16), PIECE)],
            dst_ref=weight_in.at[own],
            send_sem=all_send.at[5],
            recv_sem=all_recv.at[5],
            device_id=(pd, tx),
            device_id_type=MESH,
        ).start()

    def back_piece(pd):
        pltpu.make_async_remote_copy(
            src_ref=weight_mine,
            dst_ref=weight_sum.at[own],
            send_sem=all_send.at[6],
            recv_sem=all_recv.at[6],
            device_id=(pd, tx),
            device_id_type=MESH,
        ).start()

    first, second = emb_sum.finish()
    d_hist = rest_ref[0:Q, :] + jnp.concatenate([first, second], axis=0)
    wait_rows(hist_out, (OWNERS - 1) * 16, all_send.at[1])
    put_slots(d_hist.astype(BF), slot_h, hist_out, CAP_H)
    spread_all(hist_out, hist_back, 16, all_send.at[3], all_recv.at[3], dp, tx)

    first, second = neg_sum.finish()
    d_neg = dneg_ref[rows_of(tx, 512), :].astype(F32) + jnp.concatenate([first, second], axis=0)
    wait_rows(neg_out, (OWNERS - 1) * 16, all_send.at[2])
    put_slots(unit_back(d_neg, neg_f, neg_factor).astype(BF), slot_n, neg_out, CAP_N)
    spread_all(neg_out, neg_back, 16, all_send.at[4], all_recv.at[4], dp, tx)

    each_dp(dp, tx, out_piece)
    weight_in[own] = weight_ref[own]
    wait_rows(weight_in, (N_DP - 1) * PIECE, all_recv.at[5])
    total = weight_in[0:PIECE, :].astype(F32)
    for i in range(1, N_DP):
        total = total + weight_in[i * PIECE : (i + 1) * PIECE, :].astype(F32)
    weight_mine[...] = total.astype(BF)
    weight_sum[own] = total.astype(BF)
    each_dp(dp, tx, back_piece)

    wait_rows(hist_back, (OWNERS - 1) * 16, all_recv.at[3])
    gather_chunks(hist_back, picked_ref, 0, CAP_H)
    wait_rows(neg_back, (OWNERS - 1) * 16, all_recv.at[4])
    gather_chunks(neg_back, picked_ref, 512, CAP_N)
    wait_rows(weight_sum, (N_DP - 1) * PIECE, all_recv.at[6])
    results = [
        pltpu.make_async_copy(arrived_t_ref, ids_out, load_sems.at[0]),
        pltpu.make_async_copy(picked_ref, rows_out, load_sems.at[1]),
        pltpu.make_async_copy(weight_sum, weight_out, load_sems.at[2]),
    ]
    for move in results:
        move.start()
    for move in results:
        move.wait()
    for c in hist.first + hist.second + douts.first + douts.second:
        c.wait_send()
    wait_rows(request_ref, OWNERS - 1, all_send.at[0])
    wait_rows(hist_out, (OWNERS - 1) * 16, all_send.at[3])
    wait_rows(neg_out, (OWNERS - 1) * 16, all_send.at[4])
    wait_rows(weight_in, (N_DP - 1) * PIECE, all_send.at[5])
    wait_rows(weight_in, (N_DP - 1) * PIECE, all_send.at[6])


def layer(ids, negs, lengths, table, w_in, w_out):
    sem = pltpu.SemaphoreType.DMA
    vm = pltpu.VMEM
    return pl.pallas_call(
        layer_kernel,
        out_shape=[
            jax.ShapeDtypeStruct((128, 128), jnp.int32),
            jax.ShapeDtypeStruct((12 * OWNERS, D), BF),
            jax.ShapeDtypeStruct((2560, 128), BF),
        ],
        in_specs=[VM, VM, SM, HB, HB, HB],
        out_specs=[HB] * 3,
        scratch_shapes=[
            vm((ROWS, D), BF),
            vm((OWNERS, 1, 128), jnp.int32),
            vm((OWNERS, 1, 128), jnp.int32),
            vm((128, 128), jnp.int32),
            vm((OWNERS * 16, 128), BF),
            vm((OWNERS * 16, 256), BF),
            vm((12 * OWNERS, D), BF),
            vm((OWNERS * 16, 128), BF),
            vm((OWNERS * 16, 256), BF),
            vm((OWNERS * 16, 128), BF),
            vm((OWNERS * 16, 256), BF),
            vm((D, D), BF),
            vm((DH, D), BF),
            vm((1024, D), BF),
            vm((2048, D), BF),
            vm((1024, D), BF),
            vm((1024, D), BF),
            vm((1024, D), F32),
            vm((1024, KEYS), BF),
            vm((1024, KEYS), F32),
            vm((1024, DH), F32),
            vm((1024, DH), F32),
            vm((1024, DH), BF),
            vm((1024, D), BF),
            vm((6 * 128, D), BF),
            vm((2 * 128, D), BF),
            vm((4, Q, 512), F32),
            vm((1024, D), BF),
            vm((2048, D), BF),
            vm((1024, D), BF),
            vm((6 * 256, D), BF),
            vm((2 * 256, D), BF),
            vm((6 * 128, D), BF),
            vm((2 * 128, D), BF),
            vm((Q + 8, D), F32),
            vm((1024, DH), BF),
            vm((1024, DH), F32),
            vm((1024, DH), BF),
            vm((1024, DH), F32),
            vm((1024, D), BF),
            vm((DH, D), F32),
            vm((2560, 128), BF),
            vm((2560, 128), BF),
            vm((PIECE, 128), BF),
            vm((2560, 128), BF),
            pltpu.SemaphoreType.REGULAR,
            sem((6,)),
            sem((7,)),
            sem((7,)),
            sem((6, 6)),
            sem((6, 6)),
        ],
        compiler_params=pltpu.CompilerParams(
            collective_id=0, has_side_effects=True, vmem_limit_bytes=56 * 1024 * 1024
        ),
        name="layer",
    )(ids, negs, lengths, table, w_in, w_out)


def gather_chunks(chunks_ref, rows_ref, at, cap):
    block = 128 // cap
    many = block * 16
    q, r = iota((128, many), 0), iota((128, many), 1)
    fold = one_zero(
        (lax.rem(q, block) == lax.div(r, 16)) & (lax.div(q, block) == lax.rem(r, cap))
    )
    for b in range(cap):
        wide = unfold(chunks_ref[b * many : (b + 1) * many, :], cap, 16 // cap)
        rows = mm(fold, wide).astype(BF)
        for k in range(cap):
            rows_ref[at + k * 128 + b * block : at + k * 128 + (b + 1) * block, :] = rows[
                k * block : (k + 1) * block
            ]


def add_kernel(ids_hbm, rows_hbm, weight_hbm, out_ref, w_in_ref, w_out_ref, ids_ref, rows_ref, weight_ref, sems):
    tile = out_ref.shape[0]
    step = pl.program_id(0)

    @pl.when(step == 0)
    def _():
        moves = [
            pltpu.make_async_copy(ids_hbm, ids_ref, sems.at[0]),
            pltpu.make_async_copy(rows_hbm, rows_ref, sems.at[1]),
            pltpu.make_async_copy(weight_hbm, weight_ref, sems.at[2]),
        ]
        for move in moves:
            move.start()
        for move in moves:
            move.wait()

    total = jnp.zeros((tile, D), F32)
    for k in range(0, CAP_H + CAP_N, 4):
        row = jnp.concatenate([ids_ref[k + j : k + j + 1, :] for j in range(4)], axis=1)
        put = one_zero(row == iota((tile, 512), 0) + step * tile)
        total = total + mm(put, rows_ref[k * 128 : (k + 4) * 128, :])
    out_ref[...] = total
    w_in_ref[...] = weight_ref[pl.ds(pl.multiple_of(step * 256, 256), 256), :].astype(F32)
    w_out_ref[...] = jnp.concatenate(
        [
            weight_ref[pl.ds(pl.multiple_of(2048 + c * 128 + step * 16, 16), 16), :]
            for c in range(4)
        ],
        axis=1,
    ).astype(F32)


def add_rows(ids, rows, weight):
    tile = 512
    anywhere = pl.BlockSpec(memory_space=pl.ANY)
    return pl.pallas_call(
        add_kernel,
        out_shape=[
            jax.ShapeDtypeStruct((ROWS, D), F32),
            jax.ShapeDtypeStruct((2048, DH), F32),
            jax.ShapeDtypeStruct((DH, D), F32),
        ],
        grid=(ROWS // tile,),
        in_specs=[anywhere] * 3,
        out_specs=[
            pl.BlockSpec((tile, D), lambda i: (i, 0)),
            pl.BlockSpec((256, DH), lambda i: (i, 0)),
            pl.BlockSpec((16, D), lambda i: (i, 0)),
        ],
        scratch_shapes=[
            pltpu.VMEM((128, 128), jnp.int32),
            pltpu.VMEM((12 * OWNERS, D), BF),
            pltpu.VMEM((2560, 128), BF),
            pltpu.SemaphoreType.DMA((3,)),
        ],
        compiler_params=pltpu.CompilerParams(vmem_limit_bytes=56 * 1024 * 1024),
        name="add_rows",
    )(ids, rows, weight)


def on_device(table, item_ids, negatives, lengths, w_in, w_out):
    ids, rows, weight = layer(item_ids.reshape(1, -1), negatives, lengths, table, w_in, w_out)
    grad_table, grad_w_in, grad_w_out = add_rows(ids, rows, weight)
    return (grad_table, grad_w_in.reshape(4, D, DH), grad_w_out)


def solution(mesh):
    placed = (
        P(("dp", "table"), None),
        P(("dp", "table")),
        P("dp", "table"),
        P("dp", None),
        P(None, None, "table"),
        P("table", None),
    )
    return jax.shard_map(
        on_device,
        mesh=mesh,
        in_specs=placed,
        out_specs=(P(("dp", "table"), None), P(None, None, "table"), P("table", None)),
        check_vma=False,
    )
```

```python
import functools
import jax
import jax.numpy as jnp
from jax import lax
from jax.experimental import pallas as pl
from jax.experimental.pallas import tpu as pltpu
from jax.sharding import PartitionSpec as P

DH = 128
D = 512
CAP_H = 4
CAP_N = 8
OWNERS = 128
N_DP = 32
N_TABLE = 4
ROWS = 4096
BF = jnp.bfloat16
F32 = jnp.float32
MESH = pl.DeviceIdType.MESH

epsilon = 1e-06
sharpness = 20.0


def iota(shape, dim):
    return lax.broadcasted_iota(jnp.int32, shape, dim)


def one_zero(mask):
    return jnp.where(mask, 1.0, 0.0).astype(BF)


def mm(a, b):
    return lax.dot_general(a, b, (((1,), (0,)), ((), ())), preferred_element_type=F32)


def mm_nt(a, b):
    return lax.dot_general(a, b, (((1,), (1,)), ((), ())), preferred_element_type=F32)


def mm_tn(a, b):
    return lax.dot_general(a, b, (((0,), (0,)), ((), ())), preferred_element_type=F32)


def position():
    dp = lax.axis_index("dp")
    tx = lax.axis_index("table")
    return dp, tx


def coordinates(dp, tx):
    z, y, c = lax.div(dp, 8), lax.rem(lax.div(dp, 2), 4), lax.rem(dp, 2)
    near = [(core, lax.rem(tx + dx, 4)) for core in (1 - c, c) for dx in range(4)]
    return z, y, near[4:] + near[:4]


def plane_base(z, y, step):
    return lax.rem(z + lax.div(step, 4), 4) * 8 + lax.rem(y + lax.rem(step, 4), 4) * 2


def each_partner(dp, tx, do):
    z, y, near = coordinates(dp, tx)

    def one(i, carry):
        base = plane_base(z, y, lax.rem(i * 7, 16))
        for core, x in near:
            do(base + core, x)
        return carry

    lax.fori_loop(1, 16, one, 0)
    for core, x in near[1:]:
        do(z * 8 + y * 2 + core, x)


def each_dp(dp, tx, do):
    z, y, near = coordinates(dp, tx)
    mine, other = near[0][0], near[4][0]

    def one(i, carry):
        base = plane_base(z, y, lax.rem(i * 7, 16))
        do(base + mine)
        do(base + other)
        return carry

    lax.fori_loop(1, 16, one, 0)
    do(z * 8 + y * 2 + other)


def signal(sem, dp, x):
    pl.semaphore_signal(sem, inc=1, device_id=(dp, x), device_id_type=MESH)


def greet_planes(barrier, dp, tx):
    z, y, near = coordinates(dp, tx)
    for core, x in near[1:]:
        signal(barrier, z * 8 + y * 2 + core, x)
    core, x = near[0]
    for i in range(1, 16):
        signal(barrier, plane_base(z, y, i) + core, x)


def greet_again(sem, dp, tx):
    z, y, near = coordinates(dp, tx)
    for core, x in near[1:]:
        signal(sem, z * 8 + y * 2 + core, x)


def spread_all(src, dst, chunk, send_sem, recv_sem, dp, tx):
    me = dp * 4 + tx
    land = pl.ds(pl.multiple_of(me * chunk, chunk), chunk)

    def one(pd, px):
        pltpu.make_async_remote_copy(
            src_ref=src.at[pl.ds(pl.multiple_of((pd * 4 + px) * chunk, chunk), chunk)],
            dst_ref=dst.at[land],
            send_sem=send_sem,
            recv_sem=recv_sem,
            device_id=(pd, px),
            device_id_type=MESH,
        ).start()

    each_partner(dp, tx, one)
    dst[land] = src[land]


def wait_rows(ref, count, sem):
    pltpu.make_async_copy(ref.at[pl.ds(0, count)], ref.at[pl.ds(0, count)], sem).wait()


class Ring:
    def __init__(self, dp, tx, send_sems, recv_sems):
        self.dp = dp
        self.tx = tx
        self.right = lax.rem(tx + 1, 4)
        self.left = lax.rem(tx + 3, 4)
        self.far = lax.rem(tx + 2, 4)
        self.send_sems = send_sems
        self.recv_sems = recv_sems

    def copy(self, src, dst, slot, to):
        return pltpu.make_async_remote_copy(
            src_ref=src,
            dst_ref=dst,
            send_sem=self.send_sems.at[slot],
            recv_sem=self.recv_sems.at[slot],
            device_id=(self.dp, to),
            device_id_type=MESH,
        )


class Gather:
    def __init__(self, ring, buf, block):
        h = block // 2
        r = ring

        def part(t, half):
            return buf.at[pl.ds(pl.multiple_of(t * block + half * h, h), h)]

        self.first = [
            r.copy(part(r.tx, 0), part(r.tx, 0), 0, r.right),
            r.copy(part(r.tx, 1), part(r.tx, 1), 1, r.left),
            r.copy(part(r.tx, 1), part(r.tx, 1), 2, r.right),
            r.copy(part(r.tx, 0), part(r.tx, 0), 3, r.left),
        ]
        self.second = [
            r.copy(part(r.left, 0), part(r.left, 0), 4, r.right),
            r.copy(part(r.right, 1), part(r.right, 1), 5, r.left),
        ]

    def start(self):
        for c in self.first:
            c.start()

    def forward(self):
        for c, d in zip(self.first[:2], self.second):
            c.wait_recv()
            d.start()

    def finish(self):
        for c in self.first[2:] + self.second:
            c.wait_recv()
        for c in self.first + self.second:
            c.wait_send()


class Scatter:
    def __init__(self, ring, part, land, onward, block):
        h = block // 2
        r = ring
        self.h = h
        self.ring = r
        self.part = part
        self.land = land
        self.onward = onward
        self.block = block

        self.first = [
            r.copy(self.at(r.far, 0), self.slot(0), 0, r.right),
            r.copy(self.at(r.far, 1), self.slot(1), 1, r.left),
            r.copy(self.at(r.right, 1), self.slot(2), 2, r.right),
            r.copy(self.at(r.left, 0), self.slot(3), 3, r.left),
        ]
        self.second = [
            r.copy(onward.at[pl.ds(0, h)], self.slot(4), 4, r.right),
            r.copy(onward.at[pl.ds(h, h)], self.slot(5), 5, r.left),
        ]

    def at(self, t, half):
        return self.part.at[self.span(t, half)]

    def span(self, t, half):
        return pl.ds(pl.multiple_of(t * self.block + half * self.h, self.h), self.h)

    def slot(self, i):
        return self.land.at[pl.ds(i * self.h, self.h)]

    def start(self):
        for c in self.first:
            c.start()

    def forward(self):
        h = self.h
        for i, t in enumerate((self.ring.right, self.ring.left)):
            self.first[i].wait_recv()
            self.onward[i * h : (i + 1) * h] = (
                self.land[i * h : (i + 1) * h].astype(F32) + self.part[self.span(t, i)].astype(F32)
            ).astype(BF)
            self.second[i].start()

    def finish(self):
        h = self.h
        for c in self.first[2:] + self.second:
            c.wait_recv()
        for c in self.first + self.second:
            c.wait_send()

        def got(i):
            return self.land[i * h : (i + 1) * h].astype(F32)

        return got(3) + got(4), got(2) + got(5)


def slots_of(ids):
    n = ids.shape[1]
    holder = lax.shift_right_logical(ids, 12)
    hits = iota((OWNERS, n), 0) == holder
    earlier = one_zero(iota((n, n), 0) < iota((n, n), 1))
    hits_b = one_zero(hits)
    before = jnp.sum(jnp.where(hits, mm(hits_b, earlier), 0.0), axis=0, keepdims=True)
    return holder, hits_b, before.astype(jnp.int32)


def wanted_rows(ids, hits_b, before, offset):
    n = ids.shape[1]
    marked = (ids & (ROWS - 1)) + 1
    chosen = iota((OWNERS, n), 0) == before + offset
    high = jnp.where(chosen, lax.shift_right_logical(marked, 6).astype(F32), 0.0).astype(BF)
    low = jnp.where(chosen, (marked & 63).astype(F32), 0.0).astype(BF)
    return 64.0 * mm_nt(hits_b, high) + mm_nt(hits_b, low)


def as_column(row):
    n = row.shape[1]
    wide = jnp.broadcast_to(row.astype(F32), (128, n))
    return jnp.transpose(wide)[:, 0:1].astype(jnp.int32)


def neg_row(negs_ref):
    return jnp.concatenate([negs_ref[u : u + 1, :] for u in range(4)], axis=1)


def part_mask(rows, width, per, parts):
    which = lax.rem(iota((rows, width), 0), 16) // per
    return [one_zero(which == c) for c in range(parts)]


def pick_parts(values, per, width):
    which = lax.div(lax.rem(iota((values.shape[0], width), 0), 16), per)
    out = values[:, 0:width]
    for c in range(1, values.shape[1] // width):
        out = jnp.where(which == c, values[:, c * width : (c + 1) * width], out)
    return out


def gather_rows(table, ids_col, out_ref, at):
    step = 512

    def one(i, total):
        base = pl.multiple_of(i * step, step)
        pick = one_zero(ids_col == iota((512, step), 1) + i * step)
        return total + mm(pick, table[pl.ds(base, step), :])

    total = lax.fori_loop(0, ROWS // step, one, jnp.zeros((512, D), F32))
    out_ref[at : at + 512, :] = total.astype(BF)


def spread_chunks(rows_ref, chunks_ref, at, cap):
    width = cap * 32
    block = 128 // cap
    many = block * 16
    r, q = iota((many, 128), 0), iota((many, 128), 1)
    fold = one_zero(
        (lax.rem(q, block) == lax.div(r, 16)) & (lax.div(q, block) == lax.rem(r, cap))
    )
    for b in range(cap):
        rows = jnp.concatenate(
            [
                rows_ref[at + k * 128 + b * block : at + k * 128 + (b + 1) * block, :]
                for k in range(cap)
            ],
            axis=0,
        )
        chunks_ref[b * many : (b + 1) * many, :] = pick_parts(mm(fold, rows), cap, width).astype(BF)


def unfold(chunks, per, parts):
    rows, width = chunks.shape
    masks = part_mask(rows, width, per, parts)
    return jnp.concatenate([chunks * m for m in masks], axis=1)


def take_slots(chunks_ref, slot_col, cap):
    n = slot_col.shape[0]
    total = jnp.zeros((n, D), F32)
    step = 512
    for i in range(OWNERS * 16 // step):
        r = iota((n, step), 1) + i * step
        key = lax.div(r, 16) * cap + lax.rem(r, cap)
        total = total + mm(
            one_zero(slot_col == key),
            unfold(chunks_ref[i * step : (i + 1) * step, :], cap, 16 // cap),
        )
    return total.astype(BF)


def put_slots(rows, slot_row, chunks_ref, cap):
    n = slot_row.shape[1]
    step = 512
    for i in range(OWNERS * 16 // step):
        r = iota((step, n), 0) + i * step
        key = lax.div(r, 16) * cap + lax.rem(r, cap)
        chunks_ref[i * step : (i + 1) * step, :] = pick_parts(
            mm(one_zero(slot_row == key), rows), cap, cap * 32
        ).astype(BF)


def row_sum(values):
    return jnp.sum(values, axis=-1, keepdims=True)


def row_mean(values):
    return jnp.mean(values, axis=-1, keepdims=True)


def normal(values):
    center = values - row_mean(values)
    factor = lax.rsqrt(row_mean(center * center) + epsilon)
    return center * factor, factor


def normal_back(grad, normed, factor):
    return factor * (grad - row_mean(grad) - normed * row_mean(grad * normed))


def unit_factor(values):
    return lax.rsqrt(row_sum(values * values) + epsilon)


def unit_back(grad, values, factor):
    return factor * (grad - values * (factor * factor * row_sum(grad * values)))


class Users:
    def __init__(self, lengths_ref):
        self.lengths = [lengths_ref[0, u] for u in range(4)]
        self.ends = []
        end = 0
        for length in self.lengths:
            end = end + length
            self.ends.append(end)

    def segment(self, t):
        return sum(jnp.where(t >= end, 1, 0) for end in self.ends)

    def start(self, t):
        return sum(jnp.where(t >= e, n, 0) for e, n in zip(self.ends, self.lengths))

    def length(self, t):
        out = jnp.where(t >= 0, self.lengths[0], 0)
        for u in range(1, 4):
            out = jnp.where(t >= self.ends[u - 1], self.lengths[u], out)
        return out


VM = pl.BlockSpec(memory_space=pltpu.VMEM)
HB = pl.BlockSpec(memory_space=pl.ANY)
SM = pl.BlockSpec(memory_space=pltpu.SMEM)
Q = 256
KEYS = 768
SCALE = DH**-0.5
PIECE = 80


def layer_kernel(
    ids_ref,
    negs_ref,
    lengths_ref,
    table_hbm,
    w_in_hbm,
    w_out_hbm,
    ids_out,
    rows_out,
    weight_out,
    table_ref,
    request_ref,
    arrived_ref,
    arrived_t_ref,
    hist_back,
    neg_back,
    picked_ref,
    hist_out,
    neg_out,
    hist_in,
    neg_in,
    w_in_ref,
    w_out_ref,
    emb_ref,
    neg_ref,
    unit_ref,
    normed_ref,
    proj_ref,
    slope_ref,
    weights_ref,
    dweights_ref,
    mixed_ref,
    factor_ref,
    gated_ref,
    y_ref,
    y_factor_ref,
    y_unit_ref,
    grown_ref,
    shares_ref,
    total_ref,
    whole_ref,
    drows_ref,
    dgated_ref,
    dgated_land,
    dgated_on,
    dout_part,
    dout_land,
    dout_on,
    demb_ref,
    emb_land,
    emb_on,
    rest_ref,
    dgate_ref,
    dvalue_ref,
    dquery_ref,
    dkey_ref,
    dpre_ref,
    weight_ref,
    weight_in,
    weight_mine,
    weight_sum,
    met_sem,
    load_sems,
    all_send,
    all_recv,
    ring_send,
    ring_recv,
    total_send,
    total_recv,
):
    dp, tx = position()
    barrier = pltpu.get_barrier_semaphore()
    greet_planes(barrier, dp, tx)
    loads = [pltpu.make_async_copy(table_hbm, table_ref, load_sems.at[0])]
    for j in range(4):
        loads.append(
            pltpu.make_async_copy(
                w_in_hbm.at[j], w_in_ref.at[:, j * DH : (j + 1) * DH], load_sems.at[1 + j]
            )
        )
    loads.append(
        pltpu.make_async_copy(
            w_out_hbm, w_out_ref.at[pl.ds(pl.multiple_of(tx * DH, DH), DH)], load_sems.at[5]
        )
    )
    for load in loads:
        load.start()

    def ring(i):
        return Ring(dp, tx, ring_send.at[i], ring_recv.at[i])

    right, left, far = ring(0).right, ring(0).left, ring(0).far

    def rows_of(b, n=Q):
        return pl.ds(pl.multiple_of(b * n, n), n)

    ids, negs = ids_ref[...], neg_row(negs_ref)
    holder_h, hits_h, before_h = slots_of(ids)
    holder_n, hits_n, before_n = slots_of(negs)
    wanted = wanted_rows(ids, hits_h, before_h, 0) + wanted_rows(negs, hits_n, before_n, CAP_H)
    pl.semaphore_wait(barrier, 22)
    greet_again(met_sem, dp, tx)
    request_ref[:, 0, :] = wanted.astype(jnp.int32) - 1
    slot_h = holder_h * CAP_H + before_h
    slot_n = holder_n * CAP_N + before_n

    pl.semaphore_wait(met_sem, 7)
    spread_all(request_ref, arrived_ref, 1, all_send.at[0], all_recv.at[0], dp, tx)
    for load in loads:
        load.wait()
    w_outs = Gather(ring(1), w_out_ref, DH)
    w_outs.start()
    slot_h_col, slot_n_col = as_column(slot_h), as_column(slot_n)
    users = Users(lengths_ref)
    wait_rows(arrived_ref, OWNERS - 1, all_recv.at[0])

    arrived = arrived_ref[:, 0, :]
    columns = [arrived[:, k : k + 1] for k in range(CAP_H + CAP_N)]
    gather_rows(table_ref, jnp.concatenate(columns[0:4], axis=0), picked_ref, 0)
    spread_chunks(picked_ref, hist_out, 0, CAP_H)
    spread_all(hist_out, hist_in, 16, all_send.at[1], all_recv.at[1], dp, tx)
    w_outs.forward()
    gather_rows(table_ref, jnp.concatenate(columns[4:8], axis=0), picked_ref, 512)
    gather_rows(table_ref, jnp.concatenate(columns[8:12], axis=0), picked_ref, 1024)
    spread_chunks(picked_ref, neg_out, 512, CAP_N)
    spread_all(neg_out, neg_in, 16, all_send.at[2], all_recv.at[2], dp, tx)

    wait_rows(hist_in, (OWNERS - 1) * 16, all_recv.at[1])
    emb_ref[rows_of(tx), :] = take_slots(hist_in, slot_h_col, CAP_H)
    hist = Gather(ring(0), emb_ref, Q)
    hist.start()

    def project(b):
        at = rows_of(b)
        normed = normal(emb_ref[at, :].astype(F32))[0].astype(BF)
        normed_ref[at, :] = normed
        pre = mm(normed, w_in_ref[...])
        gate = lax.logistic(pre)
        proj_ref[at, :] = (pre * gate).astype(BF)
        slope_ref[at, :] = gate * (1.0 + pre * (1.0 - gate))

    project(tx)
    hist.forward()
    for c in hist.first[2:]:
        c.wait_recv()
    project(left)
    project(right)
    for c in hist.second:
        c.wait_recv()
    project(far)

    arrived_t_ref[...] = jnp.transpose(arrived.astype(F32)).astype(jnp.int32)

    mine = pl.multiple_of(tx * 1024, 1024)

    def keys_of(b):
        low = max(b - 2, 0)
        return slice(low * Q, (b + 1) * Q), low

    def attend(b):
        at = slice(b * Q, (b + 1) * Q)
        kr, low = keys_of(b)
        n = kr.stop - kr.start
        scores = mm_nt(proj_ref[at, 256:384], proj_ref[kr, 384:512]) * SCALE
        t = iota((Q, 1), 0) + b * Q
        s = iota((Q, n), 1) + low * Q
        seen = (s <= t) & (s >= users.start(t))
        share = 1.0 / users.length(t).astype(F32)
        gate = lax.logistic(scores)
        weights = jnp.where(seen, scores * gate * share, 0.0).astype(BF)
        weights_ref[at, 0:n] = weights
        dweights_ref[at, 0:n] = jnp.where(
            seen, gate * (1.0 + scores * (1.0 - gate)) * (share * SCALE), 0.0
        )
        mixed, factor = normal(mm(weights, proj_ref[kr, 128:256]))
        mixed_ref[at, :] = mixed
        factor_ref[at, :] = jnp.broadcast_to(factor, (Q, DH))
        gated_ref[pl.ds(mine + b * Q, Q), :] = (mixed * proj_ref[at, 0:128].astype(F32)).astype(BF)

    gates = Gather(ring(2), gated_ref, 1024)
    attend(0)
    attend(1)
    gates.first[0].start()
    gates.first[3].start()
    attend(2)
    attend(3)
    gates.first[1].start()
    gates.first[2].start()

    wait_rows(neg_in, (OWNERS - 1) * 16, all_recv.at[2])
    neg_ref[...] = take_slots(neg_in, slot_n_col, CAP_N)
    gates.forward()
    neg_f = neg_ref[...].astype(F32)
    neg_factor = unit_factor(neg_f)
    unit_ref[...] = (neg_f * neg_factor).astype(BF)
    w_outs.finish()
    arrived_t_ref[...] = jnp.transpose(arrived.astype(F32)).astype(jnp.int32)

    emb_f = emb_ref[rows_of(tx), :].astype(F32)
    follow = jnp.where(
        iota((Q, 1), 0) == Q - 1,
        emb_ref[rows_of(right), :].astype(F32)[0:1, :],
        pltpu.roll(emb_f, Q - 1, 0),
    )
    follow_factor = unit_factor(follow)
    follow_unit = (follow * follow_factor).astype(BF).astype(F32)
    t_row = iota((1, 1024), 1)
    segment = users.segment(t_row)
    valid = users.segment(t_row + 1) == segment
    users_of = [jnp.where(segment == u, 1.0, 0.0) for u in range(4)]
    gates.finish()

    for b in range(4):
        at = slice(b * Q, (b + 1) * Q)
        gated = jnp.concatenate(
            [gated_ref[h * 1024 + b * Q : h * 1024 + (b + 1) * Q, :] for h in range(4)], axis=1
        )
        y = emb_ref[at, :].astype(F32) + mm(gated, w_out_ref[...])
        factor = unit_factor(y)
        y_unit = (y * factor).astype(BF)
        y_ref[at, :] = y
        y_factor_ref[at, :] = jnp.broadcast_to(factor, (Q, DH))
        y_unit_ref[at, :] = y_unit
        grown = jnp.exp(sharpness * mm_nt(unit_ref[...], y_unit))
        grown = jnp.concatenate(
            [grown[u * DH : (u + 1) * DH, :] * users_of[u][:, at] for u in range(4)], axis=0
        )
        grown_ref[:, at] = grown
        total_ref[tx, :, at] = jnp.sum(grown, axis=0, keepdims=True)

    y_unit_f = y_unit_ref[rows_of(tx), :].astype(F32)
    grown_pos = jnp.exp(sharpness * row_sum(y_unit_f * follow_unit))
    own_lanes = pl.ds(pl.multiple_of(tx * Q, Q), Q)
    grown_pos_row = jnp.transpose(jnp.broadcast_to(grown_pos, (Q, DH)))[0:1, :]
    total_ref[tx, :, own_lanes] += grown_pos_row
    totals = [
        Ring(dp, tx, total_send, total_recv).copy(total_ref.at[tx], total_ref.at[tx], i, to)
        for i, to in enumerate((right, left, far))
    ]
    for c in totals:
        c.start()
    for c in totals:
        c.wait_recv()
    total = total_ref[0] + total_ref[1] + total_ref[2] + total_ref[3]
    whole_ref[...] = jnp.where(valid, sharpness / total, 0.0)
    scaled_own = jnp.transpose(jnp.broadcast_to(whole_ref[:, own_lanes], (DH, Q)))[:, 0:1]
    d_pos = jnp.where(scaled_own > 0.0, scaled_own * grown_pos - sharpness, 0.0)
    d_unit_pos = d_pos * follow_unit
    gate_sum = Scatter(ring(3), dgated_ref, dgated_land, dgated_on, 1024)
    for b in range(4):
        at = slice(b * Q, (b + 1) * Q)
        shares = (grown_ref[:, at] * whole_ref[:, at]).astype(BF)
        shares_ref[:, at] = shares
        d_unit = mm_tn(shares, unit_ref[...]) + jnp.where(tx == b, d_unit_pos, 0.0)
        d_rows = unit_back(d_unit, y_ref[at, :], y_factor_ref[at, :][:, 0:1])
        drows_ref[at, :] = d_rows
        d_gated = mm_nt(d_rows.astype(BF), w_out_ref[...]).astype(BF)
        for h in range(4):
            dgated_ref[h * 1024 + b * Q : h * 1024 + (b + 1) * Q, :] = d_gated[
                :, h * DH : (h + 1) * DH
            ]
        if b == 1:
            gate_sum.first[0].start()
            gate_sum.first[3].start()
    gate_sum.first[1].start()
    gate_sum.first[2].start()

    d_neg = unit_back(
        mm(shares_ref[...], y_unit_ref[...]),
        neg_ref[...].astype(F32),
        unit_factor(neg_ref[...].astype(F32)),
    )
    wait_rows(neg_out, (OWNERS - 1) * 16, all_send.at[2])
    put_slots(d_neg.astype(BF), slot_n, neg_out, CAP_N)
    gate_sum.forward()
    spread_all(neg_out, neg_back, 16, all_send.at[4], all_recv.at[4], dp, tx)
    for h in range(4):
        dout_part[h * DH : (h + 1) * DH, :] = mm_tn(
            gated_ref[h * 1024 : (h + 1) * 1024, :], drows_ref[...].astype(BF)
        ).astype(BF)
    w_out_sum = Scatter(ring(4), dout_part, dout_land, dout_on, DH)
    w_out_sum.start()
    d_follow = unit_back(d_pos * y_unit_f, follow, follow_factor)
    rest_ref[0:Q, :] = jnp.where(iota((Q, 1), 0) == 0, 0.0, pltpu.roll(d_follow, 1, 0))
    rest_ref[Q : Q + 8, :] = jnp.where(iota((8, 1), 0) == 0, d_follow[Q - 1 : Q, :], 0.0)
    dkey_ref[...] = jnp.zeros_like(dkey_ref)
    dvalue_ref[...] = jnp.zeros_like(dvalue_ref)
    halves = gate_sum.finish()

    def attend_back(b):
        at = slice(b * Q, (b + 1) * Q)
        kr, _ = keys_of(b)
        n = kr.stop - kr.start
        half = halves[b // 2][(b % 2) * Q : (b % 2 + 1) * Q, :]
        d_gated = half + dgated_ref[pl.ds(mine + b * Q, Q), :].astype(F32)
        mixed = mixed_ref[at, :]
        dgate_ref[at, :] = (d_gated * mixed).astype(BF)
        d_mixed = normal_back(
            d_gated * proj_ref[at, 0:128].astype(F32), mixed, factor_ref[at, :][:, 0:1]
        ).astype(BF)
        d_scores = (mm_nt(d_mixed, proj_ref[kr, 128:256]) * dweights_ref[at, 0:n]).astype(BF)
        dquery_ref[at, :] = mm(d_scores, proj_ref[kr, 384:512]).astype(BF)
        dkey_ref[kr, :] += mm_tn(d_scores, proj_ref[at, 256:384])
        dvalue_ref[kr, :] += mm_tn(weights_ref[at, 0:n], d_mixed)

    attend_back(0)
    attend_back(1)
    w_out_sum.forward()
    attend_back(2)
    attend_back(3)

    def project_back(b):
        at = rows_of(b)
        d_proj = jnp.concatenate(
            [
                dgate_ref[at, :].astype(F32),
                dvalue_ref[at, :].astype(BF).astype(F32),
                dquery_ref[at, :].astype(F32),
                dkey_ref[at, :].astype(BF).astype(F32),
            ],
            axis=1,
        )
        d_pre = (d_proj * slope_ref[at, :]).astype(BF)
        dpre_ref[at, :] = d_pre
        normed, factor = normal(emb_ref[at, :].astype(F32))
        d_normed = mm_nt(d_pre, w_in_ref[...]).astype(BF).astype(F32)
        return normal_back(d_normed, normed, factor) + drows_ref[at, :]

    emb_sum = Scatter(ring(5), demb_ref, emb_land, emb_on, Q)
    demb_ref[rows_of(far), :] = project_back(far).astype(BF)
    emb_sum.first[0].start()
    emb_sum.first[1].start()
    d_right = project_back(right)
    demb_ref[rows_of(right), :] = (
        d_right + jnp.where(iota((Q, 1), 0) == 0, rest_ref[Q : Q + 1, :], 0.0)
    ).astype(BF)
    emb_sum.first[2].start()
    demb_ref[rows_of(left), :] = project_back(left).astype(BF)
    emb_sum.first[3].start()
    rest_ref[0:Q, :] += project_back(tx)
    emb_sum.forward()

    d_win = mm_tn(normed_ref[...], dpre_ref[...]).astype(BF)
    first, second = w_out_sum.finish()
    d_wout = jnp.concatenate([first, second], axis=0) + dout_part[rows_of(tx, DH), :].astype(F32)
    for j in range(4):
        weight_ref[j * D : (j + 1) * D, :] = d_win[:, j * DH : (j + 1) * DH]
        weight_ref[2048 + j * DH : 2048 + (j + 1) * DH, :] = d_wout[
            :, j * DH : (j + 1) * DH
        ].astype(BF)
    own = pl.ds(pl.multiple_of(dp * PIECE, 16), PIECE)

    def out_piece(pd):
        pltpu.make_async_remote_copy(
            src_ref=weight_ref.at[pl.ds(pl.multiple_of(pd * PIECE, 16), PIECE)],
            dst_ref=weight_in.at[own],
            send_sem=all_send.at[5],
            recv_sem=all_recv.at[5],
            device_id=(pd, tx),
            device_id_type=MESH,
        ).start()

    def back_piece(pd):
        pltpu.make_async_remote_copy(
            src_ref=weight_mine,
            dst_ref=weight_sum.at[own],
            send_sem=all_send.at[6],
            recv_sem=all_recv.at[6],
            device_id=(pd, tx),
            device_id_type=MESH,
        ).start()

    each_dp(dp, tx, out_piece)
    weight_in[own] = weight_ref[own]

    first, second = emb_sum.finish()
    d_hist = rest_ref[0:Q, :] + jnp.concatenate([first, second], axis=0)
    wait_rows(hist_out, (OWNERS - 1) * 16, all_send.at[1])
    put_slots(d_hist.astype(BF), slot_h, hist_out, CAP_H)
    spread_all(hist_out, hist_back, 16, all_send.at[3], all_recv.at[3], dp, tx)

    wait_rows(weight_in, (N_DP - 1) * PIECE, all_recv.at[5])
    total = weight_in[0:PIECE, :].astype(F32)
    for i in range(1, N_DP):
        total = total + weight_in[i * PIECE : (i + 1) * PIECE, :].astype(F32)
    weight_mine[...] = total.astype(BF)
    weight_sum[own] = total.astype(BF)
    each_dp(dp, tx, back_piece)

    wait_rows(hist_back, (OWNERS - 1) * 16, all_recv.at[3])
    gather_chunks(hist_back, picked_ref, 0, CAP_H)
    wait_rows(neg_back, (OWNERS - 1) * 16, all_recv.at[4])
    gather_chunks(neg_back, picked_ref, 512, CAP_N)
    wait_rows(weight_sum, (N_DP - 1) * PIECE, all_recv.at[6])
    results = [
        pltpu.make_async_copy(arrived_t_ref, ids_out, load_sems.at[0]),
        pltpu.make_async_copy(picked_ref, rows_out, load_sems.at[1]),
        pltpu.make_async_copy(weight_sum, weight_out, load_sems.at[2]),
    ]
    for move in results:
        move.start()
    for move in results:
        move.wait()
    for c in totals + hist.first + hist.second:
        c.wait_send()
    wait_rows(request_ref, OWNERS - 1, all_send.at[0])
    wait_rows(hist_out, (OWNERS - 1) * 16, all_send.at[3])
    wait_rows(neg_out, (OWNERS - 1) * 16, all_send.at[4])
    wait_rows(weight_in, (N_DP - 1) * PIECE, all_send.at[5])
    wait_rows(weight_in, (N_DP - 1) * PIECE, all_send.at[6])


def layer(ids, negs, lengths, table, w_in, w_out):
    sem = pltpu.SemaphoreType.DMA
    vm = pltpu.VMEM
    return pl.pallas_call(
        layer_kernel,
        out_shape=[
            jax.ShapeDtypeStruct((128, 128), jnp.int32),
            jax.ShapeDtypeStruct((12 * OWNERS, D), BF),
            jax.ShapeDtypeStruct((2560, 128), BF),
        ],
        in_specs=[VM, VM, SM, HB, HB, HB],
        out_specs=[HB] * 3,
        scratch_shapes=[
            vm((ROWS, D), BF),
            vm((OWNERS, 1, 128), jnp.int32),
            vm((OWNERS, 1, 128), jnp.int32),
            vm((128, 128), jnp.int32),
            vm((OWNERS * 16, 128), BF),
            vm((OWNERS * 16, 256), BF),
            vm((12 * OWNERS, D), BF),
            vm((OWNERS * 16, 128), BF),
            vm((OWNERS * 16, 256), BF),
            vm((OWNERS * 16, 128), BF),
            vm((OWNERS * 16, 256), BF),
            vm((D, D), BF),
            vm((D, D), BF),
            vm((1024, D), BF),
            vm((512, D), BF),
            vm((512, D), BF),
            vm((1024, D), BF),
            vm((1024, D), BF),
            vm((1024, D), F32),
            vm((1024, KEYS), BF),
            vm((1024, KEYS), F32),
            vm((1024, DH), F32),
            vm((1024, DH), F32),
            vm((4096, DH), BF),
            vm((1024, D), F32),
            vm((1024, DH), F32),
            vm((1024, D), BF),
            vm((512, 1024), F32),
            vm((512, 1024), BF),
            vm((4, 1, 1024), F32),
            vm((1, 1024), F32),
            vm((1024, D), F32),
            vm((4096, DH), BF),
            vm((6 * 512, DH), BF),
            vm((2 * 512, DH), BF),
            vm((D, D), BF),
            vm((6 * 64, D), BF),
            vm((2 * 64, D), BF),
            vm((1024, D), BF),
            vm((6 * 128, D), BF),
            vm((2 * 128, D), BF),
            vm((Q + 8, D), F32),
            vm((1024, DH), BF),
            vm((1024, DH), F32),
            vm((1024, DH), BF),
            vm((1024, DH), F32),
            vm((1024, D), BF),
            vm((2560, 128), BF),
            vm((2560, 128), BF),
            vm((PIECE, 128), BF),
            vm((2560, 128), BF),
            pltpu.SemaphoreType.REGULAR,
            sem((6,)),
            sem((7,)),
            sem((7,)),
            sem((6, 6)),
            sem((6, 6)),
            sem((3,)),
            sem((3,)),
        ],
        compiler_params=pltpu.CompilerParams(
            collective_id=0, has_side_effects=True, vmem_limit_bytes=56 * 1024 * 1024
        ),
        name="layer",
    )(ids, negs, lengths, table, w_in, w_out)


def gather_chunks(chunks_ref, rows_ref, at, cap):
    block = 128 // cap
    many = block * 16
    q, r = iota((128, many), 0), iota((128, many), 1)
    fold = one_zero(
        (lax.rem(q, block) == lax.div(r, 16)) & (lax.div(q, block) == lax.rem(r, cap))
    )
    for b in range(cap):
        wide = unfold(chunks_ref[b * many : (b + 1) * many, :], cap, 16 // cap)
        rows = mm(fold, wide).astype(BF)
        for k in range(cap):
            rows_ref[at + k * 128 + b * block : at + k * 128 + (b + 1) * block, :] = rows[
                k * block : (k + 1) * block
            ]


def add_kernel(ids_hbm, rows_hbm, weight_hbm, out_ref, w_in_ref, w_out_ref, ids_ref, rows_ref, weight_ref, sems):
    tile = out_ref.shape[0]
    step = pl.program_id(0)

    @pl.when(step == 0)
    def _():
        moves = [
            pltpu.make_async_copy(ids_hbm, ids_ref, sems.at[0]),
            pltpu.make_async_copy(rows_hbm, rows_ref, sems.at[1]),
            pltpu.make_async_copy(weight_hbm, weight_ref, sems.at[2]),
        ]
        for move in moves:
            move.start()
        for move in moves:
            move.wait()

    total = jnp.zeros((tile, D), F32)
    for k in range(0, CAP_H + CAP_N, 4):
        row = jnp.concatenate([ids_ref[k + j : k + j + 1, :] for j in range(4)], axis=1)
        put = one_zero(row == iota((tile, 512), 0) + step * tile)
        total = total + mm(put, rows_ref[k * 128 : (k + 4) * 128, :])
    out_ref[...] = total
    w_in_ref[...] = weight_ref[pl.ds(pl.multiple_of(step * 256, 256), 256), :].astype(F32)
    w_out_ref[...] = jnp.concatenate(
        [
            weight_ref[pl.ds(pl.multiple_of(2048 + c * 128 + step * 16, 16), 16), :]
            for c in range(4)
        ],
        axis=1,
    ).astype(F32)


def add_rows(ids, rows, weight):
    tile = 512
    anywhere = pl.BlockSpec(memory_space=pl.ANY)
    return pl.pallas_call(
        add_kernel,
        out_shape=[
            jax.ShapeDtypeStruct((ROWS, D), F32),
            jax.ShapeDtypeStruct((2048, DH), F32),
            jax.ShapeDtypeStruct((DH, D), F32),
        ],
        grid=(ROWS // tile,),
        in_specs=[anywhere] * 3,
        out_specs=[
            pl.BlockSpec((tile, D), lambda i: (i, 0)),
            pl.BlockSpec((256, DH), lambda i: (i, 0)),
            pl.BlockSpec((16, D), lambda i: (i, 0)),
        ],
        scratch_shapes=[
            pltpu.VMEM((128, 128), jnp.int32),
            pltpu.VMEM((12 * OWNERS, D), BF),
            pltpu.VMEM((2560, 128), BF),
            pltpu.SemaphoreType.DMA((3,)),
        ],
        compiler_params=pltpu.CompilerParams(vmem_limit_bytes=56 * 1024 * 1024),
        name="add_rows",
    )(ids, rows, weight)


def on_device(table, item_ids, negatives, lengths, w_in, w_out):
    ids, rows, weight = layer(item_ids.reshape(1, -1), negatives, lengths, table, w_in, w_out)
    grad_table, grad_w_in, grad_w_out = add_rows(ids, rows, weight)
    return (grad_table, grad_w_in.reshape(4, D, DH), grad_w_out)


def solution(mesh):
    placed = (
        P(("dp", "table"), None),
        P(("dp", "table")),
        P("dp", "table"),
        P("dp", None),
        P(None, None, "table"),
        P("table", None),
    )
    return jax.shard_map(
        on_device,
        mesh=mesh,
        in_specs=placed,
        out_specs=(P(("dp", "table"), None), P(None, None, "table"), P("table", None)),
        check_vma=False,
    )
```

```python
import functools
import jax
import jax.numpy as jnp
from jax import lax
from jax.experimental import pallas as pl
from jax.experimental.pallas import tpu as pltpu
from jax.sharding import PartitionSpec as P

DH = 128
D = 512
CAP_H = 4
CAP_N = 8
OWNERS = 128
N_DP = 32
N_TABLE = 4
ROWS = 4096
BF = jnp.bfloat16
F32 = jnp.float32
MESH = pl.DeviceIdType.MESH

epsilon = 1e-06
sharpness = 20.0


def iota(shape, dim):
    return lax.broadcasted_iota(jnp.int32, shape, dim)


def one_zero(mask):
    return jnp.where(mask, 1.0, 0.0).astype(BF)


def mm(a, b):
    return lax.dot_general(a, b, (((1,), (0,)), ((), ())), preferred_element_type=F32)


def mm_nt(a, b):
    return lax.dot_general(a, b, (((1,), (1,)), ((), ())), preferred_element_type=F32)


def mm_tn(a, b):
    return lax.dot_general(a, b, (((0,), (0,)), ((), ())), preferred_element_type=F32)


def position():
    dp = lax.axis_index("dp")
    tx = lax.axis_index("table")
    return dp, tx


def coordinates(dp, tx):
    z, y, c = lax.div(dp, 8), lax.rem(lax.div(dp, 2), 4), lax.rem(dp, 2)
    near = [(core, lax.rem(tx + dx, 4)) for core in (1 - c, c) for dx in range(4)]
    return z, y, near[4:] + near[:4]


def plane_base(z, y, step):
    return lax.rem(z + lax.div(step, 4), 4) * 8 + lax.rem(y + lax.rem(step, 4), 4) * 2


def each_partner(dp, tx, do):
    z, y, near = coordinates(dp, tx)

    def one(i, carry):
        base = plane_base(z, y, lax.rem(i * 7, 16))
        for core, x in near:
            do(base + core, x)
        return carry

    lax.fori_loop(1, 16, one, 0)
    for core, x in near[1:]:
        do(z * 8 + y * 2 + core, x)


def each_dp(dp, tx, do):
    z, y, near = coordinates(dp, tx)
    mine, other = near[0][0], near[4][0]

    def one(i, carry):
        base = plane_base(z, y, lax.rem(i * 7, 16))
        do(base + mine)
        do(base + other)
        return carry

    lax.fori_loop(1, 16, one, 0)
    do(z * 8 + y * 2 + other)


def signal(sem, dp, x):
    pl.semaphore_signal(sem, inc=1, device_id=(dp, x), device_id_type=MESH)


def greet_planes(barrier, dp, tx):
    z, y, near = coordinates(dp, tx)
    for core, x in near[1:]:
        signal(barrier, z * 8 + y * 2 + core, x)
    core, x = near[0]
    for i in range(1, 16):
        signal(barrier, plane_base(z, y, i) + core, x)


def greet_again(sem, dp, tx):
    z, y, near = coordinates(dp, tx)
    for core, x in near[1:]:
        signal(sem, z * 8 + y * 2 + core, x)


def spread_all(src, dst, chunk, send_sem, recv_sem, dp, tx):
    me = dp * 4 + tx
    land = pl.ds(pl.multiple_of(me * chunk, chunk), chunk)

    def one(pd, px):
        pltpu.make_async_remote_copy(
            src_ref=src.at[pl.ds(pl.multiple_of((pd * 4 + px) * chunk, chunk), chunk)],
            dst_ref=dst.at[land],
            send_sem=send_sem,
            recv_sem=recv_sem,
            device_id=(pd, px),
            device_id_type=MESH,
        ).start()

    each_partner(dp, tx, one)
    dst[land] = src[land]


def wait_rows(ref, count, sem):
    pltpu.make_async_copy(ref.at[pl.ds(0, count)], ref.at[pl.ds(0, count)], sem).wait()


class Ring:
    def __init__(self, dp, tx, send_sems, recv_sems):
        self.dp = dp
        self.tx = tx
        self.right = lax.rem(tx + 1, 4)
        self.left = lax.rem(tx + 3, 4)
        self.far = lax.rem(tx + 2, 4)
        self.send_sems = send_sems
        self.recv_sems = recv_sems

    def copy(self, src, dst, slot, to):
        return pltpu.make_async_remote_copy(
            src_ref=src,
            dst_ref=dst,
            send_sem=self.send_sems.at[slot],
            recv_sem=self.recv_sems.at[slot],
            device_id=(self.dp, to),
            device_id_type=MESH,
        )


class Gather:
    def __init__(self, ring, buf, block):
        h = block // 2
        r = ring

        def part(t, half):
            return buf.at[pl.ds(pl.multiple_of(t * block + half * h, h), h)]

        self.first = [
            r.copy(part(r.tx, 0), part(r.tx, 0), 0, r.right),
            r.copy(part(r.tx, 1), part(r.tx, 1), 1, r.left),
            r.copy(part(r.tx, 1), part(r.tx, 1), 2, r.right),
            r.copy(part(r.tx, 0), part(r.tx, 0), 3, r.left),
        ]
        self.second = [
            r.copy(part(r.left, 0), part(r.left, 0), 4, r.right),
            r.copy(part(r.right, 1), part(r.right, 1), 5, r.left),
        ]

    def start(self):
        for c in self.first:
            c.start()

    def forward(self):
        for c, d in zip(self.first[:2], self.second):
            c.wait_recv()
            d.start()

    def finish(self):
        for c in self.first[2:] + self.second:
            c.wait_recv()
        for c in self.first + self.second:
            c.wait_send()


class Scatter:
    def __init__(self, ring, part, land, onward, block):
        h = block // 2
        r = ring
        self.h = h
        self.ring = r
        self.part = part
        self.land = land
        self.onward = onward
        self.block = block

        self.first = [
            r.copy(self.at(r.far, 0), self.slot(0), 0, r.right),
            r.copy(self.at(r.far, 1), self.slot(1), 1, r.left),
            r.copy(self.at(r.right, 1), self.slot(2), 2, r.right),
            r.copy(self.at(r.left, 0), self.slot(3), 3, r.left),
        ]
        self.second = [
            r.copy(onward.at[pl.ds(0, h)], self.slot(4), 4, r.right),
            r.copy(onward.at[pl.ds(h, h)], self.slot(5), 5, r.left),
        ]

    def at(self, t, half):
        return self.part.at[self.span(t, half)]

    def span(self, t, half):
        return pl.ds(pl.multiple_of(t * self.block + half * self.h, self.h), self.h)

    def slot(self, i):
        return self.land.at[pl.ds(i * self.h, self.h)]

    def start(self):
        for c in self.first:
            c.start()

    def forward(self):
        h = self.h
        for i, t in enumerate((self.ring.right, self.ring.left)):
            self.first[i].wait_recv()
            self.onward[i * h : (i + 1) * h] = (
                self.land[i * h : (i + 1) * h].astype(F32) + self.part[self.span(t, i)].astype(F32)
            ).astype(BF)
            self.second[i].start()

    def finish(self):
        h = self.h
        for c in self.first[2:] + self.second:
            c.wait_recv()
        for c in self.first + self.second:
            c.wait_send()

        def got(i):
            return self.land[i * h : (i + 1) * h].astype(F32)

        return got(3) + got(4), got(2) + got(5)


def slots_of(ids):
    n = ids.shape[1]
    holder = lax.shift_right_logical(ids, 12)
    hits = iota((OWNERS, n), 0) == holder
    earlier = one_zero(iota((n, n), 0) < iota((n, n), 1))
    hits_b = one_zero(hits)
    before = jnp.sum(jnp.where(hits, mm(hits_b, earlier), 0.0), axis=0, keepdims=True)
    return holder, hits_b, before.astype(jnp.int32)


def wanted_rows(ids, hits_b, before, offset):
    n = ids.shape[1]
    marked = (ids & (ROWS - 1)) + 1
    chosen = iota((OWNERS, n), 0) == before + offset
    high = jnp.where(chosen, lax.shift_right_logical(marked, 6).astype(F32), 0.0).astype(BF)
    low = jnp.where(chosen, (marked & 63).astype(F32), 0.0).astype(BF)
    return 64.0 * mm_nt(hits_b, high) + mm_nt(hits_b, low)


def as_column(row):
    n = row.shape[1]
    wide = jnp.broadcast_to(row.astype(F32), (128, n))
    return jnp.transpose(wide)[:, 0:1].astype(jnp.int32)


def neg_row(negs_ref):
    return jnp.concatenate([negs_ref[u : u + 1, :] for u in range(4)], axis=1)


def part_mask(rows, width, per, parts):
    which = lax.rem(iota((rows, width), 0), 16) // per
    return [one_zero(which == c) for c in range(parts)]


def pick_parts(values, per, width):
    which = lax.div(lax.rem(iota((values.shape[0], width), 0), 16), per)
    out = values[:, 0:width]
    for c in range(1, values.shape[1] // width):
        out = jnp.where(which == c, values[:, c * width : (c + 1) * width], out)
    return out


def gather_rows(table, ids_col, out_ref, at):
    step = 1024

    def one(i, total):
        base = pl.multiple_of(i * step, step)
        pick = one_zero(ids_col == iota((512, step), 1) + i * step)
        return total + mm(pick, table[pl.ds(base, step), :])

    total = lax.fori_loop(0, ROWS // step, one, jnp.zeros((512, D), F32))
    out_ref[at : at + 512, :] = total.astype(BF)


def spread_chunks(rows_ref, chunks_ref, at, cap):
    width = cap * 32
    block = 128 // cap
    many = block * 16
    r, q = iota((many, 128), 0), iota((many, 128), 1)
    fold = one_zero(
        (lax.rem(q, block) == lax.div(r, 16)) & (lax.div(q, block) == lax.rem(r, cap))
    )
    for b in range(cap):
        rows = jnp.concatenate(
            [
                rows_ref[at + k * 128 + b * block : at + k * 128 + (b + 1) * block, :]
                for k in range(cap)
            ],
            axis=0,
        )
        chunks_ref[b * many : (b + 1) * many, :] = pick_parts(mm(fold, rows), cap, width).astype(BF)


def unfold(chunks, per, parts):
    rows, width = chunks.shape
    masks = part_mask(rows, width, per, parts)
    return jnp.concatenate([chunks * m for m in masks], axis=1)


def take_slots(chunks_ref, slot_col, cap):
    n = slot_col.shape[0]
    total = jnp.zeros((n, D), F32)
    step = 512
    for i in range(OWNERS * 16 // step):
        r = iota((n, step), 1) + i * step
        key = lax.div(r, 16) * cap + lax.rem(r, cap)
        total = total + mm(
            one_zero(slot_col == key),
            unfold(chunks_ref[i * step : (i + 1) * step, :], cap, 16 // cap),
        )
    return total.astype(BF)


def put_slots(rows, slot_row, chunks_ref, cap):
    n = slot_row.shape[1]
    step = 512
    for i in range(OWNERS * 16 // step):
        r = iota((step, n), 0) + i * step
        key = lax.div(r, 16) * cap + lax.rem(r, cap)
        chunks_ref[i * step : (i + 1) * step, :] = pick_parts(
            mm(one_zero(slot_row == key), rows), cap, cap * 32
        ).astype(BF)


def row_sum(values):
    return jnp.sum(values, axis=-1, keepdims=True)


def row_mean(values):
    return jnp.mean(values, axis=-1, keepdims=True)


def normal(values):
    center = values - row_mean(values)
    factor = lax.rsqrt(row_mean(center * center) + epsilon)
    return center * factor, factor


def normal_back(grad, normed, factor):
    return factor * (grad - row_mean(grad) - normed * row_mean(grad * normed))


def unit_factor(values):
    return lax.rsqrt(row_sum(values * values) + epsilon)


def unit_back(grad, values, factor):
    return factor * (grad - values * (factor * factor * row_sum(grad * values)))


class Users:
    def __init__(self, lengths_ref):
        self.lengths = [lengths_ref[0, u] for u in range(4)]
        self.ends = []
        end = 0
        for length in self.lengths:
            end = end + length
            self.ends.append(end)

    def segment(self, t):
        return sum(jnp.where(t >= end, 1, 0) for end in self.ends)

    def start(self, t):
        return sum(jnp.where(t >= e, n, 0) for e, n in zip(self.ends, self.lengths))

    def length(self, t):
        out = jnp.where(t >= 0, self.lengths[0], 0)
        for u in range(1, 4):
            out = jnp.where(t >= self.ends[u - 1], self.lengths[u], out)
        return out


VM = pl.BlockSpec(memory_space=pltpu.VMEM)
HB = pl.BlockSpec(memory_space=pl.ANY)
SM = pl.BlockSpec(memory_space=pltpu.SMEM)
Q = 256
KEYS = 768
SCALE = DH**-0.5
PIECE = 80


def layer_kernel(
    ids_ref,
    negs_ref,
    lengths_ref,
    table_hbm,
    w_in_hbm,
    w_out_hbm,
    ids_out,
    rows_out,
    weight_out,
    table_out,
    table_ref,
    request_ref,
    arrived_ref,
    arrived_t_ref,
    hist_back,
    neg_back,
    picked_ref,
    hist_out,
    neg_out,
    hist_in,
    neg_in,
    w_in_ref,
    w_out_ref,
    emb_ref,
    neg_ref,
    unit_ref,
    normed_ref,
    proj_ref,
    slope_ref,
    weights_ref,
    dweights_ref,
    mixed_ref,
    factor_ref,
    gated_ref,
    y_ref,
    y_factor_ref,
    y_unit_ref,
    grown_ref,
    shares_ref,
    total_ref,
    whole_ref,
    drows_ref,
    dgated_ref,
    dgated_land,
    dgated_on,
    dout_part,
    dout_land,
    dout_on,
    demb_ref,
    emb_land,
    emb_on,
    rest_ref,
    dgate_ref,
    dvalue_ref,
    dquery_ref,
    dkey_ref,
    dpre_ref,
    weight_ref,
    weight_in,
    weight_mine,
    weight_sum,
    met_sem,
    load_sems,
    all_send,
    all_recv,
    ring_send,
    ring_recv,
    total_send,
    total_recv,
):
    dp, tx = position()
    barrier = pltpu.get_barrier_semaphore()
    greet_planes(barrier, dp, tx)
    loads = [pltpu.make_async_copy(table_hbm, table_ref, load_sems.at[0])]
    for j in range(4):
        loads.append(
            pltpu.make_async_copy(
                w_in_hbm.at[j], w_in_ref.at[:, j * DH : (j + 1) * DH], load_sems.at[1 + j]
            )
        )
    loads.append(
        pltpu.make_async_copy(
            w_out_hbm, w_out_ref.at[pl.ds(pl.multiple_of(tx * DH, DH), DH)], load_sems.at[5]
        )
    )
    for load in loads:
        load.start()

    def ring(i):
        return Ring(dp, tx, ring_send.at[i], ring_recv.at[i])

    right, left, far = ring(0).right, ring(0).left, ring(0).far

    def rows_of(b, n=Q):
        return pl.ds(pl.multiple_of(b * n, n), n)

    ids, negs = ids_ref[...], neg_row(negs_ref)
    holder_h, hits_h, before_h = slots_of(ids)
    holder_n, hits_n, before_n = slots_of(negs)
    wanted = wanted_rows(ids, hits_h, before_h, 0) + wanted_rows(negs, hits_n, before_n, CAP_H)
    pl.semaphore_wait(barrier, 22)
    greet_again(met_sem, dp, tx)
    request_ref[:, 0, :] = wanted.astype(jnp.int32) - 1
    slot_h = holder_h * CAP_H + before_h
    slot_n = holder_n * CAP_N + before_n

    pl.semaphore_wait(met_sem, 7)
    spread_all(request_ref, arrived_ref, 1, all_send.at[0], all_recv.at[0], dp, tx)
    for load in loads:
        load.wait()
    w_outs = Gather(ring(1), w_out_ref, DH)
    w_outs.start()
    slot_h_col, slot_n_col = as_column(slot_h), as_column(slot_n)
    users = Users(lengths_ref)
    wait_rows(arrived_ref, OWNERS - 1, all_recv.at[0])

    arrived = arrived_ref[:, 0, :]
    columns = [arrived[:, k : k + 1] for k in range(CAP_H + CAP_N)]
    gather_rows(table_ref, jnp.concatenate(columns[0:4], axis=0), picked_ref, 0)
    spread_chunks(picked_ref, hist_out, 0, CAP_H)
    spread_all(hist_out, hist_in, 16, all_send.at[1], all_recv.at[1], dp, tx)
    w_outs.forward()
    gather_rows(table_ref, jnp.concatenate(columns[4:8], axis=0), picked_ref, 512)

    wait_rows(hist_in, (OWNERS - 1) * 16, all_recv.at[1])
    emb_ref[rows_of(tx), :] = take_slots(hist_in, slot_h_col, CAP_H)
    hist = Gather(ring(0), emb_ref, Q)
    hist.start()

    def project(b):
        at = rows_of(b)
        normed = normal(emb_ref[at, :].astype(F32))[0].astype(BF)
        normed_ref[at, :] = normed
        pre = mm(normed, w_in_ref[...])
        gate = lax.logistic(pre)
        proj_ref[at, :] = (pre * gate).astype(BF)
        slope_ref[at, :] = gate * (1.0 + pre * (1.0 - gate))

    gather_rows(table_ref, jnp.concatenate(columns[8:12], axis=0), picked_ref, 1024)
    hist.forward()
    spread_chunks(picked_ref, neg_out, 512, CAP_N)
    spread_all(neg_out, neg_in, 16, all_send.at[2], all_recv.at[2], dp, tx)
    project(tx)
    for c in hist.first[2:]:
        c.wait_recv()
    project(left)
    project(right)
    for c in hist.second:
        c.wait_recv()
    project(far)

    arrived_t_ref[...] = jnp.transpose(arrived.astype(F32)).astype(jnp.int32)

    mine = pl.multiple_of(tx * 1024, 1024)

    def keys_of(b):
        low = max(b - 2, 0)
        return slice(low * Q, (b + 1) * Q), low

    def attend(b):
        at = slice(b * Q, (b + 1) * Q)
        kr, low = keys_of(b)
        n = kr.stop - kr.start
        scores = mm_nt(proj_ref[at, 256:384], proj_ref[kr, 384:512]) * SCALE
        t = iota((Q, 1), 0) + b * Q
        s = iota((Q, n), 1) + low * Q
        seen = (s <= t) & (s >= users.start(t))
        share = 1.0 / users.length(t).astype(F32)
        gate = lax.logistic(scores)
        weights = jnp.where(seen, scores * gate * share, 0.0).astype(BF)
        weights_ref[at, 0:n] = weights
        dweights_ref[at, 0:n] = jnp.where(
            seen, gate * (1.0 + scores * (1.0 - gate)) * (share * SCALE), 0.0
        )
        mixed, factor = normal(mm(weights, proj_ref[kr, 128:256]))
        mixed_ref[at, :] = mixed
        factor_ref[at, :] = jnp.broadcast_to(factor, (Q, DH))
        gated_ref[pl.ds(mine + b * Q, Q), :] = (mixed * proj_ref[at, 0:128].astype(F32)).astype(BF)

    gates = Gather(ring(2), gated_ref, 1024)
    attend(0)
    attend(1)
    gates.first[0].start()
    gates.first[3].start()
    attend(2)
    attend(3)
    gates.first[1].start()
    gates.first[2].start()

    wait_rows(neg_in, (OWNERS - 1) * 16, all_recv.at[2])
    neg_ref[...] = take_slots(neg_in, slot_n_col, CAP_N)
    gates.forward()
    neg_f = neg_ref[...].astype(F32)
    neg_factor = unit_factor(neg_f)
    unit_ref[...] = (neg_f * neg_factor).astype(BF)
    w_outs.finish()
    arrived_t_ref[...] = jnp.transpose(arrived.astype(F32)).astype(jnp.int32)

    emb_f = emb_ref[rows_of(tx), :].astype(F32)
    follow = jnp.where(
        iota((Q, 1), 0) == Q - 1,
        emb_ref[rows_of(right), :].astype(F32)[0:1, :],
        pltpu.roll(emb_f, Q - 1, 0),
    )
    follow_factor = unit_factor(follow)
    follow_unit = (follow * follow_factor).astype(BF).astype(F32)
    t_row = iota((1, 1024), 1)
    segment = users.segment(t_row)
    valid = users.segment(t_row + 1) == segment
    users_of = [jnp.where(segment == u, 1.0, 0.0) for u in range(4)]
    gates.finish()

    for b in range(4):
        at = slice(b * Q, (b + 1) * Q)
        gated = jnp.concatenate(
            [gated_ref[h * 1024 + b * Q : h * 1024 + (b + 1) * Q, :] for h in range(4)], axis=1
        )
        y = emb_ref[at, :].astype(F32) + mm(gated, w_out_ref[...])
        factor = unit_factor(y)
        y_unit = (y * factor).astype(BF)
        y_ref[at, :] = y
        y_factor_ref[at, :] = jnp.broadcast_to(factor, (Q, DH))
        y_unit_ref[at, :] = y_unit
        grown = jnp.exp(sharpness * mm_nt(unit_ref[...], y_unit))
        grown = jnp.concatenate(
            [grown[u * DH : (u + 1) * DH, :] * users_of[u][:, at] for u in range(4)], axis=0
        )
        grown_ref[:, at] = grown
        total_ref[tx, :, at] = jnp.sum(grown, axis=0, keepdims=True)

    y_unit_f = y_unit_ref[rows_of(tx), :].astype(F32)
    grown_pos = jnp.exp(sharpness * row_sum(y_unit_f * follow_unit))
    own_lanes = pl.ds(pl.multiple_of(tx * Q, Q), Q)
    grown_pos_row = jnp.transpose(jnp.broadcast_to(grown_pos, (Q, DH)))[0:1, :]
    total_ref[tx, :, own_lanes] += grown_pos_row
    totals = [
        Ring(dp, tx, total_send, total_recv).copy(total_ref.at[tx], total_ref.at[tx], i, to)
        for i, to in enumerate((right, left, far))
    ]
    for c in totals:
        c.start()
    for c in totals:
        c.wait_recv()
    total = total_ref[0] + total_ref[1] + total_ref[2] + total_ref[3]
    whole_ref[...] = jnp.where(valid, sharpness / total, 0.0)
    scaled_own = jnp.transpose(jnp.broadcast_to(whole_ref[:, own_lanes], (DH, Q)))[:, 0:1]
    d_pos = jnp.where(scaled_own > 0.0, scaled_own * grown_pos - sharpness, 0.0)
    d_unit_pos = d_pos * follow_unit
    gate_sum = Scatter(ring(3), dgated_ref, dgated_land, dgated_on, 1024)
    for b in range(4):
        at = slice(b * Q, (b + 1) * Q)
        shares = (grown_ref[:, at] * whole_ref[:, at]).astype(BF)
        shares_ref[:, at] = shares
        d_unit = mm_tn(shares, unit_ref[...]) + jnp.where(tx == b, d_unit_pos, 0.0)
        d_rows = unit_back(d_unit, y_ref[at, :], y_factor_ref[at, :][:, 0:1])
        drows_ref[at, :] = d_rows
        d_gated = mm_nt(d_rows.astype(BF), w_out_ref[...]).astype(BF)
        for h in range(4):
            dgated_ref[h * 1024 + b * Q : h * 1024 + (b + 1) * Q, :] = d_gated[
                :, h * DH : (h + 1) * DH
            ]
        if b == 1:
            gate_sum.first[0].start()
            gate_sum.first[3].start()
    gate_sum.first[1].start()
    gate_sum.first[2].start()

    d_neg = unit_back(
        mm(shares_ref[...], y_unit_ref[...]),
        neg_ref[...].astype(F32),
        unit_factor(neg_ref[...].astype(F32)),
    )
    wait_rows(neg_out, (OWNERS - 1) * 16, all_send.at[2])
    put_slots(d_neg.astype(BF), slot_n, neg_out, CAP_N)
    gate_sum.forward()
    spread_all(neg_out, neg_back, 16, all_send.at[4], all_recv.at[4], dp, tx)
    for h in range(4):
        dout_part[h * DH : (h + 1) * DH, :] = mm_tn(
            gated_ref[h * 1024 : (h + 1) * 1024, :], drows_ref[...].astype(BF)
        ).astype(BF)
    w_out_sum = Scatter(ring(4), dout_part, dout_land, dout_on, DH)
    w_out_sum.start()
    d_follow = unit_back(d_pos * y_unit_f, follow, follow_factor)
    rest_ref[0:Q, :] = jnp.where(iota((Q, 1), 0) == 0, 0.0, pltpu.roll(d_follow, 1, 0))
    rest_ref[Q : Q + 8, :] = jnp.where(iota((8, 1), 0) == 0, d_follow[Q - 1 : Q, :], 0.0)
    dkey_ref[...] = jnp.zeros_like(dkey_ref)
    dvalue_ref[...] = jnp.zeros_like(dvalue_ref)
    halves = gate_sum.finish()

    def attend_back(b):
        at = slice(b * Q, (b + 1) * Q)
        kr, _ = keys_of(b)
        n = kr.stop - kr.start
        half = halves[b // 2][(b % 2) * Q : (b % 2 + 1) * Q, :]
        d_gated = half + dgated_ref[pl.ds(mine + b * Q, Q), :].astype(F32)
        mixed = mixed_ref[at, :]
        dgate_ref[at, :] = (d_gated * mixed).astype(BF)
        d_mixed = normal_back(
            d_gated * proj_ref[at, 0:128].astype(F32), mixed, factor_ref[at, :][:, 0:1]
        ).astype(BF)
        d_scores = (mm_nt(d_mixed, proj_ref[kr, 128:256]) * dweights_ref[at, 0:n]).astype(BF)
        dquery_ref[at, :] = mm(d_scores, proj_ref[kr, 384:512]).astype(BF)
        dkey_ref[kr, :] += mm_tn(d_scores, proj_ref[at, 256:384])
        dvalue_ref[kr, :] += mm_tn(weights_ref[at, 0:n], d_mixed)

    attend_back(0)
    attend_back(1)
    w_out_sum.forward()
    attend_back(2)
    attend_back(3)

    def project_back(b):
        at = rows_of(b)
        d_proj = jnp.concatenate(
            [
                dgate_ref[at, :].astype(F32),
                dvalue_ref[at, :].astype(BF).astype(F32),
                dquery_ref[at, :].astype(F32),
                dkey_ref[at, :].astype(BF).astype(F32),
            ],
            axis=1,
        )
        d_pre = (d_proj * slope_ref[at, :]).astype(BF)
        dpre_ref[at, :] = d_pre
        normed, factor = normal(emb_ref[at, :].astype(F32))
        d_normed = mm_nt(d_pre, w_in_ref[...]).astype(BF).astype(F32)
        return normal_back(d_normed, normed, factor) + drows_ref[at, :]

    emb_sum = Scatter(ring(5), demb_ref, emb_land, emb_on, Q)
    demb_ref[rows_of(far), :] = project_back(far).astype(BF)
    emb_sum.first[0].start()
    emb_sum.first[1].start()
    d_right = project_back(right)
    demb_ref[rows_of(right), :] = (
        d_right + jnp.where(iota((Q, 1), 0) == 0, rest_ref[Q : Q + 1, :], 0.0)
    ).astype(BF)
    emb_sum.first[2].start()
    demb_ref[rows_of(left), :] = project_back(left).astype(BF)
    emb_sum.first[3].start()
    rest_ref[0:Q, :] += project_back(tx)
    emb_sum.forward()

    d_win = mm_tn(normed_ref[...], dpre_ref[...]).astype(BF)
    first, second = w_out_sum.finish()
    d_wout = jnp.concatenate([first, second], axis=0) + dout_part[rows_of(tx, DH), :].astype(F32)
    for j in range(4):
        weight_ref[j * D : (j + 1) * D, :] = d_win[:, j * DH : (j + 1) * DH]
        weight_ref[2048 + j * DH : 2048 + (j + 1) * DH, :] = d_wout[
            :, j * DH : (j + 1) * DH
        ].astype(BF)
    own = pl.ds(pl.multiple_of(dp * PIECE, 16), PIECE)

    def out_piece(pd):
        pltpu.make_async_remote_copy(
            src_ref=weight_ref.at[pl.ds(pl.multiple_of(pd * PIECE, 16), PIECE)],
            dst_ref=weight_in.at[own],
            send_sem=all_send.at[5],
            recv_sem=all_recv.at[5],
            device_id=(pd, tx),
            device_id_type=MESH,
        ).start()

    def back_piece(pd):
        pltpu.make_async_remote_copy(
            src_ref=weight_mine,
            dst_ref=weight_sum.at[own],
            send_sem=all_send.at[6],
            recv_sem=all_recv.at[6],
            device_id=(pd, tx),
            device_id_type=MESH,
        ).start()

    each_dp(dp, tx, out_piece)
    weight_in[own] = weight_ref[own]

    wait_rows(neg_back, (OWNERS - 1) * 16, all_recv.at[4])
    gather_chunks(neg_back, picked_ref, 512, CAP_N)

    def add_negatives(i, carry):
        at = pl.ds(pl.multiple_of(i * 512, 512), 512)
        total = put_rows(arrived_t_ref, picked_ref, i * 512, 4, 512)
        total = total + put_rows(arrived_t_ref, picked_ref, i * 512, 8, 512)
        table_ref[at, :] = total.astype(BF)
        return carry

    lax.fori_loop(0, 4, add_negatives, 0)

    first, second = emb_sum.finish()
    d_hist = rest_ref[0:Q, :] + jnp.concatenate([first, second], axis=0)
    wait_rows(hist_out, (OWNERS - 1) * 16, all_send.at[1])
    put_slots(d_hist.astype(BF), slot_h, hist_out, CAP_H)
    spread_all(hist_out, hist_back, 16, all_send.at[3], all_recv.at[3], dp, tx)

    wait_rows(weight_in, (N_DP - 1) * PIECE, all_recv.at[5])
    total = weight_in[0:PIECE, :].astype(F32)
    for i in range(1, N_DP):
        total = total + weight_in[i * PIECE : (i + 1) * PIECE, :].astype(F32)
    weight_mine[...] = total.astype(BF)
    weight_sum[own] = total.astype(BF)
    each_dp(dp, tx, back_piece)

    lax.fori_loop(4, 8, add_negatives, 0)
    keep = pltpu.make_async_copy(table_ref, table_out, load_sems.at[3])
    keep.start()
    wait_rows(hist_back, (OWNERS - 1) * 16, all_recv.at[3])
    gather_chunks(hist_back, picked_ref, 0, CAP_H)
    wait_rows(weight_sum, (N_DP - 1) * PIECE, all_recv.at[6])
    results = [
        pltpu.make_async_copy(arrived_t_ref, ids_out, load_sems.at[0]),
        pltpu.make_async_copy(picked_ref.at[0:512], rows_out, load_sems.at[1]),
        pltpu.make_async_copy(weight_sum, weight_out, load_sems.at[2]),
    ]
    for move in results:
        move.start()
    for move in results + [keep]:
        move.wait()
    for c in totals + hist.first + hist.second:
        c.wait_send()
    wait_rows(request_ref, OWNERS - 1, all_send.at[0])
    wait_rows(hist_out, (OWNERS - 1) * 16, all_send.at[3])
    wait_rows(neg_out, (OWNERS - 1) * 16, all_send.at[4])
    wait_rows(weight_in, (N_DP - 1) * PIECE, all_send.at[5])
    wait_rows(weight_in, (N_DP - 1) * PIECE, all_send.at[6])


def layer(ids, negs, lengths, table, w_in, w_out):
    sem = pltpu.SemaphoreType.DMA
    vm = pltpu.VMEM
    return pl.pallas_call(
        layer_kernel,
        out_shape=[
            jax.ShapeDtypeStruct((128, 128), jnp.int32),
            jax.ShapeDtypeStruct((CAP_H * OWNERS, D), BF),
            jax.ShapeDtypeStruct((2560, 128), BF),
            jax.ShapeDtypeStruct((ROWS, D), BF),
        ],
        in_specs=[VM, VM, SM, HB, HB, HB],
        out_specs=[HB] * 4,
        scratch_shapes=[
            vm((ROWS, D), BF),
            vm((OWNERS, 1, 128), jnp.int32),
            vm((OWNERS, 1, 128), jnp.int32),
            vm((128, 128), jnp.int32),
            vm((OWNERS * 16, 128), BF),
            vm((OWNERS * 16, 256), BF),
            vm((12 * OWNERS, D), BF),
            vm((OWNERS * 16, 128), BF),
            vm((OWNERS * 16, 256), BF),
            vm((OWNERS * 16, 128), BF),
            vm((OWNERS * 16, 256), BF),
            vm((D, D), BF),
            vm((D, D), BF),
            vm((1024, D), BF),
            vm((512, D), BF),
            vm((512, D), BF),
            vm((1024, D), BF),
            vm((1024, D), BF),
            vm((1024, D), F32),
            vm((1024, KEYS), BF),
            vm((1024, KEYS), F32),
            vm((1024, DH), F32),
            vm((1024, DH), F32),
            vm((4096, DH), BF),
            vm((1024, D), F32),
            vm((1024, DH), F32),
            vm((1024, D), BF),
            vm((512, 1024), F32),
            vm((512, 1024), BF),
            vm((4, 1, 1024), F32),
            vm((1, 1024), F32),
            vm((1024, D), F32),
            vm((4096, DH), BF),
            vm((6 * 512, DH), BF),
            vm((2 * 512, DH), BF),
            vm((D, D), BF),
            vm((6 * 64, D), BF),
            vm((2 * 64, D), BF),
            vm((1024, D), BF),
            vm((6 * 128, D), BF),
            vm((2 * 128, D), BF),
            vm((Q + 8, D), F32),
            vm((1024, DH), BF),
            vm((1024, DH), F32),
            vm((1024, DH), BF),
            vm((1024, DH), F32),
            vm((1024, D), BF),
            vm((2560, 128), BF),
            vm((2560, 128), BF),
            vm((PIECE, 128), BF),
            vm((2560, 128), BF),
            pltpu.SemaphoreType.REGULAR,
            sem((6,)),
            sem((7,)),
            sem((7,)),
            sem((6, 6)),
            sem((6, 6)),
            sem((3,)),
            sem((3,)),
        ],
        compiler_params=pltpu.CompilerParams(
            collective_id=0, has_side_effects=True, vmem_limit_bytes=56 * 1024 * 1024
        ),
        name="layer",
    )(ids, negs, lengths, table, w_in, w_out)


def gather_chunks(chunks_ref, rows_ref, at, cap):
    block = 128 // cap
    many = block * 16
    q, r = iota((128, many), 0), iota((128, many), 1)
    fold = one_zero(
        (lax.rem(q, block) == lax.div(r, 16)) & (lax.div(q, block) == lax.rem(r, cap))
    )
    for b in range(cap):
        wide = unfold(chunks_ref[b * many : (b + 1) * many, :], cap, 16 // cap)
        rows = mm(fold, wide).astype(BF)
        for k in range(cap):
            rows_ref[at + k * 128 + b * block : at + k * 128 + (b + 1) * block, :] = rows[
                k * block : (k + 1) * block
            ]


def put_rows(ids_ref, rows_ref, first, slot, tile):
    row = jnp.concatenate([ids_ref[slot + j : slot + j + 1, :] for j in range(4)], axis=1)
    put = one_zero(row == iota((tile, 512), 0) + first)
    return mm(put, rows_ref[slot * 128 : (slot + 4) * 128, :])


def add_kernel(ids_hbm, rows_hbm, weight_hbm, part_ref, out_ref, w_in_ref, w_out_ref, ids_ref, rows_ref, weight_ref, sems):
    tile = out_ref.shape[0]
    step = pl.program_id(0)

    @pl.when(step == 0)
    def _():
        moves = [
            pltpu.make_async_copy(ids_hbm, ids_ref, sems.at[0]),
            pltpu.make_async_copy(rows_hbm, rows_ref, sems.at[1]),
            pltpu.make_async_copy(weight_hbm, weight_ref, sems.at[2]),
        ]
        for move in moves:
            move.start()
        for move in moves:
            move.wait()

    out_ref[...] = part_ref[...].astype(F32) + put_rows(ids_ref, rows_ref, step * tile, 0, tile)
    w_in_ref[...] = weight_ref[pl.ds(pl.multiple_of(step * 256, 256), 256), :].astype(F32)
    w_out_ref[...] = jnp.concatenate(
        [
            weight_ref[pl.ds(pl.multiple_of(2048 + c * 128 + step * 16, 16), 16), :]
            for c in range(4)
        ],
        axis=1,
    ).astype(F32)


def add_rows(ids, rows, weight, part):
    tile = 512
    anywhere = pl.BlockSpec(memory_space=pl.ANY)
    return pl.pallas_call(
        add_kernel,
        out_shape=[
            jax.ShapeDtypeStruct((ROWS, D), F32),
            jax.ShapeDtypeStruct((2048, DH), F32),
            jax.ShapeDtypeStruct((DH, D), F32),
        ],
        grid=(ROWS // tile,),
        in_specs=[anywhere] * 3 + [pl.BlockSpec((tile, D), lambda i: (i, 0))],
        out_specs=[
            pl.BlockSpec((tile, D), lambda i: (i, 0)),
            pl.BlockSpec((256, DH), lambda i: (i, 0)),
            pl.BlockSpec((16, D), lambda i: (i, 0)),
        ],
        scratch_shapes=[
            pltpu.VMEM((128, 128), jnp.int32),
            pltpu.VMEM((CAP_H * OWNERS, D), BF),
            pltpu.VMEM((2560, 128), BF),
            pltpu.SemaphoreType.DMA((3,)),
        ],
        compiler_params=pltpu.CompilerParams(vmem_limit_bytes=56 * 1024 * 1024),
        name="add_rows",
    )(ids, rows, weight, part)


def on_device(table, item_ids, negatives, lengths, w_in, w_out):
    ids, rows, weight, part = layer(item_ids.reshape(1, -1), negatives, lengths, table, w_in, w_out)
    grad_table, grad_w_in, grad_w_out = add_rows(ids, rows, weight, part)
    return (grad_table, grad_w_in.reshape(4, D, DH), grad_w_out)


def solution(mesh):
    placed = (
        P(("dp", "table"), None),
        P(("dp", "table")),
        P("dp", "table"),
        P("dp", None),
        P(None, None, "table"),
        P("table", None),
    )
    return jax.shard_map(
        on_device,
        mesh=mesh,
        in_specs=placed,
        out_specs=(P(("dp", "table"), None), P(None, None, "table"), P("table", None)),
        check_vma=False,
    )
```

```python
import functools
import jax
import jax.numpy as jnp
from jax import lax
from jax.experimental import pallas as pl
from jax.experimental.pallas import tpu as pltpu
from jax.sharding import PartitionSpec as P

DH = 128
D = 512
CAP_H = 4
CAP_N = 8
OWNERS = 128
N_DP = 32
N_TABLE = 4
ROWS = 4096
BF = jnp.bfloat16
F32 = jnp.float32
MESH = pl.DeviceIdType.MESH

epsilon = 1e-06
sharpness = 20.0


def iota(shape, dim):
    return lax.broadcasted_iota(jnp.int32, shape, dim)


def one_zero(mask):
    return jnp.where(mask, 1.0, 0.0).astype(BF)


def mm(a, b):
    return lax.dot_general(a, b, (((1,), (0,)), ((), ())), preferred_element_type=F32)


def mm_nt(a, b):
    return lax.dot_general(a, b, (((1,), (1,)), ((), ())), preferred_element_type=F32)


def mm_tn(a, b):
    return lax.dot_general(a, b, (((0,), (0,)), ((), ())), preferred_element_type=F32)


def position():
    dp = lax.axis_index("dp")
    tx = lax.axis_index("table")
    return dp, tx


def coordinates(dp, tx):
    z, y, c = lax.div(dp, 8), lax.rem(lax.div(dp, 2), 4), lax.rem(dp, 2)
    near = [(core, lax.rem(tx + dx, 4)) for core in (1 - c, c) for dx in range(4)]
    return z, y, near[4:] + near[:4]


def plane_base(z, y, step):
    return lax.rem(z + lax.div(step, 4), 4) * 8 + lax.rem(y + lax.rem(step, 4), 4) * 2


def each_partner(dp, tx, do):
    z, y, near = coordinates(dp, tx)

    def one(i, carry):
        base = plane_base(z, y, lax.rem(i * 7, 16))
        for core, x in near:
            do(base + core, x)
        return carry

    lax.fori_loop(1, 16, one, 0)
    for core, x in near[1:]:
        do(z * 8 + y * 2 + core, x)


def each_dp(dp, tx, do):
    z, y, near = coordinates(dp, tx)
    mine, other = near[0][0], near[4][0]

    def one(i, carry):
        base = plane_base(z, y, lax.rem(i * 7, 16))
        do(base + mine)
        do(base + other)
        return carry

    lax.fori_loop(1, 16, one, 0)
    do(z * 8 + y * 2 + other)


def signal(sem, dp, x):
    pl.semaphore_signal(sem, inc=1, device_id=(dp, x), device_id_type=MESH)


def greet_planes(barrier, dp, tx):
    z, y, near = coordinates(dp, tx)
    for core, x in near[1:]:
        signal(barrier, z * 8 + y * 2 + core, x)
    core, x = near[0]
    for i in range(1, 16):
        signal(barrier, plane_base(z, y, i) + core, x)


def greet_again(sem, dp, tx):
    z, y, near = coordinates(dp, tx)
    for core, x in near[1:]:
        signal(sem, z * 8 + y * 2 + core, x)


def spread_all(src, dst, chunk, send_sem, recv_sem, dp, tx):
    me = dp * 4 + tx
    land = pl.ds(pl.multiple_of(me * chunk, chunk), chunk)

    def one(pd, px):
        pltpu.make_async_remote_copy(
            src_ref=src.at[pl.ds(pl.multiple_of((pd * 4 + px) * chunk, chunk), chunk)],
            dst_ref=dst.at[land],
            send_sem=send_sem,
            recv_sem=recv_sem,
            device_id=(pd, px),
            device_id_type=MESH,
        ).start()

    each_partner(dp, tx, one)
    dst[land] = src[land]


def wait_rows(ref, count, sem):
    pltpu.make_async_copy(ref.at[pl.ds(0, count)], ref.at[pl.ds(0, count)], sem).wait()


class Ring:
    def __init__(self, dp, tx, send_sems, recv_sems):
        self.dp = dp
        self.tx = tx
        self.right = lax.rem(tx + 1, 4)
        self.left = lax.rem(tx + 3, 4)
        self.far = lax.rem(tx + 2, 4)
        self.send_sems = send_sems
        self.recv_sems = recv_sems

    def copy(self, src, dst, slot, to):
        return pltpu.make_async_remote_copy(
            src_ref=src,
            dst_ref=dst,
            send_sem=self.send_sems.at[slot],
            recv_sem=self.recv_sems.at[slot],
            device_id=(self.dp, to),
            device_id_type=MESH,
        )


class Gather:
    def __init__(self, ring, buf, block):
        h = block // 2
        r = ring

        def part(t, half):
            return buf.at[pl.ds(pl.multiple_of(t * block + half * h, h), h)]

        self.first = [
            r.copy(part(r.tx, 0), part(r.tx, 0), 0, r.right),
            r.copy(part(r.tx, 1), part(r.tx, 1), 1, r.left),
            r.copy(part(r.tx, 1), part(r.tx, 1), 2, r.right),
            r.copy(part(r.tx, 0), part(r.tx, 0), 3, r.left),
        ]
        self.second = [
            r.copy(part(r.left, 0), part(r.left, 0), 4, r.right),
            r.copy(part(r.right, 1), part(r.right, 1), 5, r.left),
        ]

    def start(self):
        for c in self.first:
            c.start()

    def forward(self):
        for c, d in zip(self.first[:2], self.second):
            c.wait_recv()
            d.start()

    def arrived(self, half):
        self.first[3 - half].wait_recv()
        self.second[half].wait_recv()

    def sent(self):
        for c in self.first + self.second:
            c.wait_send()

    def finish(self):
        self.arrived(0)
        self.arrived(1)
        self.sent()


class Scatter:
    def __init__(self, ring, part, land, onward, block):
        h = block // 2
        r = ring
        self.h = h
        self.ring = r
        self.part = part
        self.land = land
        self.onward = onward
        self.block = block

        self.first = [
            r.copy(self.at(r.far, 0), self.slot(0), 0, r.right),
            r.copy(self.at(r.far, 1), self.slot(1), 1, r.left),
            r.copy(self.at(r.right, 1), self.slot(2), 2, r.right),
            r.copy(self.at(r.left, 0), self.slot(3), 3, r.left),
        ]
        self.second = [
            r.copy(onward.at[pl.ds(0, h)], self.slot(4), 4, r.right),
            r.copy(onward.at[pl.ds(h, h)], self.slot(5), 5, r.left),
        ]

    def at(self, t, half):
        return self.part.at[self.span(t, half)]

    def span(self, t, half):
        return pl.ds(pl.multiple_of(t * self.block + half * self.h, self.h), self.h)

    def slot(self, i):
        return self.land.at[pl.ds(i * self.h, self.h)]

    def start(self):
        for c in self.first:
            c.start()

    def forward(self):
        h = self.h
        for i, t in enumerate((self.ring.right, self.ring.left)):
            self.first[i].wait_recv()
            self.onward[i * h : (i + 1) * h] = (
                self.land[i * h : (i + 1) * h].astype(F32) + self.part[self.span(t, i)].astype(F32)
            ).astype(BF)
            self.second[i].start()

    def half(self, i):
        h = self.h
        self.first[3 - i].wait_recv()
        self.second[i].wait_recv()

        def got(j):
            return self.land[j * h : (j + 1) * h].astype(F32)

        return got(3 - i) + got(4 + i)

    def sent(self):
        for c in self.first + self.second:
            c.wait_send()

    def finish(self):
        halves = self.half(0), self.half(1)
        self.sent()
        return halves


def slots_of(ids):
    n = ids.shape[1]
    holder = lax.shift_right_logical(ids, 12)
    hits = iota((OWNERS, n), 0) == holder
    earlier = one_zero(iota((n, n), 0) < iota((n, n), 1))
    hits_b = one_zero(hits)
    before = jnp.sum(jnp.where(hits, mm(hits_b, earlier), 0.0), axis=0, keepdims=True)
    return holder, hits_b, before.astype(jnp.int32)


def wanted_rows(ids, hits_b, before, offset):
    n = ids.shape[1]
    marked = (ids & (ROWS - 1)) + 1
    chosen = iota((OWNERS, n), 0) == before + offset
    high = jnp.where(chosen, lax.shift_right_logical(marked, 6).astype(F32), 0.0).astype(BF)
    low = jnp.where(chosen, (marked & 63).astype(F32), 0.0).astype(BF)
    return 64.0 * mm_nt(hits_b, high) + mm_nt(hits_b, low)


def as_column(row):
    n = row.shape[1]
    wide = jnp.broadcast_to(row.astype(F32), (128, n))
    return jnp.transpose(wide)[:, 0:1].astype(jnp.int32)


def neg_row(negs_ref):
    return jnp.concatenate([negs_ref[u : u + 1, :] for u in range(4)], axis=1)


def part_mask(rows, width, per, parts):
    which = lax.rem(iota((rows, width), 0), 16) // per
    return [one_zero(which == c) for c in range(parts)]


def pick_parts(values, per, width):
    which = lax.div(lax.rem(iota((values.shape[0], width), 0), 16), per)
    out = values[:, 0:width]
    for c in range(1, values.shape[1] // width):
        out = jnp.where(which == c, values[:, c * width : (c + 1) * width], out)
    return out


def gather_rows(table, ids_col, out_ref, at):
    step = 1024

    def one(i, total):
        base = pl.multiple_of(i * step, step)
        pick = one_zero(ids_col == iota((512, step), 1) + i * step)
        return total + mm(pick, table[pl.ds(base, step), :])

    total = lax.fori_loop(0, ROWS // step, one, jnp.zeros((512, D), F32))
    out_ref[at : at + 512, :] = total.astype(BF)


def spread_chunks(rows_ref, chunks_ref, at, cap):
    width = cap * 32
    block = 128 // cap
    many = block * 16
    r, q = iota((many, 128), 0), iota((many, 128), 1)
    fold = one_zero(
        (lax.rem(q, block) == lax.div(r, 16)) & (lax.div(q, block) == lax.rem(r, cap))
    )
    for b in range(cap):
        rows = jnp.concatenate(
            [
                rows_ref[at + k * 128 + b * block : at + k * 128 + (b + 1) * block, :]
                for k in range(cap)
            ],
            axis=0,
        )
        chunks_ref[b * many : (b + 1) * many, :] = pick_parts(mm(fold, rows), cap, width).astype(BF)


def unfold(chunks, per, parts):
    rows, width = chunks.shape
    masks = part_mask(rows, width, per, parts)
    return jnp.concatenate([chunks * m for m in masks], axis=1)


def take_slots(chunks_ref, slot_col, cap):
    n = slot_col.shape[0]
    total = jnp.zeros((n, D), F32)
    step = 512
    for i in range(OWNERS * 16 // step):
        r = iota((n, step), 1) + i * step
        key = lax.div(r, 16) * cap + lax.rem(r, cap)
        total = total + mm(
            one_zero(slot_col == key),
            unfold(chunks_ref[i * step : (i + 1) * step, :], cap, 16 // cap),
        )
    return total.astype(BF)


def put_slots(rows, slot_row, chunks_ref, cap):
    n = slot_row.shape[1]
    step = 512
    for i in range(OWNERS * 16 // step):
        r = iota((step, n), 0) + i * step
        key = lax.div(r, 16) * cap + lax.rem(r, cap)
        chunks_ref[i * step : (i + 1) * step, :] = pick_parts(
            mm(one_zero(slot_row == key), rows), cap, cap * 32
        ).astype(BF)


def row_sum(values):
    return jnp.sum(values, axis=-1, keepdims=True)


def row_mean(values):
    return jnp.mean(values, axis=-1, keepdims=True)


def normal(values):
    center = values - row_mean(values)
    factor = lax.rsqrt(row_mean(center * center) + epsilon)
    return center * factor, factor


def normal_back(grad, normed, factor):
    return factor * (grad - row_mean(grad) - normed * row_mean(grad * normed))


def unit_factor(values):
    return lax.rsqrt(row_sum(values * values) + epsilon)


def unit_back(grad, values, factor):
    return factor * (grad - values * (factor * factor * row_sum(grad * values)))


class Users:
    def __init__(self, lengths_ref):
        self.lengths = [lengths_ref[0, u] for u in range(4)]
        self.ends = []
        end = 0
        for length in self.lengths:
            end = end + length
            self.ends.append(end)

    def segment(self, t):
        return sum(jnp.where(t >= end, 1, 0) for end in self.ends)

    def start(self, t):
        return sum(jnp.where(t >= e, n, 0) for e, n in zip(self.ends, self.lengths))

    def length(self, t):
        out = jnp.where(t >= 0, self.lengths[0], 0)
        for u in range(1, 4):
            out = jnp.where(t >= self.ends[u - 1], self.lengths[u], out)
        return out


VM = pl.BlockSpec(memory_space=pltpu.VMEM)
HB = pl.BlockSpec(memory_space=pl.ANY)
SM = pl.BlockSpec(memory_space=pltpu.SMEM)
Q = 256
KEYS = 768
SCALE = DH**-0.5
PIECE = 80


def layer_kernel(
    ids_ref,
    negs_ref,
    lengths_ref,
    table_hbm,
    w_in_hbm,
    w_out_hbm,
    ids_out,
    rows_out,
    weight_out,
    table_out,
    table_ref,
    request_ref,
    arrived_ref,
    arrived_t_ref,
    hist_back,
    neg_back,
    picked_ref,
    hist_out,
    neg_out,
    hist_in,
    neg_in,
    w_in_ref,
    w_out_ref,
    emb_ref,
    neg_ref,
    unit_ref,
    normed_ref,
    proj_ref,
    slope_ref,
    weights_ref,
    dweights_ref,
    mixed_ref,
    factor_ref,
    gated_ref,
    y_ref,
    y_factor_ref,
    y_unit_ref,
    grown_ref,
    shares_ref,
    total_ref,
    whole_ref,
    drows_ref,
    dgated_ref,
    dgated_land,
    dgated_on,
    dout_part,
    dout_land,
    dout_on,
    demb_ref,
    emb_land,
    emb_on,
    rest_ref,
    dgate_ref,
    dvalue_ref,
    dquery_ref,
    dkey_ref,
    dpre_ref,
    weight_ref,
    weight_in,
    weight_mine,
    weight_sum,
    met_sem,
    load_sems,
    all_send,
    all_recv,
    ring_send,
    ring_recv,
    total_send,
    total_recv,
):
    dp, tx = position()
    barrier = pltpu.get_barrier_semaphore()
    greet_planes(barrier, dp, tx)
    loads = [pltpu.make_async_copy(table_hbm, table_ref, load_sems.at[0])]
    for j in range(4):
        loads.append(
            pltpu.make_async_copy(
                w_in_hbm.at[j], w_in_ref.at[:, j * DH : (j + 1) * DH], load_sems.at[1 + j]
            )
        )
    loads.append(
        pltpu.make_async_copy(
            w_out_hbm, w_out_ref.at[pl.ds(pl.multiple_of(tx * DH, DH), DH)], load_sems.at[5]
        )
    )
    for load in loads:
        load.start()

    def ring(i):
        return Ring(dp, tx, ring_send.at[i], ring_recv.at[i])

    right, left, far = ring(0).right, ring(0).left, ring(0).far

    def rows_of(b, n=Q):
        return pl.ds(pl.multiple_of(b * n, n), n)

    ids, negs = ids_ref[...], neg_row(negs_ref)
    holder_h, hits_h, before_h = slots_of(ids)
    holder_n, hits_n, before_n = slots_of(negs)
    wanted = wanted_rows(ids, hits_h, before_h, 0) + wanted_rows(negs, hits_n, before_n, CAP_H)
    pl.semaphore_wait(barrier, 22)
    greet_again(met_sem, dp, tx)
    request_ref[:, 0, :] = wanted.astype(jnp.int32) - 1
    slot_h = holder_h * CAP_H + before_h
    slot_n = holder_n * CAP_N + before_n

    pl.semaphore_wait(met_sem, 7)
    spread_all(request_ref, arrived_ref, 1, all_send.at[0], all_recv.at[0], dp, tx)
    for load in loads:
        load.wait()
    w_outs = Gather(ring(1), w_out_ref, DH)
    w_outs.start()
    slot_h_col, slot_n_col = as_column(slot_h), as_column(slot_n)
    users = Users(lengths_ref)
    wait_rows(arrived_ref, OWNERS - 1, all_recv.at[0])

    arrived = arrived_ref[:, 0, :]
    columns = [arrived[:, k : k + 1] for k in range(CAP_H + CAP_N)]
    gather_rows(table_ref, jnp.concatenate(columns[0:4], axis=0), picked_ref, 0)
    spread_chunks(picked_ref, hist_out, 0, CAP_H)
    spread_all(hist_out, hist_in, 16, all_send.at[1], all_recv.at[1], dp, tx)
    w_outs.forward()
    gather_rows(table_ref, jnp.concatenate(columns[4:8], axis=0), picked_ref, 512)

    wait_rows(hist_in, (OWNERS - 1) * 16, all_recv.at[1])
    emb_ref[rows_of(tx), :] = take_slots(hist_in, slot_h_col, CAP_H)
    hist = Gather(ring(0), emb_ref, Q)
    hist.start()

    def project(b):
        at = rows_of(b)
        normed = normal(emb_ref[at, :].astype(F32))[0].astype(BF)
        normed_ref[at, :] = normed
        pre = mm(normed, w_in_ref[...])
        gate = lax.logistic(pre)
        proj_ref[at, :] = (pre * gate).astype(BF)
        slope_ref[at, :] = gate * (1.0 + pre * (1.0 - gate))

    gather_rows(table_ref, jnp.concatenate(columns[8:12], axis=0), picked_ref, 1024)
    hist.forward()
    spread_chunks(picked_ref, neg_out, 512, CAP_N)
    spread_all(neg_out, neg_in, 16, all_send.at[2], all_recv.at[2], dp, tx)
    project(tx)
    for c in hist.first[2:]:
        c.wait_recv()
    project(left)
    project(right)
    for c in hist.second:
        c.wait_recv()
    project(far)

    arrived_t_ref[...] = jnp.transpose(arrived.astype(F32)).astype(jnp.int32)

    mine = pl.multiple_of(tx * 1024, 1024)

    def keys_of(b):
        low = max(b - 2, 0)
        return slice(low * Q, (b + 1) * Q), low

    def attend(b):
        at = slice(b * Q, (b + 1) * Q)
        kr, low = keys_of(b)
        n = kr.stop - kr.start
        scores = mm_nt(proj_ref[at, 256:384], proj_ref[kr, 384:512]) * SCALE
        t = iota((Q, 1), 0) + b * Q
        s = iota((Q, n), 1) + low * Q
        seen = (s <= t) & (s >= users.start(t))
        share = 1.0 / users.length(t).astype(F32)
        gate = lax.logistic(scores)
        weights = jnp.where(seen, scores * gate * share, 0.0).astype(BF)
        weights_ref[at, 0:n] = weights
        dweights_ref[at, 0:n] = jnp.where(
            seen, gate * (1.0 + scores * (1.0 - gate)) * (share * SCALE), 0.0
        )
        mixed, factor = normal(mm(weights, proj_ref[kr, 128:256]))
        mixed_ref[at, :] = mixed
        factor_ref[at, :] = jnp.broadcast_to(factor, (Q, DH))
        gated_ref[pl.ds(mine + b * Q, Q), :] = (mixed * proj_ref[at, 0:128].astype(F32)).astype(BF)

    gates = Gather(ring(2), gated_ref, 1024)
    attend(0)
    attend(1)
    gates.first[0].start()
    gates.first[3].start()
    attend(2)
    attend(3)
    gates.first[1].start()
    gates.first[2].start()

    wait_rows(neg_in, (OWNERS - 1) * 16, all_recv.at[2])
    neg_ref[...] = take_slots(neg_in, slot_n_col, CAP_N)
    gates.forward()
    neg_f = neg_ref[...].astype(F32)
    neg_factor = unit_factor(neg_f)
    unit_ref[...] = (neg_f * neg_factor).astype(BF)
    w_outs.finish()
    arrived_t_ref[...] = jnp.transpose(arrived.astype(F32)).astype(jnp.int32)

    emb_f = emb_ref[rows_of(tx), :].astype(F32)
    follow = jnp.where(
        iota((Q, 1), 0) == Q - 1,
        emb_ref[rows_of(right), :].astype(F32)[0:1, :],
        pltpu.roll(emb_f, Q - 1, 0),
    )
    follow_factor = unit_factor(follow)
    follow_unit = (follow * follow_factor).astype(BF).astype(F32)
    t_row = iota((1, 1024), 1)
    segment = users.segment(t_row)
    valid = users.segment(t_row + 1) == segment
    users_of = [jnp.where(segment == u, 1.0, 0.0) for u in range(4)]
    gates.arrived(0)

    for b in range(4):
        if b == 2:
            gates.arrived(1)
        at = slice(b * Q, (b + 1) * Q)
        gated = jnp.concatenate(
            [gated_ref[h * 1024 + b * Q : h * 1024 + (b + 1) * Q, :] for h in range(4)], axis=1
        )
        y = emb_ref[at, :].astype(F32) + mm(gated, w_out_ref[...])
        factor = unit_factor(y)
        y_unit = (y * factor).astype(BF)
        y_ref[at, :] = y
        y_factor_ref[at, :] = jnp.broadcast_to(factor, (Q, DH))
        y_unit_ref[at, :] = y_unit
        grown = jnp.exp(sharpness * mm_nt(unit_ref[...], y_unit))
        grown = jnp.concatenate(
            [grown[u * DH : (u + 1) * DH, :] * users_of[u][:, at] for u in range(4)], axis=0
        )
        grown_ref[:, at] = grown
        total_ref[tx, :, at] = jnp.sum(grown, axis=0, keepdims=True)

    y_unit_f = y_unit_ref[rows_of(tx), :].astype(F32)
    grown_pos = jnp.exp(sharpness * row_sum(y_unit_f * follow_unit))
    own_lanes = pl.ds(pl.multiple_of(tx * Q, Q), Q)
    grown_pos_row = jnp.transpose(jnp.broadcast_to(grown_pos, (Q, DH)))[0:1, :]
    total_ref[tx, :, own_lanes] += grown_pos_row
    totals = [
        Ring(dp, tx, total_send, total_recv).copy(total_ref.at[tx], total_ref.at[tx], i, to)
        for i, to in enumerate((right, left, far))
    ]
    for c in totals:
        c.start()
    for c in totals:
        c.wait_recv()
    total = total_ref[0] + total_ref[1] + total_ref[2] + total_ref[3]
    whole_ref[...] = jnp.where(valid, sharpness / total, 0.0)
    scaled_own = jnp.transpose(jnp.broadcast_to(whole_ref[:, own_lanes], (DH, Q)))[:, 0:1]
    d_pos = jnp.where(scaled_own > 0.0, scaled_own * grown_pos - sharpness, 0.0)
    d_unit_pos = d_pos * follow_unit
    gate_sum = Scatter(ring(3), dgated_ref, dgated_land, dgated_on, 1024)
    for b in range(4):
        at = slice(b * Q, (b + 1) * Q)
        shares = (grown_ref[:, at] * whole_ref[:, at]).astype(BF)
        shares_ref[:, at] = shares
        d_unit = mm_tn(shares, unit_ref[...]) + jnp.where(tx == b, d_unit_pos, 0.0)
        d_rows = unit_back(d_unit, y_ref[at, :], y_factor_ref[at, :][:, 0:1])
        drows_ref[at, :] = d_rows
        d_gated = mm_nt(d_rows.astype(BF), w_out_ref[...]).astype(BF)
        for h in range(4):
            dgated_ref[h * 1024 + b * Q : h * 1024 + (b + 1) * Q, :] = d_gated[
                :, h * DH : (h + 1) * DH
            ]
        if b == 1:
            gate_sum.first[0].start()
            gate_sum.first[3].start()
    gate_sum.first[1].start()
    gate_sum.first[2].start()

    d_neg = unit_back(
        mm(shares_ref[...], y_unit_ref[...]),
        neg_ref[...].astype(F32),
        unit_factor(neg_ref[...].astype(F32)),
    )
    wait_rows(neg_out, (OWNERS - 1) * 16, all_send.at[2])
    put_slots(d_neg.astype(BF), slot_n, neg_out, CAP_N)
    gate_sum.forward()
    spread_all(neg_out, neg_back, 16, all_send.at[4], all_recv.at[4], dp, tx)
    for h in range(4):
        dout_part[h * DH : (h + 1) * DH, :] = mm_tn(
            gated_ref[h * 1024 : (h + 1) * 1024, :], drows_ref[...].astype(BF)
        ).astype(BF)
    w_out_sum = Scatter(ring(4), dout_part, dout_land, dout_on, DH)
    w_out_sum.start()
    d_follow = unit_back(d_pos * y_unit_f, follow, follow_factor)
    rest_ref[0:Q, :] = jnp.where(iota((Q, 1), 0) == 0, 0.0, pltpu.roll(d_follow, 1, 0))
    rest_ref[Q : Q + 8, :] = jnp.where(iota((8, 1), 0) == 0, d_follow[Q - 1 : Q, :], 0.0)
    dkey_ref[...] = jnp.zeros_like(dkey_ref)
    dvalue_ref[...] = jnp.zeros_like(dvalue_ref)
    halves = [gate_sum.half(0)]

    def attend_back(b):
        at = slice(b * Q, (b + 1) * Q)
        kr, _ = keys_of(b)
        n = kr.stop - kr.start
        half = halves[b // 2][(b % 2) * Q : (b % 2 + 1) * Q, :]
        d_gated = half + dgated_ref[pl.ds(mine + b * Q, Q), :].astype(F32)
        mixed = mixed_ref[at, :]
        dgate_ref[at, :] = (d_gated * mixed).astype(BF)
        d_mixed = normal_back(
            d_gated * proj_ref[at, 0:128].astype(F32), mixed, factor_ref[at, :][:, 0:1]
        ).astype(BF)
        d_scores = (mm_nt(d_mixed, proj_ref[kr, 128:256]) * dweights_ref[at, 0:n]).astype(BF)
        dquery_ref[at, :] = mm(d_scores, proj_ref[kr, 384:512]).astype(BF)
        dkey_ref[kr, :] += mm_tn(d_scores, proj_ref[at, 256:384])
        dvalue_ref[kr, :] += mm_tn(weights_ref[at, 0:n], d_mixed)

    attend_back(0)
    attend_back(1)
    w_out_sum.forward()
    halves.append(gate_sum.half(1))
    attend_back(2)
    attend_back(3)

    def project_back(b):
        at = rows_of(b)
        d_proj = jnp.concatenate(
            [
                dgate_ref[at, :].astype(F32),
                dvalue_ref[at, :].astype(BF).astype(F32),
                dquery_ref[at, :].astype(F32),
                dkey_ref[at, :].astype(BF).astype(F32),
            ],
            axis=1,
        )
        d_pre = (d_proj * slope_ref[at, :]).astype(BF)
        dpre_ref[at, :] = d_pre
        normed, factor = normal(emb_ref[at, :].astype(F32))
        d_normed = mm_nt(d_pre, w_in_ref[...]).astype(BF).astype(F32)
        return normal_back(d_normed, normed, factor) + drows_ref[at, :]

    emb_sum = Scatter(ring(5), demb_ref, emb_land, emb_on, Q)
    demb_ref[rows_of(far), :] = project_back(far).astype(BF)
    emb_sum.first[0].start()
    emb_sum.first[1].start()
    d_right = project_back(right)
    demb_ref[rows_of(right), :] = (
        d_right + jnp.where(iota((Q, 1), 0) == 0, rest_ref[Q : Q + 1, :], 0.0)
    ).astype(BF)
    emb_sum.first[2].start()
    demb_ref[rows_of(left), :] = project_back(left).astype(BF)
    emb_sum.first[3].start()
    rest_ref[0:Q, :] += project_back(tx)
    emb_sum.forward()

    d_win = mm_tn(normed_ref[...], dpre_ref[...]).astype(BF)
    first, second = w_out_sum.finish()
    d_wout = jnp.concatenate([first, second], axis=0) + dout_part[rows_of(tx, DH), :].astype(F32)
    for j in range(4):
        weight_ref[j * D : (j + 1) * D, :] = d_win[:, j * DH : (j + 1) * DH]
        weight_ref[2048 + j * DH : 2048 + (j + 1) * DH, :] = d_wout[
            :, j * DH : (j + 1) * DH
        ].astype(BF)
    own = pl.ds(pl.multiple_of(dp * PIECE, 16), PIECE)

    def out_piece(pd):
        pltpu.make_async_remote_copy(
            src_ref=weight_ref.at[pl.ds(pl.multiple_of(pd * PIECE, 16), PIECE)],
            dst_ref=weight_in.at[own],
            send_sem=all_send.at[5],
            recv_sem=all_recv.at[5],
            device_id=(pd, tx),
            device_id_type=MESH,
        ).start()

    def back_piece(pd):
        pltpu.make_async_remote_copy(
            src_ref=weight_mine,
            dst_ref=weight_sum.at[own],
            send_sem=all_send.at[6],
            recv_sem=all_recv.at[6],
            device_id=(pd, tx),
            device_id_type=MESH,
        ).start()

    each_dp(dp, tx, out_piece)
    weight_in[own] = weight_ref[own]

    wait_rows(neg_back, (OWNERS - 1) * 16, all_recv.at[4])
    gather_chunks(neg_back, picked_ref, 512, CAP_N)

    def add_negatives(i, carry):
        at = pl.ds(pl.multiple_of(i * 512, 512), 512)
        total = put_rows(arrived_t_ref, picked_ref, i * 512, 4, 512)
        total = total + put_rows(arrived_t_ref, picked_ref, i * 512, 8, 512)
        table_ref[at, :] = total.astype(BF)
        return carry

    lax.fori_loop(0, 4, add_negatives, 0)

    first, second = emb_sum.finish()
    d_hist = rest_ref[0:Q, :] + jnp.concatenate([first, second], axis=0)
    wait_rows(hist_out, (OWNERS - 1) * 16, all_send.at[1])
    put_slots(d_hist.astype(BF), slot_h, hist_out, CAP_H)
    spread_all(hist_out, hist_back, 16, all_send.at[3], all_recv.at[3], dp, tx)

    wait_rows(weight_in, (N_DP - 1) * PIECE, all_recv.at[5])
    total = weight_in[0:PIECE, :].astype(F32)
    for i in range(1, N_DP):
        total = total + weight_in[i * PIECE : (i + 1) * PIECE, :].astype(F32)
    weight_mine[...] = total.astype(BF)
    weight_sum[own] = total.astype(BF)
    each_dp(dp, tx, back_piece)

    lax.fori_loop(4, 8, add_negatives, 0)
    keep = pltpu.make_async_copy(table_ref, table_out, load_sems.at[3])
    keep.start()
    wait_rows(hist_back, (OWNERS - 1) * 16, all_recv.at[3])
    gather_chunks(hist_back, picked_ref, 0, CAP_H)
    wait_rows(weight_sum, (N_DP - 1) * PIECE, all_recv.at[6])
    results = [
        pltpu.make_async_copy(arrived_t_ref, ids_out, load_sems.at[0]),
        pltpu.make_async_copy(picked_ref.at[0:512], rows_out, load_sems.at[1]),
        pltpu.make_async_copy(weight_sum, weight_out, load_sems.at[2]),
    ]
    for move in results:
        move.start()
    for move in results + [keep]:
        move.wait()
    for c in totals + hist.first + hist.second:
        c.wait_send()
    gates.sent()
    gate_sum.sent()
    wait_rows(request_ref, OWNERS - 1, all_send.at[0])
    wait_rows(hist_out, (OWNERS - 1) * 16, all_send.at[3])
    wait_rows(neg_out, (OWNERS - 1) * 16, all_send.at[4])
    wait_rows(weight_in, (N_DP - 1) * PIECE, all_send.at[5])
    wait_rows(weight_in, (N_DP - 1) * PIECE, all_send.at[6])


def layer(ids, negs, lengths, table, w_in, w_out):
    sem = pltpu.SemaphoreType.DMA
    vm = pltpu.VMEM
    return pl.pallas_call(
        layer_kernel,
        out_shape=[
            jax.ShapeDtypeStruct((128, 128), jnp.int32),
            jax.ShapeDtypeStruct((CAP_H * OWNERS, D), BF),
            jax.ShapeDtypeStruct((2560, 128), BF),
            jax.ShapeDtypeStruct((ROWS, D), BF),
        ],
        in_specs=[VM, VM, SM, HB, HB, HB],
        out_specs=[HB] * 4,
        scratch_shapes=[
            vm((ROWS, D), BF),
            vm((OWNERS, 1, 128), jnp.int32),
            vm((OWNERS, 1, 128), jnp.int32),
            vm((128, 128), jnp.int32),
            vm((OWNERS * 16, 128), BF),
            vm((OWNERS * 16, 256), BF),
            vm((12 * OWNERS, D), BF),
            vm((OWNERS * 16, 128), BF),
            vm((OWNERS * 16, 256), BF),
            vm((OWNERS * 16, 128), BF),
            vm((OWNERS * 16, 256), BF),
            vm((D, D), BF),
            vm((D, D), BF),
            vm((1024, D), BF),
            vm((512, D), BF),
            vm((512, D), BF),
            vm((1024, D), BF),
            vm((1024, D), BF),
            vm((1024, D), F32),
            vm((1024, KEYS), BF),
            vm((1024, KEYS), F32),
            vm((1024, DH), F32),
            vm((1024, DH), F32),
            vm((4096, DH), BF),
            vm((1024, D), F32),
            vm((1024, DH), F32),
            vm((1024, D), BF),
            vm((512, 1024), F32),
            vm((512, 1024), BF),
            vm((4, 1, 1024), F32),
            vm((1, 1024), F32),
            vm((1024, D), F32),
            vm((4096, DH), BF),
            vm((6 * 512, DH), BF),
            vm((2 * 512, DH), BF),
            vm((D, D), BF),
            vm((6 * 64, D), BF),
            vm((2 * 64, D), BF),
            vm((1024, D), BF),
            vm((6 * 128, D), BF),
            vm((2 * 128, D), BF),
            vm((Q + 8, D), F32),
            vm((1024, DH), BF),
            vm((1024, DH), F32),
            vm((1024, DH), BF),
            vm((1024, DH), F32),
            vm((1024, D), BF),
            vm((2560, 128), BF),
            vm((2560, 128), BF),
            vm((PIECE, 128), BF),
            vm((2560, 128), BF),
            pltpu.SemaphoreType.REGULAR,
            sem((6,)),
            sem((7,)),
            sem((7,)),
            sem((6, 6)),
            sem((6, 6)),
            sem((3,)),
            sem((3,)),
        ],
        compiler_params=pltpu.CompilerParams(
            collective_id=0, has_side_effects=True, vmem_limit_bytes=56 * 1024 * 1024
        ),
        name="layer",
    )(ids, negs, lengths, table, w_in, w_out)


def gather_chunks(chunks_ref, rows_ref, at, cap):
    block = 128 // cap
    many = block * 16
    q, r = iota((128, many), 0), iota((128, many), 1)
    fold = one_zero(
        (lax.rem(q, block) == lax.div(r, 16)) & (lax.div(q, block) == lax.rem(r, cap))
    )
    for b in range(cap):
        wide = unfold(chunks_ref[b * many : (b + 1) * many, :], cap, 16 // cap)
        rows = mm(fold, wide).astype(BF)
        for k in range(cap):
            rows_ref[at + k * 128 + b * block : at + k * 128 + (b + 1) * block, :] = rows[
                k * block : (k + 1) * block
            ]


def put_rows(ids_ref, rows_ref, first, slot, tile):
    row = jnp.concatenate([ids_ref[slot + j : slot + j + 1, :] for j in range(4)], axis=1)
    put = one_zero(row == iota((tile, 512), 0) + first)
    return mm(put, rows_ref[slot * 128 : (slot + 4) * 128, :])


TILES = 8


def add_kernel(
    ids_hbm,
    rows_hbm,
    weight_hbm,
    part_hbm,
    out_hbm,
    w_in_hbm,
    w_out_hbm,
    ids_ref,
    rows_ref,
    weight_ref,
    part_ref,
    out_ref,
    w_in_ref,
    w_out_ref,
    in_sems,
    part_sems,
    out_sems,
    w_sems,
):
    tile = ROWS // TILES
    moves = [
        pltpu.make_async_copy(ids_hbm, ids_ref, in_sems.at[0]),
        pltpu.make_async_copy(rows_hbm, rows_ref, in_sems.at[1]),
        pltpu.make_async_copy(weight_hbm, weight_ref, in_sems.at[2]),
    ]
    parts, outs = [], []
    for i in range(TILES):
        at = pl.ds(i * tile, tile)
        parts.append(pltpu.make_async_copy(part_hbm.at[at], part_ref.at[at], part_sems.at[i]))
        outs.append(pltpu.make_async_copy(out_ref.at[at], out_hbm.at[at], out_sems.at[i]))
    for move in moves + parts:
        move.start()
    moves[0].wait()
    moves[1].wait()
    for i in range(TILES):
        at = pl.ds(i * tile, tile)
        parts[i].wait()
        out_ref[at, :] = part_ref[at, :].astype(F32) + put_rows(ids_ref, rows_ref, i * tile, 0, tile)
        outs[i].start()
    moves[2].wait()
    w_in_ref[...] = weight_ref[0:2048, :].astype(F32)
    w_out_ref[...] = jnp.concatenate(
        [weight_ref[2048 + c * 128 : 2048 + (c + 1) * 128, :] for c in range(4)], axis=1
    ).astype(F32)
    weights = [
        pltpu.make_async_copy(w_in_ref, w_in_hbm, w_sems.at[0]),
        pltpu.make_async_copy(w_out_ref, w_out_hbm, w_sems.at[1]),
    ]
    for move in weights:
        move.start()
    for move in outs + weights:
        move.wait()


def add_rows(ids, rows, weight, part):
    anywhere = pl.BlockSpec(memory_space=pl.ANY)
    sem = pltpu.SemaphoreType.DMA
    return pl.pallas_call(
        add_kernel,
        out_shape=[
            jax.ShapeDtypeStruct((ROWS, D), F32),
            jax.ShapeDtypeStruct((2048, DH), F32),
            jax.ShapeDtypeStruct((DH, D), F32),
        ],
        in_specs=[anywhere] * 4,
        out_specs=[anywhere] * 3,
        scratch_shapes=[
            pltpu.VMEM((128, 128), jnp.int32),
            pltpu.VMEM((CAP_H * OWNERS, D), BF),
            pltpu.VMEM((2560, 128), BF),
            pltpu.VMEM((ROWS, D), BF),
            pltpu.VMEM((ROWS, D), F32),
            pltpu.VMEM((2048, DH), F32),
            pltpu.VMEM((DH, D), F32),
            sem((3,)),
            sem((TILES,)),
            sem((TILES,)),
            sem((2,)),
        ],
        compiler_params=pltpu.CompilerParams(vmem_limit_bytes=56 * 1024 * 1024),
        name="add_rows",
    )(ids, rows, weight, part)


def on_device(table, item_ids, negatives, lengths, w_in, w_out):
    ids, rows, weight, part = layer(item_ids.reshape(1, -1), negatives, lengths, table, w_in, w_out)
    grad_table, grad_w_in, grad_w_out = add_rows(ids, rows, weight, part)
    return (grad_table, grad_w_in.reshape(4, D, DH), grad_w_out)


def solution(mesh):
    placed = (
        P(("dp", "table"), None),
        P(("dp", "table")),
        P("dp", "table"),
        P("dp", None),
        P(None, None, "table"),
        P("table", None),
    )
    return jax.shard_map(
        on_device,
        mesh=mesh,
        in_specs=placed,
        out_specs=(P(("dp", "table"), None), P(None, None, "table"), P("table", None)),
        check_vma=False,
    )
```

```python
import functools
import jax
import jax.numpy as jnp
from jax import lax
from jax.experimental import pallas as pl
from jax.experimental.pallas import tpu as pltpu
from jax.sharding import PartitionSpec as P

DH = 128
D = 512
CAP_H = 4
CAP_N = 8
OWNERS = 128
N_DP = 32
N_TABLE = 4
ROWS = 4096
BF = jnp.bfloat16
F32 = jnp.float32
MESH = pl.DeviceIdType.MESH

epsilon = 1e-06
sharpness = 20.0


def iota(shape, dim):
    return lax.broadcasted_iota(jnp.int32, shape, dim)


def one_zero(mask):
    return jnp.where(mask, 1.0, 0.0).astype(BF)


def mm(a, b):
    return lax.dot_general(a, b, (((1,), (0,)), ((), ())), preferred_element_type=F32)


def mm_nt(a, b):
    return lax.dot_general(a, b, (((1,), (1,)), ((), ())), preferred_element_type=F32)


def mm_tn(a, b):
    return lax.dot_general(a, b, (((0,), (0,)), ((), ())), preferred_element_type=F32)


def position():
    dp = lax.axis_index("dp")
    tx = lax.axis_index("table")
    return dp, tx


def coordinates(dp, tx):
    z, y, c = lax.div(dp, 8), lax.rem(lax.div(dp, 2), 4), lax.rem(dp, 2)
    near = [(core, lax.rem(tx + dx, 4)) for core in (1 - c, c) for dx in range(4)]
    return z, y, near[4:] + near[:4]


def plane_base(z, y, step):
    return lax.rem(z + lax.div(step, 4), 4) * 8 + lax.rem(y + lax.rem(step, 4), 4) * 2


def each_partner(dp, tx, do):
    z, y, near = coordinates(dp, tx)

    def one(i, carry):
        base = plane_base(z, y, lax.rem(i * 7, 16))
        for core, x in near:
            do(base + core, x)
        return carry

    lax.fori_loop(1, 16, one, 0)
    for core, x in near[1:]:
        do(z * 8 + y * 2 + core, x)


def each_chip(dp, tx, do):
    z, y, _ = coordinates(dp, tx)

    def one(i, carry):
        do(plane_base(z, y, lax.rem(i * 7, 16)))
        return carry

    lax.fori_loop(1, 16, one, 0)


def signal(sem, dp, x):
    pl.semaphore_signal(sem, inc=1, device_id=(dp, x), device_id_type=MESH)


def greet_planes(barrier, dp, tx):
    z, y, near = coordinates(dp, tx)
    for core, x in near[1:]:
        signal(barrier, z * 8 + y * 2 + core, x)
    core, x = near[0]
    for i in range(1, 16):
        signal(barrier, plane_base(z, y, i) + core, x)


def greet_again(sem, dp, tx):
    z, y, near = coordinates(dp, tx)
    for core, x in near[1:]:
        signal(sem, z * 8 + y * 2 + core, x)


def spread_all(src, dst, chunk, send_sem, recv_sem, dp, tx):
    me = dp * 4 + tx
    land = pl.ds(pl.multiple_of(me * chunk, chunk), chunk)

    def one(pd, px):
        pltpu.make_async_remote_copy(
            src_ref=src.at[pl.ds(pl.multiple_of((pd * 4 + px) * chunk, chunk), chunk)],
            dst_ref=dst.at[land],
            send_sem=send_sem,
            recv_sem=recv_sem,
            device_id=(pd, px),
            device_id_type=MESH,
        ).start()

    each_partner(dp, tx, one)
    dst[land] = src[land]


def wait_rows(ref, count, sem):
    pltpu.make_async_copy(ref.at[pl.ds(0, count)], ref.at[pl.ds(0, count)], sem).wait()


class Group:
    def __init__(self, dp, tx, send_sems, recv_sems):
        p, q = lax.rem(tx, 2), lax.rem(dp, 2)
        self.chip = dp - q
        self.first_x = tx - p
        self.role = p * 2 + q
        self.core = p * 2 + 1 - q
        self.over = (1 - p) * 2 + q
        self.cross = (1 - p) * 2 + 1 - q
        self.send_sems = send_sems
        self.recv_sems = recv_sems

    def copy(self, src, dst, slot, to):
        return pltpu.make_async_remote_copy(
            src_ref=src,
            dst_ref=dst,
            send_sem=self.send_sems.at[slot],
            recv_sem=self.recv_sems.at[slot],
            device_id=(self.chip + lax.rem(to, 2), self.first_x + lax.div(to, 2)),
            device_id_type=MESH,
        )


class Gather:
    def __init__(self, group, buf, block):
        h = block // 2
        g = group

        def part(t, half):
            return buf.at[pl.ds(pl.multiple_of(t * block + half * h, h), h)]

        self.first = [g.copy(part(g.role, i), part(g.role, i), i, g.over) for i in range(2)] + [
            g.copy(part(g.role, i), part(g.role, i), 2 + i, g.core) for i in range(2)
        ]
        self.second = [
            g.copy(part(g.over, i), part(g.over, i), 4 + i, g.core) for i in range(2)
        ]

    def start_half(self, half):
        self.first[half].start()
        self.first[2 + half].start()

    def start(self):
        self.start_half(0)
        self.start_half(1)

    def forward(self):
        for c, d in zip(self.first[:2], self.second):
            c.wait_recv()
            d.start()

    def near(self):
        for c in self.first[2:]:
            c.wait_recv()

    def arrived(self, half):
        self.first[2 + half].wait_recv()
        self.second[half].wait_recv()

    def sent(self):
        for c in self.first + self.second:
            c.wait_send()

    def finish(self):
        self.arrived(0)
        self.arrived(1)
        self.sent()


class Scatter:
    def __init__(self, group, part, land, onward, block):
        h = block // 2
        g = group
        self.h = h
        self.group = g
        self.part = part
        self.land = land
        self.onward = onward
        self.block = block

        self.first = [g.copy(self.at(g.cross, i), self.slot(i), i, g.core) for i in range(2)] + [
            g.copy(self.at(g.core, i), self.slot(2 + i), 2 + i, g.core) for i in range(2)
        ]
        self.second = [
            g.copy(onward.at[pl.ds(i * h, h)], self.slot(4 + i), 4 + i, g.over) for i in range(2)
        ]

    def at(self, t, half):
        return self.part.at[self.span(t, half)]

    def span(self, t, half):
        return pl.ds(pl.multiple_of(t * self.block + half * self.h, self.h), self.h)

    def slot(self, i):
        return self.land.at[pl.ds(i * self.h, self.h)]

    def start_half(self, half):
        self.first[half].start()
        self.first[2 + half].start()

    def start(self):
        self.start_half(0)
        self.start_half(1)

    def forward_half(self, i):
        h = self.h
        self.first[i].wait_recv()
        self.onward[i * h : (i + 1) * h] = (
            self.land[i * h : (i + 1) * h].astype(F32)
            + self.part[self.span(self.group.over, i)].astype(F32)
        ).astype(BF)
        self.second[i].start()

    def forward(self):
        self.forward_half(0)
        self.forward_half(1)

    def half(self, i):
        h = self.h
        self.first[2 + i].wait_recv()
        self.second[i].wait_recv()

        def got(j):
            return self.land[j * h : (j + 1) * h].astype(F32)

        return got(2 + i) + got(4 + i)

    def sent(self):
        for c in self.first + self.second:
            c.wait_send()

    def finish(self):
        halves = self.half(0), self.half(1)
        self.sent()
        return halves


def slots_of(ids):
    n = ids.shape[1]
    holder = lax.shift_right_logical(ids, 12)
    hits = iota((OWNERS, n), 0) == holder
    earlier = one_zero(iota((n, n), 0) < iota((n, n), 1))
    hits_b = one_zero(hits)
    before = jnp.sum(jnp.where(hits, mm(hits_b, earlier), 0.0), axis=0, keepdims=True)
    return holder, hits_b, before.astype(jnp.int32)


def wanted_rows(ids, hits_b, before, offset):
    n = ids.shape[1]
    marked = (ids & (ROWS - 1)) + 1
    chosen = iota((OWNERS, n), 0) == before + offset
    high = jnp.where(chosen, lax.shift_right_logical(marked, 6).astype(F32), 0.0).astype(BF)
    low = jnp.where(chosen, (marked & 63).astype(F32), 0.0).astype(BF)
    return 64.0 * mm_nt(hits_b, high) + mm_nt(hits_b, low)


def as_column(row):
    n = row.shape[1]
    wide = jnp.broadcast_to(row.astype(F32), (128, n))
    return jnp.transpose(wide)[:, 0:1].astype(jnp.int32)


def neg_row(negs_ref):
    return jnp.concatenate([negs_ref[u : u + 1, :] for u in range(4)], axis=1)


def part_mask(rows, width, per, parts):
    which = lax.rem(iota((rows, width), 0), 16) // per
    return [one_zero(which == c) for c in range(parts)]


def pick_parts(values, per, width):
    which = lax.div(lax.rem(iota((values.shape[0], width), 0), 16), per)
    out = values[:, 0:width]
    for c in range(1, values.shape[1] // width):
        out = jnp.where(which == c, values[:, c * width : (c + 1) * width], out)
    return out


def gather_rows(table, ids_col, out_ref, at):
    step = 1024

    def one(i, total):
        base = pl.multiple_of(i * step, step)
        pick = one_zero(ids_col == iota((512, step), 1) + i * step)
        return total + mm(pick, table[pl.ds(base, step), :])

    total = lax.fori_loop(0, ROWS // step, one, jnp.zeros((512, D), F32))
    out_ref[at : at + 512, :] = total.astype(BF)


def spread_chunks(rows_ref, chunks_ref, at, cap):
    width = cap * 32
    block = 128 // cap
    many = block * 16
    r, q = iota((many, 128), 0), iota((many, 128), 1)
    fold = one_zero(
        (lax.rem(q, block) == lax.div(r, 16)) & (lax.div(q, block) == lax.rem(r, cap))
    )
    for b in range(cap):
        rows = jnp.concatenate(
            [
                rows_ref[at + k * 128 + b * block : at + k * 128 + (b + 1) * block, :]
                for k in range(cap)
            ],
            axis=0,
        )
        chunks_ref[b * many : (b + 1) * many, :] = pick_parts(mm(fold, rows), cap, width).astype(BF)


def unfold(chunks, per, parts):
    rows, width = chunks.shape
    masks = part_mask(rows, width, per, parts)
    return jnp.concatenate([chunks * m for m in masks], axis=1)


def take_slots(chunks_ref, slot_col, cap):
    n = slot_col.shape[0]
    total = jnp.zeros((n, D), F32)
    step = 512
    for i in range(OWNERS * 16 // step):
        r = iota((n, step), 1) + i * step
        key = lax.div(r, 16) * cap + lax.rem(r, cap)
        total = total + mm(
            one_zero(slot_col == key),
            unfold(chunks_ref[i * step : (i + 1) * step, :], cap, 16 // cap),
        )
    return total.astype(BF)


def put_slots(rows, slot_row, chunks_ref, cap):
    n = slot_row.shape[1]
    step = 512
    for i in range(OWNERS * 16 // step):
        r = iota((step, n), 0) + i * step
        key = lax.div(r, 16) * cap + lax.rem(r, cap)
        chunks_ref[i * step : (i + 1) * step, :] = pick_parts(
            mm(one_zero(slot_row == key), rows), cap, cap * 32
        ).astype(BF)


def row_sum(values):
    return jnp.sum(values, axis=-1, keepdims=True)


def row_mean(values):
    return jnp.mean(values, axis=-1, keepdims=True)


def normal(values):
    center = values - row_mean(values)
    factor = lax.rsqrt(row_mean(center * center) + epsilon)
    return center * factor, factor


def normal_back(grad, normed, factor):
    return factor * (grad - row_mean(grad) - normed * row_mean(grad * normed))


def unit_factor(values):
    return lax.rsqrt(row_sum(values * values) + epsilon)


def unit_back(grad, values, factor):
    return factor * (grad - values * (factor * factor * row_sum(grad * values)))


class Users:
    def __init__(self, lengths_ref):
        self.lengths = [lengths_ref[0:1, u : u + 1] for u in range(4)]
        self.ends = []
        end = 0
        for length in self.lengths:
            end = end + length
            self.ends.append(end)

    def segment(self, t):
        return sum(jnp.where(t >= end, 1, 0) for end in self.ends)

    def start(self, t):
        return sum(jnp.where(t >= e, n, 0) for e, n in zip(self.ends, self.lengths))

    def length(self, t):
        out = jnp.where(t >= 0, self.lengths[0], 0)
        for u in range(1, 4):
            out = jnp.where(t >= self.ends[u - 1], self.lengths[u], out)
        return out


VM = pl.BlockSpec(memory_space=pltpu.VMEM)
HB = pl.BlockSpec(memory_space=pl.ANY)
Q = 256
KEYS = 768
SCALE = DH**-0.5
PIECE = 80


def layer_kernel(
    ids_ref,
    negs_ref,
    lengths_ref,
    table_hbm,
    w_in_hbm,
    w_out_hbm,
    ids_out,
    rows_out,
    weight_out,
    table_out,
    lengths_mine,
    ids_own,
    negs_own,
    lengths_own,
    table_ref,
    request_ref,
    arrived_ref,
    arrived_t_ref,
    hist_back,
    neg_back,
    picked_ref,
    hist_out,
    neg_out,
    hist_in,
    neg_in,
    w_in_ref,
    w_out_ref,
    emb_ref,
    neg_ref,
    unit_ref,
    normed_ref,
    proj_ref,
    slope_ref,
    weights_ref,
    dweights_ref,
    mixed_ref,
    factor_ref,
    gated_ref,
    y_ref,
    y_factor_ref,
    y_unit_ref,
    grown_ref,
    shares_ref,
    total_ref,
    whole_ref,
    drows_ref,
    dgated_ref,
    dgated_land,
    dgated_on,
    dout_part,
    dout_land,
    dout_on,
    demb_ref,
    emb_land,
    emb_on,
    rest_ref,
    dgate_ref,
    dvalue_ref,
    dquery_ref,
    dkey_ref,
    dpre_ref,
    weight_ref,
    weight_in,
    weight_mine,
    weight_sum,
    met_sem,
    load_sems,
    all_send,
    all_recv,
    ring_send,
    ring_recv,
    total_send,
    total_recv,
    move_send,
    move_recv,
):
    dp, tx = position()
    barrier = pltpu.get_barrier_semaphore()
    greet_planes(barrier, dp, tx)
    load = pltpu.make_async_copy(table_hbm, table_ref, load_sems.at[0])
    load.start()
    lengths_mine[...] = jnp.zeros_like(lengths_mine)
    lengths_mine[:, 0:4] = lengths_ref[...]

    def group(i):
        return Group(dp, tx, ring_send.at[i], ring_recv.at[i])

    here = group(0)
    role, chip, p, q = here.role, here.chip, lax.rem(tx, 2), lax.rem(dp, 2)
    after = lax.rem(role + 1, 4)
    group_dp = chip + lax.div(tx, 2)

    def rows_of(b, n=Q):
        return pl.ds(pl.multiple_of(b * n, n), n)

    to_dp, to_x = chip + p, 2 * q + lax.div(tx, 2)
    moved = [
        (ids_ref, ids_own),
        (negs_ref, negs_own),
        (lengths_mine, lengths_own),
        (w_out_hbm, w_out_ref.at[rows_of(tx, DH)]),
    ] + [(w_in_hbm.at[j], w_in_ref.at[:, j * DH : (j + 1) * DH]) for j in range(4)]
    stays = role == tx

    def remote(i):
        return pltpu.make_async_remote_copy(
            src_ref=moved[i][0],
            dst_ref=moved[i][1],
            send_sem=move_send.at[i],
            recv_sem=move_recv.at[i],
            device_id=(to_dp, to_x),
            device_id_type=MESH,
        )

    def moved_in(i):
        at = w_out_ref.at[rows_of(role, DH)] if i == 3 else moved[i][1]
        pltpu.make_async_copy(at, at, move_recv.at[i]).wait()

    pl.semaphore_wait(barrier, 22)
    greet_again(met_sem, dp, tx)

    @pl.when(stays)
    def _():
        for i, (src, dst) in enumerate(moved):
            pltpu.make_async_copy(src, dst, move_recv.at[i]).start()

    @pl.when(jnp.logical_not(stays))
    def _():
        for i in range(len(moved)):
            remote(i).start()

    for i in range(3):
        moved_in(i)

    ids, negs = ids_own[...], neg_row(negs_own)
    holder_h, hits_h, before_h = slots_of(ids)
    holder_n, hits_n, before_n = slots_of(negs)
    wanted = wanted_rows(ids, hits_h, before_h, 0) + wanted_rows(negs, hits_n, before_n, CAP_H)
    request_ref[:, 0, :] = wanted.astype(jnp.int32) - 1
    slot_h = holder_h * CAP_H + before_h
    slot_n = holder_n * CAP_N + before_n

    pl.semaphore_wait(met_sem, 7)
    spread_all(request_ref, arrived_ref, 1, all_send.at[0], all_recv.at[0], dp, tx)
    load.wait()
    moved_in(3)
    w_outs = Gather(group(1), w_out_ref, DH)
    w_outs.start()
    slot_h_col, slot_n_col = as_column(slot_h), as_column(slot_n)
    users = Users(lengths_own)
    wait_rows(arrived_ref, OWNERS - 1, all_recv.at[0])

    arrived = arrived_ref[:, 0, :]
    columns = [arrived[:, k : k + 1] for k in range(CAP_H + CAP_N)]
    gather_rows(table_ref, jnp.concatenate(columns[0:4], axis=0), picked_ref, 0)
    spread_chunks(picked_ref, hist_out, 0, CAP_H)
    spread_all(hist_out, hist_in, 16, all_send.at[1], all_recv.at[1], dp, tx)
    w_outs.forward()
    gather_rows(table_ref, jnp.concatenate(columns[4:8], axis=0), picked_ref, 512)

    wait_rows(hist_in, (OWNERS - 1) * 16, all_recv.at[1])
    emb_ref[rows_of(role), :] = take_slots(hist_in, slot_h_col, CAP_H)
    hist = Gather(group(0), emb_ref, Q)
    hist.start()

    def project(b):
        at = rows_of(b)
        normed = normal(emb_ref[at, :].astype(F32))[0].astype(BF)
        normed_ref[at, :] = normed
        pre = mm(normed, w_in_ref[...])
        gate = lax.logistic(pre)
        proj_ref[at, :] = (pre * gate).astype(BF)
        slope_ref[at, :] = gate * (1.0 + pre * (1.0 - gate))

    gather_rows(table_ref, jnp.concatenate(columns[8:12], axis=0), picked_ref, 1024)
    hist.forward()
    spread_chunks(picked_ref, neg_out, 512, CAP_N)
    spread_all(neg_out, neg_in, 16, all_send.at[2], all_recv.at[2], dp, tx)
    for i in range(4, 8):
        moved_in(i)
    project(role)
    hist.near()
    project(here.core)
    project(here.over)
    for c in hist.second:
        c.wait_recv()
    project(here.cross)

    arrived_t_ref[...] = jnp.transpose(arrived.astype(F32)).astype(jnp.int32)

    mine = pl.multiple_of(role * 1024, 1024)

    def keys_of(b):
        low = max(b - 2, 0)
        return slice(low * Q, (b + 1) * Q), low

    def attend(b):
        at = slice(b * Q, (b + 1) * Q)
        kr, low = keys_of(b)
        n = kr.stop - kr.start
        scores = mm_nt(proj_ref[at, 256:384], proj_ref[kr, 384:512]) * SCALE
        t = iota((Q, 1), 0) + b * Q
        s = iota((Q, n), 1) + low * Q
        seen = (s <= t) & (s >= users.start(t))
        share = 1.0 / users.length(t).astype(F32)
        gate = lax.logistic(scores)
        weights = jnp.where(seen, scores * gate * share, 0.0).astype(BF)
        weights_ref[at, 0:n] = weights
        dweights_ref[at, 0:n] = jnp.where(
            seen, gate * (1.0 + scores * (1.0 - gate)) * (share * SCALE), 0.0
        )
        mixed, factor = normal(mm(weights, proj_ref[kr, 128:256]))
        mixed_ref[at, :] = mixed
        factor_ref[at, :] = jnp.broadcast_to(factor, (Q, DH))
        gated_ref[pl.ds(mine + b * Q, Q), :] = (mixed * proj_ref[at, 0:128].astype(F32)).astype(BF)

    gates = Gather(group(2), gated_ref, 1024)
    attend(0)
    attend(1)
    gates.start_half(0)
    attend(2)
    attend(3)
    gates.start_half(1)

    wait_rows(neg_in, (OWNERS - 1) * 16, all_recv.at[2])
    neg_ref[...] = take_slots(neg_in, slot_n_col, CAP_N)
    gates.forward()
    neg_f = neg_ref[...].astype(F32)
    neg_factor = unit_factor(neg_f)
    unit_ref[...] = (neg_f * neg_factor).astype(BF)
    w_outs.finish()
    arrived_t_ref[...] = jnp.transpose(arrived.astype(F32)).astype(jnp.int32)

    emb_f = emb_ref[rows_of(role), :].astype(F32)
    follow = jnp.where(
        iota((Q, 1), 0) == Q - 1,
        emb_ref[rows_of(after), :].astype(F32)[0:1, :],
        pltpu.roll(emb_f, Q - 1, 0),
    )
    follow_factor = unit_factor(follow)
    follow_unit = (follow * follow_factor).astype(BF).astype(F32)
    t_row = iota((1, 1024), 1)
    segment = users.segment(t_row)
    valid = users.segment(t_row + 1) == segment
    users_of = [jnp.where(segment == u, 1.0, 0.0) for u in range(4)]
    gates.arrived(0)

    for b in range(4):
        if b == 2:
            gates.arrived(1)
        at = slice(b * Q, (b + 1) * Q)
        gated = jnp.concatenate(
            [gated_ref[h * 1024 + b * Q : h * 1024 + (b + 1) * Q, :] for h in range(4)], axis=1
        )
        y = emb_ref[at, :].astype(F32) + mm(gated, w_out_ref[...])
        factor = unit_factor(y)
        y_unit = (y * factor).astype(BF)
        y_ref[at, :] = y
        y_factor_ref[at, :] = jnp.broadcast_to(factor, (Q, DH))
        y_unit_ref[at, :] = y_unit
        grown = jnp.exp(sharpness * mm_nt(unit_ref[...], y_unit))
        grown = jnp.concatenate(
            [grown[u * DH : (u + 1) * DH, :] * users_of[u][:, at] for u in range(4)], axis=0
        )
        grown_ref[:, at] = grown
        total_ref[role, :, at] = jnp.sum(grown, axis=0, keepdims=True)

    y_unit_f = y_unit_ref[rows_of(role), :].astype(F32)
    grown_pos = jnp.exp(sharpness * row_sum(y_unit_f * follow_unit))
    own_lanes = pl.ds(pl.multiple_of(role * Q, Q), Q)
    grown_pos_row = jnp.transpose(jnp.broadcast_to(grown_pos, (Q, DH)))[0:1, :]
    total_ref[role, :, own_lanes] += grown_pos_row
    totals = [
        Group(dp, tx, total_send, total_recv).copy(total_ref.at[role], total_ref.at[role], i, to)
        for i, to in enumerate((here.over, here.cross, here.core))
    ]
    for c in totals:
        c.start()
    for c in totals:
        c.wait_recv()
    total = total_ref[0] + total_ref[1] + total_ref[2] + total_ref[3]
    whole_ref[...] = jnp.where(valid, sharpness / total, 0.0)
    scaled_own = jnp.transpose(jnp.broadcast_to(whole_ref[:, own_lanes], (DH, Q)))[:, 0:1]
    d_pos = jnp.where(scaled_own > 0.0, scaled_own * grown_pos - sharpness, 0.0)
    d_unit_pos = d_pos * follow_unit
    gate_sum = Scatter(group(3), dgated_ref, dgated_land, dgated_on, 1024)
    for b in range(4):
        at = slice(b * Q, (b + 1) * Q)
        shares = (grown_ref[:, at] * whole_ref[:, at]).astype(BF)
        shares_ref[:, at] = shares
        d_unit = mm_tn(shares, unit_ref[...]) + jnp.where(role == b, d_unit_pos, 0.0)
        d_rows = unit_back(d_unit, y_ref[at, :], y_factor_ref[at, :][:, 0:1])
        drows_ref[at, :] = d_rows
        d_gated = mm_nt(d_rows.astype(BF), w_out_ref[...]).astype(BF)
        for h in range(4):
            dgated_ref[h * 1024 + b * Q : h * 1024 + (b + 1) * Q, :] = d_gated[
                :, h * DH : (h + 1) * DH
            ]
        if b == 1:
            gate_sum.start_half(0)
    gate_sum.start_half(1)
    gate_sum.forward()

    d_neg = unit_back(
        mm(shares_ref[...], y_unit_ref[...]),
        neg_ref[...].astype(F32),
        unit_factor(neg_ref[...].astype(F32)),
    )
    wait_rows(neg_out, (OWNERS - 1) * 16, all_send.at[2])
    put_slots(d_neg.astype(BF), slot_n, neg_out, CAP_N)
    spread_all(neg_out, neg_back, 16, all_send.at[4], all_recv.at[4], dp, tx)
    for h in range(4):
        dout_part[h * DH : (h + 1) * DH, :] = mm_tn(
            gated_ref[h * 1024 : (h + 1) * 1024, :], drows_ref[...].astype(BF)
        ).astype(BF)
    w_out_sum = Scatter(group(4), dout_part, dout_land, dout_on, DH)
    w_out_sum.start()
    d_follow = unit_back(d_pos * y_unit_f, follow, follow_factor)
    rest_ref[0:Q, :] = jnp.where(iota((Q, 1), 0) == 0, 0.0, pltpu.roll(d_follow, 1, 0))
    rest_ref[Q : Q + 8, :] = jnp.where(iota((8, 1), 0) == 0, d_follow[Q - 1 : Q, :], 0.0)
    dkey_ref[...] = jnp.zeros_like(dkey_ref)
    dvalue_ref[...] = jnp.zeros_like(dvalue_ref)
    halves = [gate_sum.half(0)]

    def attend_back(b):
        at = slice(b * Q, (b + 1) * Q)
        kr, _ = keys_of(b)
        n = kr.stop - kr.start
        half = halves[b // 2][(b % 2) * Q : (b % 2 + 1) * Q, :]
        d_gated = half + dgated_ref[pl.ds(mine + b * Q, Q), :].astype(F32)
        mixed = mixed_ref[at, :]
        dgate_ref[at, :] = (d_gated * mixed).astype(BF)
        d_mixed = normal_back(
            d_gated * proj_ref[at, 0:128].astype(F32), mixed, factor_ref[at, :][:, 0:1]
        ).astype(BF)
        d_scores = (mm_nt(d_mixed, proj_ref[kr, 128:256]) * dweights_ref[at, 0:n]).astype(BF)
        dquery_ref[at, :] = mm(d_scores, proj_ref[kr, 384:512]).astype(BF)
        dkey_ref[kr, :] += mm_tn(d_scores, proj_ref[at, 256:384])
        dvalue_ref[kr, :] += mm_tn(weights_ref[at, 0:n], d_mixed)

    attend_back(0)
    attend_back(1)
    w_out_sum.forward()
    halves.append(gate_sum.half(1))
    attend_back(2)
    attend_back(3)

    def project_back(b):
        at = rows_of(b)
        d_proj = jnp.concatenate(
            [
                dgate_ref[at, :].astype(F32),
                dvalue_ref[at, :].astype(BF).astype(F32),
                dquery_ref[at, :].astype(F32),
                dkey_ref[at, :].astype(BF).astype(F32),
            ],
            axis=1,
        )
        d_pre = (d_proj * slope_ref[at, :]).astype(BF)
        dpre_ref[at, :] = d_pre
        normed, factor = normal(emb_ref[at, :].astype(F32))
        d_normed = mm_nt(d_pre, w_in_ref[...]).astype(BF).astype(F32)
        return normal_back(d_normed, normed, factor) + drows_ref[at, :]

    emb_sum = Scatter(group(5), demb_ref, emb_land, emb_on, Q)
    def send_part(b):
        next_first = jnp.where((iota((Q, 1), 0) == 0) & (b == after), rest_ref[Q : Q + 1, :], 0.0)
        demb_ref[rows_of(b), :] = (project_back(b) + next_first).astype(BF)

    send_part(here.cross)
    emb_sum.first[0].start()
    emb_sum.first[1].start()
    send_part(here.over)
    emb_sum.forward()
    send_part(here.core)
    emb_sum.first[2].start()
    emb_sum.first[3].start()
    rest_ref[0:Q, :] += project_back(role)

    d_win = mm_tn(normed_ref[...], dpre_ref[...]).astype(BF)
    first, second = w_out_sum.finish()
    d_wout = jnp.concatenate([first, second], axis=0) + dout_part[rows_of(role, DH), :].astype(F32)
    for j in range(4):
        weight_ref[j * D : (j + 1) * D, :] = d_win[:, j * DH : (j + 1) * DH]
        weight_ref[2048 + j * DH : 2048 + (j + 1) * DH, :] = d_wout[
            :, j * DH : (j + 1) * DH
        ].astype(BF)
    own = pl.ds(pl.multiple_of(group_dp * PIECE, 16), PIECE)

    def out_piece(base, other):
        to = base + other
        pltpu.make_async_remote_copy(
            src_ref=weight_ref.at[pl.ds(pl.multiple_of(to * PIECE, 16), PIECE)],
            dst_ref=weight_in.at[own],
            send_sem=all_send.at[5],
            recv_sem=all_recv.at[5],
            device_id=(base + q, 2 * other + p),
            device_id_type=MESH,
        ).start()

    def back_piece(to):
        pltpu.make_async_remote_copy(
            src_ref=weight_mine,
            dst_ref=weight_sum.at[own],
            send_sem=all_send.at[6],
            recv_sem=all_recv.at[6],
            device_id=(to, role),
            device_id_type=MESH,
        ).start()

    def out_pieces(base):
        out_piece(base, 0)
        out_piece(base, 1)

    def back_pieces(base):
        back_piece(base)
        back_piece(base + 1)

    each_chip(dp, tx, out_pieces)
    out_piece(chip, 1 - lax.div(tx, 2))
    weight_in[own] = weight_ref[own]

    wait_rows(neg_back, (OWNERS - 1) * 16, all_recv.at[4])
    gather_chunks(neg_back, picked_ref, 512, CAP_N)

    def add_negatives(i, carry):
        at = pl.ds(pl.multiple_of(i * 512, 512), 512)
        total = put_rows(arrived_t_ref, picked_ref, i * 512, 4, 512)
        total = total + put_rows(arrived_t_ref, picked_ref, i * 512, 8, 512)
        table_ref[at, :] = total.astype(BF)
        return carry

    lax.fori_loop(0, 4, add_negatives, 0)

    first, second = emb_sum.finish()
    d_hist = rest_ref[0:Q, :] + jnp.concatenate([first, second], axis=0)
    wait_rows(hist_out, (OWNERS - 1) * 16, all_send.at[1])
    put_slots(d_hist.astype(BF), slot_h, hist_out, CAP_H)
    spread_all(hist_out, hist_back, 16, all_send.at[3], all_recv.at[3], dp, tx)

    wait_rows(weight_in, (N_DP - 1) * PIECE, all_recv.at[5])
    total = weight_in[0:PIECE, :].astype(F32)
    for i in range(1, N_DP):
        total = total + weight_in[i * PIECE : (i + 1) * PIECE, :].astype(F32)
    weight_mine[...] = total.astype(BF)
    each_chip(dp, tx, back_pieces)
    back_piece(chip + 1 - q)

    @pl.when(stays)
    def _():
        weight_sum[own] = weight_mine[...]

    @pl.when(jnp.logical_not(stays))
    def _():
        back_piece(dp)


    lax.fori_loop(4, 8, add_negatives, 0)
    keep = pltpu.make_async_copy(table_ref, table_out, load_sems.at[3])
    keep.start()
    wait_rows(hist_back, (OWNERS - 1) * 16, all_recv.at[3])
    gather_chunks(hist_back, picked_ref, 0, CAP_H)

    @pl.when(stays)
    def _():
        wait_rows(weight_sum, (N_DP - 1) * PIECE, all_recv.at[6])
        wait_rows(weight_in, (N_DP - 1) * PIECE, all_send.at[6])

    @pl.when(jnp.logical_not(stays))
    def _():
        wait_rows(weight_sum, N_DP * PIECE, all_recv.at[6])
        wait_rows(weight_in, N_DP * PIECE, all_send.at[6])
        for i in range(len(moved)):
            remote(i).wait_send()

    results = [
        pltpu.make_async_copy(arrived_t_ref, ids_out, load_sems.at[0]),
        pltpu.make_async_copy(picked_ref.at[0:512], rows_out, load_sems.at[1]),
        pltpu.make_async_copy(weight_sum, weight_out, load_sems.at[2]),
    ]
    for move in results:
        move.start()
    for move in results + [keep]:
        move.wait()
    for c in totals + hist.first + hist.second:
        c.wait_send()
    gates.sent()
    gate_sum.sent()
    wait_rows(request_ref, OWNERS - 1, all_send.at[0])
    wait_rows(hist_out, (OWNERS - 1) * 16, all_send.at[3])
    wait_rows(neg_out, (OWNERS - 1) * 16, all_send.at[4])
    wait_rows(weight_in, (N_DP - 1) * PIECE, all_send.at[5])


def layer(ids, negs, lengths, table, w_in, w_out):
    sem = pltpu.SemaphoreType.DMA
    vm = pltpu.VMEM
    return pl.pallas_call(
        layer_kernel,
        out_shape=[
            jax.ShapeDtypeStruct((128, 128), jnp.int32),
            jax.ShapeDtypeStruct((CAP_H * OWNERS, D), BF),
            jax.ShapeDtypeStruct((2560, 128), BF),
            jax.ShapeDtypeStruct((ROWS, D), BF),
        ],
        in_specs=[VM, VM, VM, HB, HB, HB],
        out_specs=[HB] * 4,
        scratch_shapes=[
            vm((1, 128), jnp.int32),
            vm((1, 256), jnp.int32),
            vm((4, 128), jnp.int32),
            vm((1, 128), jnp.int32),
            vm((ROWS, D), BF),
            vm((OWNERS, 1, 128), jnp.int32),
            vm((OWNERS, 1, 128), jnp.int32),
            vm((128, 128), jnp.int32),
            vm((OWNERS * 16, 128), BF),
            vm((OWNERS * 16, 256), BF),
            vm((12 * OWNERS, D), BF),
            vm((OWNERS * 16, 128), BF),
            vm((OWNERS * 16, 256), BF),
            vm((OWNERS * 16, 128), BF),
            vm((OWNERS * 16, 256), BF),
            vm((D, D), BF),
            vm((D, D), BF),
            vm((1024, D), BF),
            vm((512, D), BF),
            vm((512, D), BF),
            vm((1024, D), BF),
            vm((1024, D), BF),
            vm((1024, D), F32),
            vm((1024, KEYS), BF),
            vm((1024, KEYS), F32),
            vm((1024, DH), F32),
            vm((1024, DH), F32),
            vm((4096, DH), BF),
            vm((1024, D), F32),
            vm((1024, DH), F32),
            vm((1024, D), BF),
            vm((512, 1024), F32),
            vm((512, 1024), BF),
            vm((4, 1, 1024), F32),
            vm((1, 1024), F32),
            vm((1024, D), F32),
            vm((4096, DH), BF),
            vm((6 * 512, DH), BF),
            vm((2 * 512, DH), BF),
            vm((D, D), BF),
            vm((6 * 64, D), BF),
            vm((2 * 64, D), BF),
            vm((1024, D), BF),
            vm((6 * 128, D), BF),
            vm((2 * 128, D), BF),
            vm((Q + 8, D), F32),
            vm((1024, DH), BF),
            vm((1024, DH), F32),
            vm((1024, DH), BF),
            vm((1024, DH), F32),
            vm((1024, D), BF),
            vm((2560, 128), BF),
            vm((2560, 128), BF),
            vm((PIECE, 128), BF),
            vm((2560, 128), BF),
            pltpu.SemaphoreType.REGULAR,
            sem((6,)),
            sem((7,)),
            sem((7,)),
            sem((6, 6)),
            sem((6, 6)),
            sem((3,)),
            sem((3,)),
            sem((8,)),
            sem((8,)),
        ],
        compiler_params=pltpu.CompilerParams(
            collective_id=0, has_side_effects=True, vmem_limit_bytes=56 * 1024 * 1024
        ),
        name="layer",
    )(ids, negs, lengths, table, w_in, w_out)


def gather_chunks(chunks_ref, rows_ref, at, cap):
    block = 128 // cap
    many = block * 16
    q, r = iota((128, many), 0), iota((128, many), 1)
    fold = one_zero(
        (lax.rem(q, block) == lax.div(r, 16)) & (lax.div(q, block) == lax.rem(r, cap))
    )
    for b in range(cap):
        wide = unfold(chunks_ref[b * many : (b + 1) * many, :], cap, 16 // cap)
        rows = mm(fold, wide).astype(BF)
        for k in range(cap):
            rows_ref[at + k * 128 + b * block : at + k * 128 + (b + 1) * block, :] = rows[
                k * block : (k + 1) * block
            ]


def put_rows(ids_ref, rows_ref, first, slot, tile):
    row = jnp.concatenate([ids_ref[slot + j : slot + j + 1, :] for j in range(4)], axis=1)
    put = one_zero(row == iota((tile, 512), 0) + first)
    return mm(put, rows_ref[slot * 128 : (slot + 4) * 128, :])


TILES = 8


def add_kernel(
    ids_hbm,
    rows_hbm,
    weight_hbm,
    part_hbm,
    out_hbm,
    w_in_hbm,
    w_out_hbm,
    ids_ref,
    rows_ref,
    weight_ref,
    part_ref,
    out_ref,
    w_in_ref,
    w_out_ref,
    in_sems,
    part_sems,
    out_sems,
    w_sems,
):
    tile = ROWS // TILES
    moves = [
        pltpu.make_async_copy(ids_hbm, ids_ref, in_sems.at[0]),
        pltpu.make_async_copy(rows_hbm, rows_ref, in_sems.at[1]),
        pltpu.make_async_copy(weight_hbm, weight_ref, in_sems.at[2]),
    ]
    parts, outs = [], []
    for i in range(TILES):
        at = pl.ds(i * tile, tile)
        parts.append(pltpu.make_async_copy(part_hbm.at[at], part_ref.at[at], part_sems.at[i]))
        outs.append(pltpu.make_async_copy(out_ref.at[at], out_hbm.at[at], out_sems.at[i]))
    for move in moves + parts:
        move.start()
    moves[0].wait()
    moves[1].wait()
    for i in range(TILES):
        at = pl.ds(i * tile, tile)
        parts[i].wait()
        out_ref[at, :] = part_ref[at, :].astype(F32) + put_rows(ids_ref, rows_ref, i * tile, 0, tile)
        outs[i].start()
    moves[2].wait()
    w_in_ref[...] = weight_ref[0:2048, :].astype(F32)
    w_out_ref[...] = jnp.concatenate(
        [weight_ref[2048 + c * 128 : 2048 + (c + 1) * 128, :] for c in range(4)], axis=1
    ).astype(F32)
    weights = [
        pltpu.make_async_copy(w_in_ref, w_in_hbm, w_sems.at[0]),
        pltpu.make_async_copy(w_out_ref, w_out_hbm, w_sems.at[1]),
    ]
    for move in weights:
        move.start()
    for move in outs + weights:
        move.wait()


def add_rows(ids, rows, weight, part):
    anywhere = pl.BlockSpec(memory_space=pl.ANY)
    sem = pltpu.SemaphoreType.DMA
    return pl.pallas_call(
        add_kernel,
        out_shape=[
            jax.ShapeDtypeStruct((ROWS, D), F32),
            jax.ShapeDtypeStruct((2048, DH), F32),
            jax.ShapeDtypeStruct((DH, D), F32),
        ],
        in_specs=[anywhere] * 4,
        out_specs=[anywhere] * 3,
        scratch_shapes=[
            pltpu.VMEM((128, 128), jnp.int32),
            pltpu.VMEM((CAP_H * OWNERS, D), BF),
            pltpu.VMEM((2560, 128), BF),
            pltpu.VMEM((ROWS, D), BF),
            pltpu.VMEM((ROWS, D), F32),
            pltpu.VMEM((2048, DH), F32),
            pltpu.VMEM((DH, D), F32),
            sem((3,)),
            sem((TILES,)),
            sem((TILES,)),
            sem((2,)),
        ],
        compiler_params=pltpu.CompilerParams(vmem_limit_bytes=56 * 1024 * 1024),
        name="add_rows",
    )(ids, rows, weight, part)


def on_device(table, item_ids, negatives, lengths, w_in, w_out):
    ids, rows, weight, part = layer(item_ids.reshape(1, -1), negatives, lengths, table, w_in, w_out)
    grad_table, grad_w_in, grad_w_out = add_rows(ids, rows, weight, part)
    return (grad_table, grad_w_in.reshape(4, D, DH), grad_w_out)


def solution(mesh):
    placed = (
        P(("dp", "table"), None),
        P(("dp", "table")),
        P("dp", "table"),
        P("dp", None),
        P(None, None, "table"),
        P("table", None),
    )
    return jax.shard_map(
        on_device,
        mesh=mesh,
        in_specs=placed,
        out_specs=(P(("dp", "table"), None), P(None, None, "table"), P("table", None)),
        check_vma=False,
    )
```

```python
import functools
import jax
import jax.numpy as jnp
from jax import lax
from jax.experimental import pallas as pl
from jax.experimental.pallas import tpu as pltpu
from jax.sharding import PartitionSpec as P

DH = 128
D = 512
CAP_H = 4
CAP_N = 8
OWNERS = 128
N_DP = 32
N_TABLE = 4
ROWS = 4096
BF = jnp.bfloat16
F32 = jnp.float32
MESH = pl.DeviceIdType.MESH

epsilon = 1e-06
sharpness = 20.0


def iota(shape, dim):
    return lax.broadcasted_iota(jnp.int32, shape, dim)


def one_zero(mask):
    return jnp.where(mask, 1.0, 0.0).astype(BF)


def mm(a, b):
    return lax.dot_general(a, b, (((1,), (0,)), ((), ())), preferred_element_type=F32)


def mm_nt(a, b):
    return lax.dot_general(a, b, (((1,), (1,)), ((), ())), preferred_element_type=F32)


def mm_tn(a, b):
    return lax.dot_general(a, b, (((0,), (0,)), ((), ())), preferred_element_type=F32)


def position():
    dp = lax.axis_index("dp")
    tx = lax.axis_index("table")
    return dp, tx


def coordinates(dp, tx):
    z, y, c = lax.div(dp, 8), lax.rem(lax.div(dp, 2), 4), lax.rem(dp, 2)
    near = [(core, lax.rem(tx + dx, 4)) for core in (1 - c, c) for dx in range(4)]
    return z, y, near[4:] + near[:4]


def plane_base(z, y, step):
    return lax.rem(z + lax.div(step, 4), 4) * 8 + lax.rem(y + lax.rem(step, 4), 4) * 2


def each_partner(dp, tx, do):
    z, y, near = coordinates(dp, tx)

    def one(i, carry):
        base = plane_base(z, y, lax.rem(i * 7, 16))
        for core, x in near:
            do(base + core, x)
        return carry

    lax.fori_loop(1, 16, one, 0)
    for core, x in near[1:]:
        do(z * 8 + y * 2 + core, x)


def each_chip(dp, tx, do):
    z, y, _ = coordinates(dp, tx)

    def one(i, carry):
        do(plane_base(z, y, lax.rem(i * 7, 16)))
        return carry

    lax.fori_loop(1, 16, one, 0)


def signal(sem, dp, x):
    pl.semaphore_signal(sem, inc=1, device_id=(dp, x), device_id_type=MESH)


def greet_planes(barrier, dp, tx):
    z, y, near = coordinates(dp, tx)
    for core, x in near[1:]:
        signal(barrier, z * 8 + y * 2 + core, x)
    core, x = near[0]
    for i in range(1, 16):
        signal(barrier, plane_base(z, y, i) + core, x)


def greet_again(sem, dp, tx):
    z, y, near = coordinates(dp, tx)
    for core, x in near[1:]:
        signal(sem, z * 8 + y * 2 + core, x)


def spread_all(src, dst, chunk, send_sem, recv_sem, dp, tx):
    me = dp * 4 + tx
    land = pl.ds(pl.multiple_of(me * chunk, chunk), chunk)

    def one(pd, px):
        pltpu.make_async_remote_copy(
            src_ref=src.at[pl.ds(pl.multiple_of((pd * 4 + px) * chunk, chunk), chunk)],
            dst_ref=dst.at[land],
            send_sem=send_sem,
            recv_sem=recv_sem,
            device_id=(pd, px),
            device_id_type=MESH,
        ).start()

    each_partner(dp, tx, one)
    dst[land] = src[land]


def wait_rows(ref, count, sem):
    pltpu.make_async_copy(ref.at[pl.ds(0, count)], ref.at[pl.ds(0, count)], sem).wait()


class Group:
    def __init__(self, dp, tx, send_sems, recv_sems):
        p, q = lax.rem(tx, 2), lax.rem(dp, 2)
        self.chip = dp - q
        self.first_x = tx - p
        self.role = p * 2 + q
        self.core = p * 2 + 1 - q
        self.over = (1 - p) * 2 + q
        self.cross = (1 - p) * 2 + 1 - q
        self.send_sems = send_sems
        self.recv_sems = recv_sems

    def copy(self, src, dst, slot, to):
        return pltpu.make_async_remote_copy(
            src_ref=src,
            dst_ref=dst,
            send_sem=self.send_sems.at[slot],
            recv_sem=self.recv_sems.at[slot],
            device_id=(self.chip + lax.rem(to, 2), self.first_x + lax.div(to, 2)),
            device_id_type=MESH,
        )


class Gather:
    def __init__(self, group, buf, block):
        h = block // 2
        g = group

        def part(t, half):
            return buf.at[pl.ds(pl.multiple_of(t * block + half * h, h), h)]

        self.first = [g.copy(part(g.role, i), part(g.role, i), i, g.over) for i in range(2)] + [
            g.copy(part(g.role, i), part(g.role, i), 2 + i, g.core) for i in range(2)
        ]
        self.second = [
            g.copy(part(g.over, i), part(g.over, i), 4 + i, g.core) for i in range(2)
        ]

    def start_half(self, half):
        self.first[half].start()
        self.first[2 + half].start()

    def start(self):
        self.start_half(0)
        self.start_half(1)

    def forward(self):
        for c, d in zip(self.first[:2], self.second):
            c.wait_recv()
            d.start()

    def near(self):
        for c in self.first[2:]:
            c.wait_recv()

    def arrived(self, half):
        self.first[2 + half].wait_recv()
        self.second[half].wait_recv()

    def sent(self):
        for c in self.first + self.second:
            c.wait_send()

    def finish(self):
        self.arrived(0)
        self.arrived(1)
        self.sent()


class Scatter:
    def __init__(self, group, part, land, onward, block):
        h = block // 2
        g = group
        self.h = h
        self.group = g
        self.part = part
        self.land = land
        self.onward = onward
        self.block = block

        self.first = [g.copy(self.at(g.cross, i), self.slot(i), i, g.core) for i in range(2)] + [
            g.copy(self.at(g.core, i), self.slot(2 + i), 2 + i, g.core) for i in range(2)
        ]
        self.second = [
            g.copy(onward.at[pl.ds(i * h, h)], self.slot(4 + i), 4 + i, g.over) for i in range(2)
        ]

    def at(self, t, half):
        return self.part.at[self.span(t, half)]

    def span(self, t, half):
        return pl.ds(pl.multiple_of(t * self.block + half * self.h, self.h), self.h)

    def slot(self, i):
        return self.land.at[pl.ds(i * self.h, self.h)]

    def start_half(self, half):
        self.first[half].start()
        self.first[2 + half].start()

    def start(self):
        self.start_half(0)
        self.start_half(1)

    def forward_half(self, i):
        h = self.h
        self.first[i].wait_recv()
        self.onward[i * h : (i + 1) * h] = (
            self.land[i * h : (i + 1) * h].astype(F32)
            + self.part[self.span(self.group.over, i)].astype(F32)
        ).astype(BF)
        self.second[i].start()

    def forward(self):
        self.forward_half(0)
        self.forward_half(1)

    def half(self, i):
        h = self.h
        self.first[2 + i].wait_recv()
        self.second[i].wait_recv()

        def got(j):
            return self.land[j * h : (j + 1) * h].astype(F32)

        return got(2 + i) + got(4 + i)

    def sent(self):
        for c in self.first + self.second:
            c.wait_send()

    def finish(self):
        halves = self.half(0), self.half(1)
        self.sent()
        return halves


def slots_of(ids):
    n = ids.shape[1]
    holder = lax.shift_right_logical(ids, 12)
    hits = iota((OWNERS, n), 0) == holder
    earlier = one_zero(iota((n, n), 0) < iota((n, n), 1))
    hits_b = one_zero(hits)
    before = jnp.sum(jnp.where(hits, mm(hits_b, earlier), 0.0), axis=0, keepdims=True)
    return holder, hits_b, before.astype(jnp.int32)


def wanted_rows(ids, hits_b, before, offset):
    n = ids.shape[1]
    marked = (ids & (ROWS - 1)) + 1
    chosen = iota((OWNERS, n), 0) == before + offset
    high = jnp.where(chosen, lax.shift_right_logical(marked, 6).astype(F32), 0.0).astype(BF)
    low = jnp.where(chosen, (marked & 63).astype(F32), 0.0).astype(BF)
    return 64.0 * mm_nt(hits_b, high) + mm_nt(hits_b, low)


def as_column(row):
    n = row.shape[1]
    wide = jnp.broadcast_to(row.astype(F32), (128, n))
    return jnp.transpose(wide)[:, 0:1].astype(jnp.int32)


def neg_row(negs_ref):
    return jnp.concatenate([negs_ref[u : u + 1, :] for u in range(4)], axis=1)


def part_mask(rows, width, per, parts):
    which = lax.rem(iota((rows, width), 0), 16) // per
    return [one_zero(which == c) for c in range(parts)]


def pick_parts(values, per, width):
    which = lax.div(lax.rem(iota((values.shape[0], width), 0), 16), per)
    out = values[:, 0:width]
    for c in range(1, values.shape[1] // width):
        out = jnp.where(which == c, values[:, c * width : (c + 1) * width], out)
    return out


def gather_rows(table, ids_col, out_ref, at):
    step = 1024

    def one(i, total):
        base = pl.multiple_of(i * step, step)
        pick = one_zero(ids_col == iota((512, step), 1) + i * step)
        return total + mm(pick, table[pl.ds(base, step), :])

    total = lax.fori_loop(0, ROWS // step, one, jnp.zeros((512, D), F32))
    out_ref[at : at + 512, :] = total.astype(BF)


def spread_chunks(rows_ref, chunks_ref, at, cap):
    width = cap * 32
    block = 128 // cap
    many = block * 16
    r, q = iota((many, 128), 0), iota((many, 128), 1)
    fold = one_zero(
        (lax.rem(q, block) == lax.div(r, 16)) & (lax.div(q, block) == lax.rem(r, cap))
    )
    for b in range(cap):
        rows = jnp.concatenate(
            [
                rows_ref[at + k * 128 + b * block : at + k * 128 + (b + 1) * block, :]
                for k in range(cap)
            ],
            axis=0,
        )
        chunks_ref[b * many : (b + 1) * many, :] = pick_parts(mm(fold, rows), cap, width).astype(BF)


def unfold(chunks, per, parts):
    rows, width = chunks.shape
    masks = part_mask(rows, width, per, parts)
    return jnp.concatenate([chunks * m for m in masks], axis=1)


def take_slots(chunks_ref, slot_col, cap):
    n = slot_col.shape[0]
    total = jnp.zeros((n, D), F32)
    step = 512
    for i in range(OWNERS * 16 // step):
        r = iota((n, step), 1) + i * step
        key = lax.div(r, 16) * cap + lax.rem(r, cap)
        total = total + mm(
            one_zero(slot_col == key),
            unfold(chunks_ref[i * step : (i + 1) * step, :], cap, 16 // cap),
        )
    return total.astype(BF)


def put_slots(rows, slot_row, chunks_ref, cap):
    n = slot_row.shape[1]
    step = 512
    for i in range(OWNERS * 16 // step):
        r = iota((step, n), 0) + i * step
        key = lax.div(r, 16) * cap + lax.rem(r, cap)
        chunks_ref[i * step : (i + 1) * step, :] = pick_parts(
            mm(one_zero(slot_row == key), rows), cap, cap * 32
        ).astype(BF)


def row_sum(values):
    return jnp.sum(values, axis=-1, keepdims=True)


def row_mean(values):
    return jnp.mean(values, axis=-1, keepdims=True)


def normal(values):
    center = values - row_mean(values)
    factor = lax.rsqrt(row_mean(center * center) + epsilon)
    return center * factor, factor


def normal_back(grad, normed, factor):
    return factor * (grad - row_mean(grad) - normed * row_mean(grad * normed))


def unit_factor(values):
    return lax.rsqrt(row_sum(values * values) + epsilon)


def unit_back(grad, values, factor):
    return factor * (grad - values * (factor * factor * row_sum(grad * values)))


class Users:
    def __init__(self, lengths_ref):
        self.lengths = [lengths_ref[0:1, u : u + 1] for u in range(4)]
        self.ends = []
        end = 0
        for length in self.lengths:
            end = end + length
            self.ends.append(end)

    def segment(self, t):
        return sum(jnp.where(t >= end, 1, 0) for end in self.ends)

    def start(self, t):
        return sum(jnp.where(t >= e, n, 0) for e, n in zip(self.ends, self.lengths))

    def length(self, t):
        out = jnp.where(t >= 0, self.lengths[0], 0)
        for u in range(1, 4):
            out = jnp.where(t >= self.ends[u - 1], self.lengths[u], out)
        return out


VM = pl.BlockSpec(memory_space=pltpu.VMEM)
HB = pl.BlockSpec(memory_space=pl.ANY)
Q = 256
KEYS = 768
SCALE = DH**-0.5
PIECE = 80


def layer_kernel(
    ids_ref,
    negs_ref,
    lengths_ref,
    table_hbm,
    w_in_hbm,
    w_out_hbm,
    ids_out,
    rows_out,
    weight_out,
    table_out,
    lengths_mine,
    ids_own,
    negs_own,
    lengths_own,
    table_ref,
    request_ref,
    arrived_ref,
    arrived_t_ref,
    hist_back,
    neg_back,
    picked_ref,
    hist_out,
    neg_out,
    hist_in,
    neg_in,
    w_in_ref,
    w_out_ref,
    emb_ref,
    neg_ref,
    unit_ref,
    normed_ref,
    proj_ref,
    slope_ref,
    weights_ref,
    dweights_ref,
    mixed_ref,
    factor_ref,
    gated_ref,
    y_ref,
    y_factor_ref,
    y_unit_ref,
    grown_ref,
    shares_ref,
    total_ref,
    whole_ref,
    drows_ref,
    dgated_ref,
    dgated_land,
    dgated_on,
    dout_part,
    dout_land,
    dout_on,
    demb_ref,
    emb_land,
    emb_on,
    rest_ref,
    dgate_ref,
    dvalue_ref,
    dquery_ref,
    dkey_ref,
    dpre_ref,
    weight_ref,
    weight_in,
    weight_mine,
    weight_sum,
    met_sem,
    load_sems,
    all_send,
    all_recv,
    ring_send,
    ring_recv,
    total_send,
    total_recv,
    move_send,
    move_recv,
):
    dp, tx = position()
    barrier = pltpu.get_barrier_semaphore()
    greet_planes(barrier, dp, tx)
    load = pltpu.make_async_copy(table_hbm, table_ref, load_sems.at[0])
    load.start()
    lengths_mine[...] = jnp.zeros_like(lengths_mine)
    lengths_mine[:, 0:4] = lengths_ref[...]

    def group(i):
        return Group(dp, tx, ring_send.at[i], ring_recv.at[i])

    here = group(0)
    role, chip, p, q = here.role, here.chip, lax.rem(tx, 2), lax.rem(dp, 2)
    after = lax.rem(role + 1, 4)
    group_dp = chip + lax.div(tx, 2)

    def rows_of(b, n=Q):
        return pl.ds(pl.multiple_of(b * n, n), n)

    to_dp, to_x = chip + p, 2 * q + lax.div(tx, 2)
    moved = [
        (ids_ref, ids_own),
        (negs_ref, negs_own),
        (lengths_mine, lengths_own),
        (w_out_hbm, w_out_ref.at[rows_of(tx, DH)]),
    ] + [(w_in_hbm.at[j], w_in_ref.at[:, j * DH : (j + 1) * DH]) for j in range(4)]
    stays = role == tx

    def remote(i):
        return pltpu.make_async_remote_copy(
            src_ref=moved[i][0],
            dst_ref=moved[i][1],
            send_sem=move_send.at[i],
            recv_sem=move_recv.at[i],
            device_id=(to_dp, to_x),
            device_id_type=MESH,
        )

    def moved_in(i):
        at = w_out_ref.at[rows_of(role, DH)] if i == 3 else moved[i][1]
        pltpu.make_async_copy(at, at, move_recv.at[i]).wait()

    pl.semaphore_wait(barrier, 22)
    greet_again(met_sem, dp, tx)

    def move(which):
        @pl.when(stays)
        def _():
            for i in which:
                pltpu.make_async_copy(*moved[i], move_recv.at[i]).start()

        @pl.when(jnp.logical_not(stays))
        def _():
            for i in which:
                remote(i).start()

    move(range(3))
    for i in range(3):
        moved_in(i)

    ids, negs = ids_own[...], neg_row(negs_own)
    holder_h, hits_h, before_h = slots_of(ids)
    holder_n, hits_n, before_n = slots_of(negs)
    wanted = wanted_rows(ids, hits_h, before_h, 0) + wanted_rows(negs, hits_n, before_n, CAP_H)
    request_ref[:, 0, :] = wanted.astype(jnp.int32) - 1
    slot_h = holder_h * CAP_H + before_h
    slot_n = holder_n * CAP_N + before_n

    pl.semaphore_wait(met_sem, 7)
    spread_all(request_ref, arrived_ref, 1, all_send.at[0], all_recv.at[0], dp, tx)
    load.wait()
    slot_h_col, slot_n_col = as_column(slot_h), as_column(slot_n)
    users = Users(lengths_own)
    wait_rows(arrived_ref, OWNERS - 1, all_recv.at[0])
    move(range(3, 8))

    arrived = arrived_ref[:, 0, :]
    columns = [arrived[:, k : k + 1] for k in range(CAP_H + CAP_N)]
    gather_rows(table_ref, jnp.concatenate(columns[0:4], axis=0), picked_ref, 0)
    spread_chunks(picked_ref, hist_out, 0, CAP_H)
    spread_all(hist_out, hist_in, 16, all_send.at[1], all_recv.at[1], dp, tx)
    gather_rows(table_ref, jnp.concatenate(columns[4:8], axis=0), picked_ref, 512)
    moved_in(3)
    w_outs = Gather(group(1), w_out_ref, DH)
    w_outs.start()

    wait_rows(hist_in, (OWNERS - 1) * 16, all_recv.at[1])
    emb_ref[rows_of(role), :] = take_slots(hist_in, slot_h_col, CAP_H)
    hist = Gather(group(0), emb_ref, Q)
    hist.start()

    def project(b):
        at = rows_of(b)
        normed = normal(emb_ref[at, :].astype(F32))[0].astype(BF)
        normed_ref[at, :] = normed
        pre = mm(normed, w_in_ref[...])
        gate = lax.logistic(pre)
        proj_ref[at, :] = (pre * gate).astype(BF)
        slope_ref[at, :] = gate * (1.0 + pre * (1.0 - gate))

    w_outs.forward()
    gather_rows(table_ref, jnp.concatenate(columns[8:12], axis=0), picked_ref, 1024)
    hist.forward()
    spread_chunks(picked_ref, neg_out, 512, CAP_N)
    spread_all(neg_out, neg_in, 16, all_send.at[2], all_recv.at[2], dp, tx)
    for i in range(4, 8):
        moved_in(i)
    project(role)
    hist.near()
    project(here.core)
    project(here.over)
    for c in hist.second:
        c.wait_recv()
    project(here.cross)

    arrived_t_ref[...] = jnp.transpose(arrived.astype(F32)).astype(jnp.int32)

    mine = pl.multiple_of(role * 1024, 1024)

    def keys_of(b):
        low = max(b - 2, 0)
        return slice(low * Q, (b + 1) * Q), low

    def attend(b):
        at = slice(b * Q, (b + 1) * Q)
        kr, low = keys_of(b)
        n = kr.stop - kr.start
        scores = mm_nt(proj_ref[at, 256:384], proj_ref[kr, 384:512]) * SCALE
        t = iota((Q, 1), 0) + b * Q
        s = iota((Q, n), 1) + low * Q
        seen = (s <= t) & (s >= users.start(t))
        share = 1.0 / users.length(t).astype(F32)
        gate = lax.logistic(scores)
        weights = jnp.where(seen, scores * gate * share, 0.0).astype(BF)
        weights_ref[at, 0:n] = weights
        dweights_ref[at, 0:n] = jnp.where(
            seen, gate * (1.0 + scores * (1.0 - gate)) * (share * SCALE), 0.0
        )
        mixed, factor = normal(mm(weights, proj_ref[kr, 128:256]))
        mixed_ref[at, :] = mixed
        factor_ref[at, :] = jnp.broadcast_to(factor, (Q, DH))
        gated_ref[pl.ds(mine + b * Q, Q), :] = (mixed * proj_ref[at, 0:128].astype(F32)).astype(BF)

    gates = Gather(group(2), gated_ref, 1024)
    attend(0)
    attend(1)
    gates.start_half(0)
    attend(2)
    attend(3)
    gates.start_half(1)

    wait_rows(neg_in, (OWNERS - 1) * 16, all_recv.at[2])
    neg_ref[...] = take_slots(neg_in, slot_n_col, CAP_N)
    gates.forward()
    neg_f = neg_ref[...].astype(F32)
    neg_factor = unit_factor(neg_f)
    unit_ref[...] = (neg_f * neg_factor).astype(BF)
    w_outs.finish()
    arrived_t_ref[...] = jnp.transpose(arrived.astype(F32)).astype(jnp.int32)

    emb_f = emb_ref[rows_of(role), :].astype(F32)
    follow = jnp.where(
        iota((Q, 1), 0) == Q - 1,
        emb_ref[rows_of(after), :].astype(F32)[0:1, :],
        pltpu.roll(emb_f, Q - 1, 0),
    )
    follow_factor = unit_factor(follow)
    follow_unit = (follow * follow_factor).astype(BF).astype(F32)
    t_row = iota((1, 1024), 1)
    segment = users.segment(t_row)
    valid = users.segment(t_row + 1) == segment
    users_of = [jnp.where(segment == u, 1.0, 0.0) for u in range(4)]
    gates.arrived(0)

    for b in range(4):
        if b == 2:
            gates.arrived(1)
        at = slice(b * Q, (b + 1) * Q)
        gated = jnp.concatenate(
            [gated_ref[h * 1024 + b * Q : h * 1024 + (b + 1) * Q, :] for h in range(4)], axis=1
        )
        y = emb_ref[at, :].astype(F32) + mm(gated, w_out_ref[...])
        factor = unit_factor(y)
        y_unit = (y * factor).astype(BF)
        y_ref[at, :] = y
        y_factor_ref[at, :] = jnp.broadcast_to(factor, (Q, DH))
        y_unit_ref[at, :] = y_unit
        grown = jnp.exp(sharpness * mm_nt(unit_ref[...], y_unit))
        grown = jnp.concatenate(
            [grown[u * DH : (u + 1) * DH, :] * users_of[u][:, at] for u in range(4)], axis=0
        )
        grown_ref[:, at] = grown
        total_ref[role, :, at] = jnp.sum(grown, axis=0, keepdims=True)

    y_unit_f = y_unit_ref[rows_of(role), :].astype(F32)
    grown_pos = jnp.exp(sharpness * row_sum(y_unit_f * follow_unit))
    own_lanes = pl.ds(pl.multiple_of(role * Q, Q), Q)
    grown_pos_row = jnp.transpose(jnp.broadcast_to(grown_pos, (Q, DH)))[0:1, :]
    total_ref[role, :, own_lanes] += grown_pos_row
    totals = [
        Group(dp, tx, total_send, total_recv).copy(total_ref.at[role], total_ref.at[role], i, to)
        for i, to in enumerate((here.over, here.cross, here.core))
    ]
    for c in totals:
        c.start()
    for c in totals:
        c.wait_recv()
    total = total_ref[0] + total_ref[1] + total_ref[2] + total_ref[3]
    whole_ref[...] = jnp.where(valid, sharpness / total, 0.0)
    scaled_own = jnp.transpose(jnp.broadcast_to(whole_ref[:, own_lanes], (DH, Q)))[:, 0:1]
    d_pos = jnp.where(scaled_own > 0.0, scaled_own * grown_pos - sharpness, 0.0)
    d_unit_pos = d_pos * follow_unit
    gate_sum = Scatter(group(3), dgated_ref, dgated_land, dgated_on, 1024)
    for b in range(4):
        at = slice(b * Q, (b + 1) * Q)
        shares = (grown_ref[:, at] * whole_ref[:, at]).astype(BF)
        shares_ref[:, at] = shares
        d_unit = mm_tn(shares, unit_ref[...]) + jnp.where(role == b, d_unit_pos, 0.0)
        d_rows = unit_back(d_unit, y_ref[at, :], y_factor_ref[at, :][:, 0:1])
        drows_ref[at, :] = d_rows
        d_gated = mm_nt(d_rows.astype(BF), w_out_ref[...]).astype(BF)
        for h in range(4):
            dgated_ref[h * 1024 + b * Q : h * 1024 + (b + 1) * Q, :] = d_gated[
                :, h * DH : (h + 1) * DH
            ]
        if b == 1:
            gate_sum.start_half(0)
    gate_sum.start_half(1)
    gate_sum.forward()

    d_neg = unit_back(
        mm(shares_ref[...], y_unit_ref[...]),
        neg_ref[...].astype(F32),
        unit_factor(neg_ref[...].astype(F32)),
    )
    wait_rows(neg_out, (OWNERS - 1) * 16, all_send.at[2])
    put_slots(d_neg.astype(BF), slot_n, neg_out, CAP_N)
    spread_all(neg_out, neg_back, 16, all_send.at[4], all_recv.at[4], dp, tx)
    for h in range(4):
        dout_part[h * DH : (h + 1) * DH, :] = mm_tn(
            gated_ref[h * 1024 : (h + 1) * 1024, :], drows_ref[...].astype(BF)
        ).astype(BF)
    w_out_sum = Scatter(group(4), dout_part, dout_land, dout_on, DH)
    w_out_sum.start()
    d_follow = unit_back(d_pos * y_unit_f, follow, follow_factor)
    rest_ref[0:Q, :] = jnp.where(iota((Q, 1), 0) == 0, 0.0, pltpu.roll(d_follow, 1, 0))
    rest_ref[Q : Q + 8, :] = jnp.where(iota((8, 1), 0) == 0, d_follow[Q - 1 : Q, :], 0.0)
    dkey_ref[...] = jnp.zeros_like(dkey_ref)
    dvalue_ref[...] = jnp.zeros_like(dvalue_ref)
    halves = [gate_sum.half(0)]

    def attend_back(b):
        at = slice(b * Q, (b + 1) * Q)
        kr, _ = keys_of(b)
        n = kr.stop - kr.start
        half = halves[b // 2][(b % 2) * Q : (b % 2 + 1) * Q, :]
        d_gated = half + dgated_ref[pl.ds(mine + b * Q, Q), :].astype(F32)
        mixed = mixed_ref[at, :]
        dgate_ref[at, :] = (d_gated * mixed).astype(BF)
        d_mixed = normal_back(
            d_gated * proj_ref[at, 0:128].astype(F32), mixed, factor_ref[at, :][:, 0:1]
        ).astype(BF)
        d_scores = (mm_nt(d_mixed, proj_ref[kr, 128:256]) * dweights_ref[at, 0:n]).astype(BF)
        dquery_ref[at, :] = mm(d_scores, proj_ref[kr, 384:512]).astype(BF)
        dkey_ref[kr, :] += mm_tn(d_scores, proj_ref[at, 256:384])
        dvalue_ref[kr, :] += mm_tn(weights_ref[at, 0:n], d_mixed)

    attend_back(0)
    attend_back(1)
    w_out_sum.forward()
    halves.append(gate_sum.half(1))
    attend_back(2)
    attend_back(3)

    def project_back(b):
        at = rows_of(b)
        d_proj = jnp.concatenate(
            [
                dgate_ref[at, :].astype(F32),
                dvalue_ref[at, :].astype(BF).astype(F32),
                dquery_ref[at, :].astype(F32),
                dkey_ref[at, :].astype(BF).astype(F32),
            ],
            axis=1,
        )
        d_pre = (d_proj * slope_ref[at, :]).astype(BF)
        dpre_ref[at, :] = d_pre
        normed, factor = normal(emb_ref[at, :].astype(F32))
        d_normed = mm_nt(d_pre, w_in_ref[...]).astype(BF).astype(F32)
        return normal_back(d_normed, normed, factor) + drows_ref[at, :]

    emb_sum = Scatter(group(5), demb_ref, emb_land, emb_on, Q)
    def send_part(b):
        next_first = jnp.where((iota((Q, 1), 0) == 0) & (b == after), rest_ref[Q : Q + 1, :], 0.0)
        demb_ref[rows_of(b), :] = (project_back(b) + next_first).astype(BF)

    send_part(here.cross)
    emb_sum.first[0].start()
    emb_sum.first[1].start()
    send_part(here.over)
    emb_sum.forward()
    send_part(here.core)
    emb_sum.first[2].start()
    emb_sum.first[3].start()
    rest_ref[0:Q, :] += project_back(role)

    d_win = mm_tn(normed_ref[...], dpre_ref[...]).astype(BF)
    first, second = w_out_sum.finish()
    d_wout = jnp.concatenate([first, second], axis=0) + dout_part[rows_of(role, DH), :].astype(F32)
    for j in range(4):
        weight_ref[j * D : (j + 1) * D, :] = d_win[:, j * DH : (j + 1) * DH]
        weight_ref[2048 + j * DH : 2048 + (j + 1) * DH, :] = d_wout[
            :, j * DH : (j + 1) * DH
        ].astype(BF)
    own = pl.ds(pl.multiple_of(group_dp * PIECE, 16), PIECE)

    def out_piece(base, other):
        to = base + other
        pltpu.make_async_remote_copy(
            src_ref=weight_ref.at[pl.ds(pl.multiple_of(to * PIECE, 16), PIECE)],
            dst_ref=weight_in.at[own],
            send_sem=all_send.at[5],
            recv_sem=all_recv.at[5],
            device_id=(base + q, 2 * other + p),
            device_id_type=MESH,
        ).start()

    def back_piece(to):
        pltpu.make_async_remote_copy(
            src_ref=weight_mine,
            dst_ref=weight_sum.at[own],
            send_sem=all_send.at[6],
            recv_sem=all_recv.at[6],
            device_id=(to, role),
            device_id_type=MESH,
        ).start()

    def out_pieces(base):
        out_piece(base, 0)
        out_piece(base, 1)

    def back_pieces(base):
        back_piece(base)
        back_piece(base + 1)

    each_chip(dp, tx, out_pieces)
    out_piece(chip, 1 - lax.div(tx, 2))
    weight_in[own] = weight_ref[own]

    wait_rows(neg_back, (OWNERS - 1) * 16, all_recv.at[4])
    gather_chunks(neg_back, picked_ref, 512, CAP_N)

    def add_negatives(i, carry):
        at = pl.ds(pl.multiple_of(i * 512, 512), 512)
        total = put_rows(arrived_t_ref, picked_ref, i * 512, 4, 512)
        total = total + put_rows(arrived_t_ref, picked_ref, i * 512, 8, 512)
        table_ref[at, :] = total.astype(BF)
        return carry

    lax.fori_loop(0, 4, add_negatives, 0)

    first, second = emb_sum.finish()
    d_hist = rest_ref[0:Q, :] + jnp.concatenate([first, second], axis=0)
    wait_rows(hist_out, (OWNERS - 1) * 16, all_send.at[1])
    put_slots(d_hist.astype(BF), slot_h, hist_out, CAP_H)
    spread_all(hist_out, hist_back, 16, all_send.at[3], all_recv.at[3], dp, tx)

    wait_rows(weight_in, (N_DP - 1) * PIECE, all_recv.at[5])
    total = weight_in[0:PIECE, :].astype(F32)
    for i in range(1, N_DP):
        total = total + weight_in[i * PIECE : (i + 1) * PIECE, :].astype(F32)
    weight_mine[...] = total.astype(BF)
    each_chip(dp, tx, back_pieces)
    back_piece(chip + 1 - q)

    @pl.when(stays)
    def _():
        weight_sum[own] = weight_mine[...]

    @pl.when(jnp.logical_not(stays))
    def _():
        back_piece(dp)


    lax.fori_loop(4, 8, add_negatives, 0)
    keep = pltpu.make_async_copy(table_ref, table_out, load_sems.at[3])
    keep.start()
    wait_rows(hist_back, (OWNERS - 1) * 16, all_recv.at[3])
    gather_chunks(hist_back, picked_ref, 0, CAP_H)

    @pl.when(stays)
    def _():
        wait_rows(weight_sum, (N_DP - 1) * PIECE, all_recv.at[6])
        wait_rows(weight_in, (N_DP - 1) * PIECE, all_send.at[6])

    @pl.when(jnp.logical_not(stays))
    def _():
        wait_rows(weight_sum, N_DP * PIECE, all_recv.at[6])
        wait_rows(weight_in, N_DP * PIECE, all_send.at[6])
        for i in range(len(moved)):
            remote(i).wait_send()

    results = [
        pltpu.make_async_copy(arrived_t_ref, ids_out, load_sems.at[0]),
        pltpu.make_async_copy(picked_ref.at[0:512], rows_out, load_sems.at[1]),
        pltpu.make_async_copy(weight_sum, weight_out, load_sems.at[2]),
    ]
    for move in results:
        move.start()
    for move in results + [keep]:
        move.wait()
    for c in totals + hist.first + hist.second:
        c.wait_send()
    gates.sent()
    gate_sum.sent()
    wait_rows(request_ref, OWNERS - 1, all_send.at[0])
    wait_rows(hist_out, (OWNERS - 1) * 16, all_send.at[3])
    wait_rows(neg_out, (OWNERS - 1) * 16, all_send.at[4])
    wait_rows(weight_in, (N_DP - 1) * PIECE, all_send.at[5])


def layer(ids, negs, lengths, table, w_in, w_out):
    sem = pltpu.SemaphoreType.DMA
    vm = pltpu.VMEM
    return pl.pallas_call(
        layer_kernel,
        out_shape=[
            jax.ShapeDtypeStruct((128, 128), jnp.int32),
            jax.ShapeDtypeStruct((CAP_H * OWNERS, D), BF),
            jax.ShapeDtypeStruct((2560, 128), BF),
            jax.ShapeDtypeStruct((ROWS, D), BF),
        ],
        in_specs=[VM, VM, VM, HB, HB, HB],
        out_specs=[HB] * 4,
        scratch_shapes=[
            vm((1, 128), jnp.int32),
            vm((1, 256), jnp.int32),
            vm((4, 128), jnp.int32),
            vm((1, 128), jnp.int32),
            vm((ROWS, D), BF),
            vm((OWNERS, 1, 128), jnp.int32),
            vm((OWNERS, 1, 128), jnp.int32),
            vm((128, 128), jnp.int32),
            vm((OWNERS * 16, 128), BF),
            vm((OWNERS * 16, 256), BF),
            vm((12 * OWNERS, D), BF),
            vm((OWNERS * 16, 128), BF),
            vm((OWNERS * 16, 256), BF),
            vm((OWNERS * 16, 128), BF),
            vm((OWNERS * 16, 256), BF),
            vm((D, D), BF),
            vm((D, D), BF),
            vm((1024, D), BF),
            vm((512, D), BF),
            vm((512, D), BF),
            vm((1024, D), BF),
            vm((1024, D), BF),
            vm((1024, D), F32),
            vm((1024, KEYS), BF),
            vm((1024, KEYS), F32),
            vm((1024, DH), F32),
            vm((1024, DH), F32),
            vm((4096, DH), BF),
            vm((1024, D), F32),
            vm((1024, DH), F32),
            vm((1024, D), BF),
            vm((512, 1024), F32),
            vm((512, 1024), BF),
            vm((4, 1, 1024), F32),
            vm((1, 1024), F32),
            vm((1024, D), F32),
            vm((4096, DH), BF),
            vm((6 * 512, DH), BF),
            vm((2 * 512, DH), BF),
            vm((D, D), BF),
            vm((6 * 64, D), BF),
            vm((2 * 64, D), BF),
            vm((1024, D), BF),
            vm((6 * 128, D), BF),
            vm((2 * 128, D), BF),
            vm((Q + 8, D), F32),
            vm((1024, DH), BF),
            vm((1024, DH), F32),
            vm((1024, DH), BF),
            vm((1024, DH), F32),
            vm((1024, D), BF),
            vm((2560, 128), BF),
            vm((2560, 128), BF),
            vm((PIECE, 128), BF),
            vm((2560, 128), BF),
            pltpu.SemaphoreType.REGULAR,
            sem((6,)),
            sem((7,)),
            sem((7,)),
            sem((6, 6)),
            sem((6, 6)),
            sem((3,)),
            sem((3,)),
            sem((8,)),
            sem((8,)),
        ],
        compiler_params=pltpu.CompilerParams(
            collective_id=0, has_side_effects=True, vmem_limit_bytes=56 * 1024 * 1024
        ),
        name="layer",
    )(ids, negs, lengths, table, w_in, w_out)


def gather_chunks(chunks_ref, rows_ref, at, cap):
    block = 128 // cap
    many = block * 16
    q, r = iota((128, many), 0), iota((128, many), 1)
    fold = one_zero(
        (lax.rem(q, block) == lax.div(r, 16)) & (lax.div(q, block) == lax.rem(r, cap))
    )
    for b in range(cap):
        wide = unfold(chunks_ref[b * many : (b + 1) * many, :], cap, 16 // cap)
        rows = mm(fold, wide).astype(BF)
        for k in range(cap):
            rows_ref[at + k * 128 + b * block : at + k * 128 + (b + 1) * block, :] = rows[
                k * block : (k + 1) * block
            ]


def put_rows(ids_ref, rows_ref, first, slot, tile):
    row = jnp.concatenate([ids_ref[slot + j : slot + j + 1, :] for j in range(4)], axis=1)
    put = one_zero(row == iota((tile, 512), 0) + first)
    return mm(put, rows_ref[slot * 128 : (slot + 4) * 128, :])


TILES = 8


def add_kernel(
    ids_hbm,
    rows_hbm,
    weight_hbm,
    part_hbm,
    out_hbm,
    w_in_hbm,
    w_out_hbm,
    ids_ref,
    rows_ref,
    weight_ref,
    part_ref,
    out_ref,
    w_in_ref,
    w_out_ref,
    in_sems,
    part_sems,
    out_sems,
    w_sems,
):
    tile = ROWS // TILES
    moves = [
        pltpu.make_async_copy(ids_hbm, ids_ref, in_sems.at[0]),
        pltpu.make_async_copy(rows_hbm, rows_ref, in_sems.at[1]),
        pltpu.make_async_copy(weight_hbm, weight_ref, in_sems.at[2]),
    ]
    parts, outs = [], []
    for i in range(TILES):
        at = pl.ds(i * tile, tile)
        parts.append(pltpu.make_async_copy(part_hbm.at[at], part_ref.at[at], part_sems.at[i]))
        outs.append(pltpu.make_async_copy(out_ref.at[at], out_hbm.at[at], out_sems.at[i]))
    for move in moves + parts:
        move.start()
    moves[0].wait()
    moves[1].wait()
    for i in range(TILES):
        at = pl.ds(i * tile, tile)
        parts[i].wait()
        out_ref[at, :] = part_ref[at, :].astype(F32) + put_rows(ids_ref, rows_ref, i * tile, 0, tile)
        outs[i].start()
    moves[2].wait()
    w_in_ref[...] = weight_ref[0:2048, :].astype(F32)
    w_out_ref[...] = jnp.concatenate(
        [weight_ref[2048 + c * 128 : 2048 + (c + 1) * 128, :] for c in range(4)], axis=1
    ).astype(F32)
    weights = [
        pltpu.make_async_copy(w_in_ref, w_in_hbm, w_sems.at[0]),
        pltpu.make_async_copy(w_out_ref, w_out_hbm, w_sems.at[1]),
    ]
    for move in weights:
        move.start()
    for move in outs + weights:
        move.wait()


def add_rows(ids, rows, weight, part):
    anywhere = pl.BlockSpec(memory_space=pl.ANY)
    sem = pltpu.SemaphoreType.DMA
    return pl.pallas_call(
        add_kernel,
        out_shape=[
            jax.ShapeDtypeStruct((ROWS, D), F32),
            jax.ShapeDtypeStruct((2048, DH), F32),
            jax.ShapeDtypeStruct((DH, D), F32),
        ],
        in_specs=[anywhere] * 4,
        out_specs=[anywhere] * 3,
        scratch_shapes=[
            pltpu.VMEM((128, 128), jnp.int32),
            pltpu.VMEM((CAP_H * OWNERS, D), BF),
            pltpu.VMEM((2560, 128), BF),
            pltpu.VMEM((ROWS, D), BF),
            pltpu.VMEM((ROWS, D), F32),
            pltpu.VMEM((2048, DH), F32),
            pltpu.VMEM((DH, D), F32),
            sem((3,)),
            sem((TILES,)),
            sem((TILES,)),
            sem((2,)),
        ],
        compiler_params=pltpu.CompilerParams(vmem_limit_bytes=56 * 1024 * 1024),
        name="add_rows",
    )(ids, rows, weight, part)


def on_device(table, item_ids, negatives, lengths, w_in, w_out):
    ids, rows, weight, part = layer(item_ids.reshape(1, -1), negatives, lengths, table, w_in, w_out)
    grad_table, grad_w_in, grad_w_out = add_rows(ids, rows, weight, part)
    return (grad_table, grad_w_in.reshape(4, D, DH), grad_w_out)


def solution(mesh):
    placed = (
        P(("dp", "table"), None),
        P(("dp", "table")),
        P("dp", "table"),
        P("dp", None),
        P(None, None, "table"),
        P("table", None),
    )
    return jax.shard_map(
        on_device,
        mesh=mesh,
        in_specs=placed,
        out_specs=(P(("dp", "table"), None), P(None, None, "table"), P("table", None)),
        check_vma=False,
    )
```

```python
import functools
import jax
import jax.numpy as jnp
from jax import lax
from jax.experimental import pallas as pl
from jax.experimental.pallas import tpu as pltpu
from jax.sharding import PartitionSpec as P

DH = 128
D = 512
CAP_H = 4
CAP_N = 8
OWNERS = 128
N_DP = 32
N_TABLE = 4
ROWS = 4096
BF = jnp.bfloat16
F32 = jnp.float32
MESH = pl.DeviceIdType.MESH

epsilon = 1e-06
sharpness = 20.0


def iota(shape, dim):
    return lax.broadcasted_iota(jnp.int32, shape, dim)


def one_zero(mask):
    return jnp.where(mask, 1.0, 0.0).astype(BF)


def mm(a, b):
    return lax.dot_general(a, b, (((1,), (0,)), ((), ())), preferred_element_type=F32)


def mm_nt(a, b):
    return lax.dot_general(a, b, (((1,), (1,)), ((), ())), preferred_element_type=F32)


def mm_tn(a, b):
    return lax.dot_general(a, b, (((0,), (0,)), ((), ())), preferred_element_type=F32)


def position():
    dp = lax.axis_index("dp")
    tx = lax.axis_index("table")
    return dp, tx


def coordinates(dp, tx):
    z, y, c = lax.div(dp, 8), lax.rem(lax.div(dp, 2), 4), lax.rem(dp, 2)
    near = [(core, lax.rem(tx + dx, 4)) for core in (1 - c, c) for dx in range(4)]
    return z, y, near[4:] + near[:4]


def plane_base(z, y, step):
    return lax.rem(z + lax.div(step, 4), 4) * 8 + lax.rem(y + lax.rem(step, 4), 4) * 2


def each_partner(dp, tx, do):
    z, y, near = coordinates(dp, tx)

    def one(i, carry):
        base = plane_base(z, y, lax.rem(i * 7, 16))
        for core, x in near:
            do(base + core, x)
        return carry

    lax.fori_loop(1, 16, one, 0)
    for core, x in near[1:]:
        do(z * 8 + y * 2 + core, x)


def each_dp(dp, tx, do):
    z, y, near = coordinates(dp, tx)
    mine, other = near[0][0], near[4][0]

    def one(i, carry):
        base = plane_base(z, y, lax.rem(i * 7, 16))
        do(base + mine)
        do(base + other)
        return carry

    lax.fori_loop(1, 16, one, 0)
    do(z * 8 + y * 2 + other)


def signal(sem, dp, x):
    pl.semaphore_signal(sem, inc=1, device_id=(dp, x), device_id_type=MESH)


def greet_planes(barrier, dp, tx):
    z, y, near = coordinates(dp, tx)
    for core, x in near[1:]:
        signal(barrier, z * 8 + y * 2 + core, x)
    core, x = near[0]
    for i in range(1, 16):
        signal(barrier, plane_base(z, y, i) + core, x)


def greet_again(sem, dp, tx):
    z, y, near = coordinates(dp, tx)
    for core, x in near[1:]:
        signal(sem, z * 8 + y * 2 + core, x)


def spread_all(src, dst, chunk, send_sem, recv_sem, dp, tx):
    me = dp * 4 + tx
    land = pl.ds(pl.multiple_of(me * chunk, chunk), chunk)

    def one(pd, px):
        pltpu.make_async_remote_copy(
            src_ref=src.at[pl.ds(pl.multiple_of((pd * 4 + px) * chunk, chunk), chunk)],
            dst_ref=dst.at[land],
            send_sem=send_sem,
            recv_sem=recv_sem,
            device_id=(pd, px),
            device_id_type=MESH,
        ).start()

    each_partner(dp, tx, one)
    dst[land] = src[land]


def wait_rows(ref, count, sem):
    pltpu.make_async_copy(ref.at[pl.ds(0, count)], ref.at[pl.ds(0, count)], sem).wait()


class Ring:
    def __init__(self, dp, tx, send_sems, recv_sems):
        self.dp = dp
        self.tx = tx
        self.right = lax.rem(tx + 1, 4)
        self.left = lax.rem(tx + 3, 4)
        self.far = lax.rem(tx + 2, 4)
        self.send_sems = send_sems
        self.recv_sems = recv_sems

    def copy(self, src, dst, slot, to):
        return pltpu.make_async_remote_copy(
            src_ref=src,
            dst_ref=dst,
            send_sem=self.send_sems.at[slot],
            recv_sem=self.recv_sems.at[slot],
            device_id=(self.dp, to),
            device_id_type=MESH,
        )


class Gather:
    def __init__(self, ring, buf, block):
        h = block // 2
        r = ring

        def part(t, half):
            return buf.at[pl.ds(pl.multiple_of(t * block + half * h, h), h)]

        self.first = [
            r.copy(part(r.tx, 0), part(r.tx, 0), 0, r.right),
            r.copy(part(r.tx, 1), part(r.tx, 1), 1, r.left),
            r.copy(part(r.tx, 1), part(r.tx, 1), 2, r.right),
            r.copy(part(r.tx, 0), part(r.tx, 0), 3, r.left),
        ]
        self.second = [
            r.copy(part(r.left, 0), part(r.left, 0), 4, r.right),
            r.copy(part(r.right, 1), part(r.right, 1), 5, r.left),
        ]

    def start(self):
        for c in self.first:
            c.start()

    def forward(self):
        for c, d in zip(self.first[:2], self.second):
            c.wait_recv()
            d.start()

    def arrived(self, half):
        self.first[3 - half].wait_recv()
        self.second[half].wait_recv()

    def sent(self):
        for c in self.first + self.second:
            c.wait_send()

    def finish(self):
        self.arrived(0)
        self.arrived(1)
        self.sent()


class Scatter:
    def __init__(self, ring, part, land, onward, block):
        h = block // 2
        r = ring
        self.h = h
        self.ring = r
        self.part = part
        self.land = land
        self.onward = onward
        self.block = block

        self.first = [
            r.copy(self.at(r.far, 0), self.slot(0), 0, r.right),
            r.copy(self.at(r.far, 1), self.slot(1), 1, r.left),
            r.copy(self.at(r.right, 1), self.slot(2), 2, r.right),
            r.copy(self.at(r.left, 0), self.slot(3), 3, r.left),
        ]
        self.second = [
            r.copy(onward.at[pl.ds(0, h)], self.slot(4), 4, r.right),
            r.copy(onward.at[pl.ds(h, h)], self.slot(5), 5, r.left),
        ]

    def at(self, t, half):
        return self.part.at[self.span(t, half)]

    def span(self, t, half):
        return pl.ds(pl.multiple_of(t * self.block + half * self.h, self.h), self.h)

    def slot(self, i):
        return self.land.at[pl.ds(i * self.h, self.h)]

    def start(self):
        for c in self.first:
            c.start()

    def forward(self):
        h = self.h
        for i, t in enumerate((self.ring.right, self.ring.left)):
            self.first[i].wait_recv()
            self.onward[i * h : (i + 1) * h] = (
                self.land[i * h : (i + 1) * h].astype(F32) + self.part[self.span(t, i)].astype(F32)
            ).astype(BF)
            self.second[i].start()

    def half(self, i):
        h = self.h
        self.first[3 - i].wait_recv()
        self.second[i].wait_recv()

        def got(j):
            return self.land[j * h : (j + 1) * h].astype(F32)

        return got(3 - i) + got(4 + i)

    def sent(self):
        for c in self.first + self.second:
            c.wait_send()

    def finish(self):
        halves = self.half(0), self.half(1)
        self.sent()
        return halves


def slots_of(ids):
    n = ids.shape[1]
    holder = lax.shift_right_logical(ids, 12)
    hits = iota((OWNERS, n), 0) == holder
    earlier = one_zero(iota((n, n), 0) < iota((n, n), 1))
    hits_b = one_zero(hits)
    before = jnp.sum(jnp.where(hits, mm(hits_b, earlier), 0.0), axis=0, keepdims=True)
    return holder, hits_b, before.astype(jnp.int32)


def wanted_rows(ids, hits_b, before, offset):
    n = ids.shape[1]
    marked = (ids & (ROWS - 1)) + 1
    chosen = iota((OWNERS, n), 0) == before + offset
    high = jnp.where(chosen, lax.shift_right_logical(marked, 6).astype(F32), 0.0).astype(BF)
    low = jnp.where(chosen, (marked & 63).astype(F32), 0.0).astype(BF)
    return 64.0 * mm_nt(hits_b, high) + mm_nt(hits_b, low)


def as_column(row):
    n = row.shape[1]
    wide = jnp.broadcast_to(row.astype(F32), (128, n))
    return jnp.transpose(wide)[:, 0:1].astype(jnp.int32)


def neg_row(negs_ref):
    return jnp.concatenate([negs_ref[u : u + 1, :] for u in range(4)], axis=1)


def part_mask(rows, width, per, parts):
    which = lax.rem(iota((rows, width), 0), 16) // per
    return [one_zero(which == c) for c in range(parts)]


def pick_parts(values, per, width):
    which = lax.div(lax.rem(iota((values.shape[0], width), 0), 16), per)
    out = values[:, 0:width]
    for c in range(1, values.shape[1] // width):
        out = jnp.where(which == c, values[:, c * width : (c + 1) * width], out)
    return out


def gather_rows(table, ids_col, out_ref, at):
    step = 1024

    def one(i, total):
        base = pl.multiple_of(i * step, step)
        pick = one_zero(ids_col == iota((512, step), 1) + i * step)
        return total + mm(pick, table[pl.ds(base, step), :])

    total = lax.fori_loop(0, ROWS // step, one, jnp.zeros((512, D), F32))
    out_ref[at : at + 512, :] = total.astype(BF)


def spread_chunks(rows_ref, chunks_ref, at, cap):
    width = cap * 32
    block = 128 // cap
    many = block * 16
    r, q = iota((many, 128), 0), iota((many, 128), 1)
    fold = one_zero(
        (lax.rem(q, block) == lax.div(r, 16)) & (lax.div(q, block) == lax.rem(r, cap))
    )
    for b in range(cap):
        rows = jnp.concatenate(
            [
                rows_ref[at + k * 128 + b * block : at + k * 128 + (b + 1) * block, :]
                for k in range(cap)
            ],
            axis=0,
        )
        chunks_ref[b * many : (b + 1) * many, :] = pick_parts(mm(fold, rows), cap, width).astype(BF)


def unfold(chunks, per, parts):
    rows, width = chunks.shape
    masks = part_mask(rows, width, per, parts)
    return jnp.concatenate([chunks * m for m in masks], axis=1)


def take_slots(chunks_ref, slot_col, cap):
    n = slot_col.shape[0]
    total = jnp.zeros((n, D), F32)
    step = 512
    for i in range(OWNERS * 16 // step):
        r = iota((n, step), 1) + i * step
        key = lax.div(r, 16) * cap + lax.rem(r, cap)
        total = total + mm(
            one_zero(slot_col == key),
            unfold(chunks_ref[i * step : (i + 1) * step, :], cap, 16 // cap),
        )
    return total.astype(BF)


def put_slots(rows, slot_row, chunks_ref, cap):
    n = slot_row.shape[1]
    step = 512
    for i in range(OWNERS * 16 // step):
        r = iota((step, n), 0) + i * step
        key = lax.div(r, 16) * cap + lax.rem(r, cap)
        chunks_ref[i * step : (i + 1) * step, :] = pick_parts(
            mm(one_zero(slot_row == key), rows), cap, cap * 32
        ).astype(BF)


def row_sum(values):
    return jnp.sum(values, axis=-1, keepdims=True)


def row_mean(values):
    return jnp.mean(values, axis=-1, keepdims=True)


def normal(values):
    center = values - row_mean(values)
    factor = lax.rsqrt(row_mean(center * center) + epsilon)
    return center * factor, factor


def normal_back(grad, normed, factor):
    return factor * (grad - row_mean(grad) - normed * row_mean(grad * normed))


def unit_factor(values):
    return lax.rsqrt(row_sum(values * values) + epsilon)


def unit_back(grad, values, factor):
    return factor * (grad - values * (factor * factor * row_sum(grad * values)))


class Users:
    def __init__(self, lengths_ref):
        self.lengths = [lengths_ref[0, u] for u in range(4)]
        self.ends = []
        end = 0
        for length in self.lengths:
            end = end + length
            self.ends.append(end)

    def segment(self, t):
        return sum(jnp.where(t >= end, 1, 0) for end in self.ends)

    def start(self, t):
        return sum(jnp.where(t >= e, n, 0) for e, n in zip(self.ends, self.lengths))

    def length(self, t):
        out = jnp.where(t >= 0, self.lengths[0], 0)
        for u in range(1, 4):
            out = jnp.where(t >= self.ends[u - 1], self.lengths[u], out)
        return out


VM = pl.BlockSpec(memory_space=pltpu.VMEM)
HB = pl.BlockSpec(memory_space=pl.ANY)
SM = pl.BlockSpec(memory_space=pltpu.SMEM)
Q = 256
KEYS = 768
SCALE = DH**-0.5
PIECE = 80


def layer_kernel(
    ids_ref,
    negs_ref,
    lengths_ref,
    table_hbm,
    w_in_hbm,
    w_out_hbm,
    ids_out,
    rows_out,
    weight_out,
    table_out,
    table_ref,
    request_ref,
    arrived_ref,
    arrived_t_ref,
    hist_back,
    neg_back,
    picked_ref,
    hist_out,
    neg_out,
    hist_in,
    neg_in,
    w_in_ref,
    w_out_ref,
    emb_ref,
    neg_ref,
    unit_ref,
    normed_ref,
    proj_ref,
    slope_ref,
    weights_ref,
    dweights_ref,
    mixed_ref,
    factor_ref,
    gated_ref,
    y_ref,
    y_factor_ref,
    y_unit_ref,
    grown_ref,
    shares_ref,
    total_ref,
    whole_ref,
    drows_ref,
    dgated_ref,
    dgated_land,
    dgated_on,
    dout_part,
    dout_land,
    dout_on,
    demb_ref,
    emb_land,
    emb_on,
    rest_ref,
    dgate_ref,
    dvalue_ref,
    dquery_ref,
    dkey_ref,
    dpre_ref,
    weight_ref,
    weight_in,
    weight_mine,
    weight_sum,
    met_sem,
    load_sems,
    all_send,
    all_recv,
    ring_send,
    ring_recv,
    total_send,
    total_recv,
    keep_sems,
):
    dp, tx = position()
    barrier = pltpu.get_barrier_semaphore()
    greet_planes(barrier, dp, tx)
    loads = [pltpu.make_async_copy(table_hbm, table_ref, load_sems.at[0])]
    for j in range(4):
        loads.append(
            pltpu.make_async_copy(
                w_in_hbm.at[j], w_in_ref.at[:, j * DH : (j + 1) * DH], load_sems.at[1 + j]
            )
        )
    loads.append(
        pltpu.make_async_copy(
            w_out_hbm, w_out_ref.at[pl.ds(pl.multiple_of(tx * DH, DH), DH)], load_sems.at[5]
        )
    )
    for load in loads:
        load.start()

    def ring(i):
        return Ring(dp, tx, ring_send.at[i], ring_recv.at[i])

    right, left, far = ring(0).right, ring(0).left, ring(0).far

    def rows_of(b, n=Q):
        return pl.ds(pl.multiple_of(b * n, n), n)

    ids, negs = ids_ref[...], neg_row(negs_ref)
    holder_h, hits_h, before_h = slots_of(ids)
    holder_n, hits_n, before_n = slots_of(negs)
    wanted = wanted_rows(ids, hits_h, before_h, 0) + wanted_rows(negs, hits_n, before_n, CAP_H)
    pl.semaphore_wait(barrier, 22)
    greet_again(met_sem, dp, tx)
    request_ref[:, 0, :] = wanted.astype(jnp.int32) - 1
    slot_h = holder_h * CAP_H + before_h
    slot_n = holder_n * CAP_N + before_n

    pl.semaphore_wait(met_sem, 7)
    spread_all(request_ref, arrived_ref, 1, all_send.at[0], all_recv.at[0], dp, tx)
    for load in loads:
        load.wait()
    w_outs = Gather(ring(1), w_out_ref, DH)
    w_outs.start()
    slot_h_col, slot_n_col = as_column(slot_h), as_column(slot_n)
    users = Users(lengths_ref)
    wait_rows(arrived_ref, OWNERS - 1, all_recv.at[0])

    arrived = arrived_ref[:, 0, :]
    columns = [arrived[:, k : k + 1] for k in range(CAP_H + CAP_N)]
    gather_rows(table_ref, jnp.concatenate(columns[0:4], axis=0), picked_ref, 0)
    spread_chunks(picked_ref, hist_out, 0, CAP_H)
    spread_all(hist_out, hist_in, 16, all_send.at[1], all_recv.at[1], dp, tx)
    w_outs.forward()
    gather_rows(table_ref, jnp.concatenate(columns[4:8], axis=0), picked_ref, 512)

    wait_rows(hist_in, (OWNERS - 1) * 16, all_recv.at[1])
    emb_ref[rows_of(tx), :] = take_slots(hist_in, slot_h_col, CAP_H)
    hist = Gather(ring(0), emb_ref, Q)
    hist.start()

    def project(b):
        at = rows_of(b)
        normed = normal(emb_ref[at, :].astype(F32))[0].astype(BF)
        normed_ref[at, :] = normed
        pre = mm(normed, w_in_ref[...])
        gate = lax.logistic(pre)
        proj_ref[at, :] = (pre * gate).astype(BF)
        slope_ref[at, :] = gate * (1.0 + pre * (1.0 - gate))

    gather_rows(table_ref, jnp.concatenate(columns[8:12], axis=0), picked_ref, 1024)
    hist.forward()
    spread_chunks(picked_ref, neg_out, 512, CAP_N)
    spread_all(neg_out, neg_in, 16, all_send.at[2], all_recv.at[2], dp, tx)
    project(tx)
    for c in hist.first[2:]:
        c.wait_recv()
    project(left)
    project(right)
    for c in hist.second:
        c.wait_recv()
    project(far)

    arrived_t_ref[...] = jnp.transpose(arrived.astype(F32)).astype(jnp.int32)

    mine = pl.multiple_of(tx * 1024, 1024)

    def keys_of(b):
        low = max(b - 2, 0)
        return slice(low * Q, (b + 1) * Q), low

    def attend(b):
        at = slice(b * Q, (b + 1) * Q)
        kr, low = keys_of(b)
        n = kr.stop - kr.start
        scores = mm_nt(proj_ref[at, 256:384], proj_ref[kr, 384:512]) * SCALE
        t = iota((Q, 1), 0) + b * Q
        s = iota((Q, n), 1) + low * Q
        seen = (s <= t) & (s >= users.start(t))
        share = 1.0 / users.length(t).astype(F32)
        gate = lax.logistic(scores)
        weights = jnp.where(seen, scores * gate * share, 0.0).astype(BF)
        weights_ref[at, 0:n] = weights
        dweights_ref[at, 0:n] = jnp.where(
            seen, gate * (1.0 + scores * (1.0 - gate)) * (share * SCALE), 0.0
        )
        mixed, factor = normal(mm(weights, proj_ref[kr, 128:256]))
        mixed_ref[at, :] = mixed
        factor_ref[at, :] = jnp.broadcast_to(factor, (Q, DH))
        gated_ref[pl.ds(mine + b * Q, Q), :] = (mixed * proj_ref[at, 0:128].astype(F32)).astype(BF)

    gates = Gather(ring(2), gated_ref, 1024)
    attend(0)
    attend(1)
    gates.first[0].start()
    gates.first[3].start()
    attend(2)
    attend(3)
    gates.first[1].start()
    gates.first[2].start()

    wait_rows(neg_in, (OWNERS - 1) * 16, all_recv.at[2])
    neg_ref[...] = take_slots(neg_in, slot_n_col, CAP_N)
    gates.forward()
    neg_f = neg_ref[...].astype(F32)
    neg_factor = unit_factor(neg_f)
    unit_ref[...] = (neg_f * neg_factor).astype(BF)
    w_outs.finish()
    arrived_t_ref[...] = jnp.transpose(arrived.astype(F32)).astype(jnp.int32)

    emb_f = emb_ref[rows_of(tx), :].astype(F32)
    follow = jnp.where(
        iota((Q, 1), 0) == Q - 1,
        emb_ref[rows_of(right), :].astype(F32)[0:1, :],
        pltpu.roll(emb_f, Q - 1, 0),
    )
    follow_factor = unit_factor(follow)
    follow_unit = (follow * follow_factor).astype(BF).astype(F32)
    t_row = iota((1, 1024), 1)
    segment = users.segment(t_row)
    valid = users.segment(t_row + 1) == segment
    users_of = [jnp.where(segment == u, 1.0, 0.0) for u in range(4)]
    gates.arrived(0)

    for b in range(4):
        if b == 2:
            gates.arrived(1)
        at = slice(b * Q, (b + 1) * Q)
        gated = jnp.concatenate(
            [gated_ref[h * 1024 + b * Q : h * 1024 + (b + 1) * Q, :] for h in range(4)], axis=1
        )
        y = emb_ref[at, :].astype(F32) + mm(gated, w_out_ref[...])
        factor = unit_factor(y)
        y_unit = (y * factor).astype(BF)
        y_ref[at, :] = y
        y_factor_ref[at, :] = jnp.broadcast_to(factor, (Q, DH))
        y_unit_ref[at, :] = y_unit
        grown = jnp.exp(sharpness * mm_nt(unit_ref[...], y_unit))
        grown = jnp.concatenate(
            [grown[u * DH : (u + 1) * DH, :] * users_of[u][:, at] for u in range(4)], axis=0
        )
        grown_ref[:, at] = grown
        total_ref[tx, :, at] = jnp.sum(grown, axis=0, keepdims=True)

    y_unit_f = y_unit_ref[rows_of(tx), :].astype(F32)
    grown_pos = jnp.exp(sharpness * row_sum(y_unit_f * follow_unit))
    own_lanes = pl.ds(pl.multiple_of(tx * Q, Q), Q)
    grown_pos_row = jnp.transpose(jnp.broadcast_to(grown_pos, (Q, DH)))[0:1, :]
    total_ref[tx, :, own_lanes] += grown_pos_row
    totals = [
        Ring(dp, tx, total_send, total_recv).copy(total_ref.at[tx], total_ref.at[tx], i, to)
        for i, to in enumerate((right, left, far))
    ]
    for c in totals:
        c.start()
    for c in totals:
        c.wait_recv()
    total = total_ref[0] + total_ref[1] + total_ref[2] + total_ref[3]
    whole_ref[...] = jnp.where(valid, sharpness / total, 0.0)
    scaled_own = jnp.transpose(jnp.broadcast_to(whole_ref[:, own_lanes], (DH, Q)))[:, 0:1]
    d_pos = jnp.where(scaled_own > 0.0, scaled_own * grown_pos - sharpness, 0.0)
    d_unit_pos = d_pos * follow_unit
    gate_sum = Scatter(ring(3), dgated_ref, dgated_land, dgated_on, 1024)
    for b in range(4):
        at = slice(b * Q, (b + 1) * Q)
        shares = (grown_ref[:, at] * whole_ref[:, at]).astype(BF)
        shares_ref[:, at] = shares
        d_unit = mm_tn(shares, unit_ref[...]) + jnp.where(tx == b, d_unit_pos, 0.0)
        d_rows = unit_back(d_unit, y_ref[at, :], y_factor_ref[at, :][:, 0:1])
        drows_ref[at, :] = d_rows
        d_gated = mm_nt(d_rows.astype(BF), w_out_ref[...]).astype(BF)
        for h in range(4):
            dgated_ref[h * 1024 + b * Q : h * 1024 + (b + 1) * Q, :] = d_gated[
                :, h * DH : (h + 1) * DH
            ]
        if b == 1:
            gate_sum.first[0].start()
            gate_sum.first[3].start()
    gate_sum.first[1].start()
    gate_sum.first[2].start()

    d_neg = unit_back(
        mm(shares_ref[...], y_unit_ref[...]),
        neg_ref[...].astype(F32),
        unit_factor(neg_ref[...].astype(F32)),
    )
    wait_rows(neg_out, (OWNERS - 1) * 16, all_send.at[2])
    put_slots(d_neg.astype(BF), slot_n, neg_out, CAP_N)
    gate_sum.forward()
    spread_all(neg_out, neg_back, 16, all_send.at[4], all_recv.at[4], dp, tx)
    for h in range(4):
        dout_part[h * DH : (h + 1) * DH, :] = mm_tn(
            gated_ref[h * 1024 : (h + 1) * 1024, :], drows_ref[...].astype(BF)
        ).astype(BF)
    w_out_sum = Scatter(ring(4), dout_part, dout_land, dout_on, DH)
    w_out_sum.start()
    d_follow = unit_back(d_pos * y_unit_f, follow, follow_factor)
    rest_ref[0:Q, :] = jnp.where(iota((Q, 1), 0) == 0, 0.0, pltpu.roll(d_follow, 1, 0))
    rest_ref[Q : Q + 8, :] = jnp.where(iota((8, 1), 0) == 0, d_follow[Q - 1 : Q, :], 0.0)
    dkey_ref[...] = jnp.zeros_like(dkey_ref)
    dvalue_ref[...] = jnp.zeros_like(dvalue_ref)
    halves = [gate_sum.half(0)]

    def attend_back(b):
        at = slice(b * Q, (b + 1) * Q)
        kr, _ = keys_of(b)
        n = kr.stop - kr.start
        half = halves[b // 2][(b % 2) * Q : (b % 2 + 1) * Q, :]
        d_gated = half + dgated_ref[pl.ds(mine + b * Q, Q), :].astype(F32)
        mixed = mixed_ref[at, :]
        dgate_ref[at, :] = (d_gated * mixed).astype(BF)
        d_mixed = normal_back(
            d_gated * proj_ref[at, 0:128].astype(F32), mixed, factor_ref[at, :][:, 0:1]
        ).astype(BF)
        d_scores = (mm_nt(d_mixed, proj_ref[kr, 128:256]) * dweights_ref[at, 0:n]).astype(BF)
        dquery_ref[at, :] = mm(d_scores, proj_ref[kr, 384:512]).astype(BF)
        dkey_ref[kr, :] += mm_tn(d_scores, proj_ref[at, 256:384])
        dvalue_ref[kr, :] += mm_tn(weights_ref[at, 0:n], d_mixed)

    attend_back(0)
    attend_back(1)
    w_out_sum.forward()
    halves.append(gate_sum.half(1))
    attend_back(2)
    attend_back(3)

    def project_back(b):
        at = rows_of(b)
        d_proj = jnp.concatenate(
            [
                dgate_ref[at, :].astype(F32),
                dvalue_ref[at, :].astype(BF).astype(F32),
                dquery_ref[at, :].astype(F32),
                dkey_ref[at, :].astype(BF).astype(F32),
            ],
            axis=1,
        )
        d_pre = (d_proj * slope_ref[at, :]).astype(BF)
        dpre_ref[at, :] = d_pre
        normed, factor = normal(emb_ref[at, :].astype(F32))
        d_normed = mm_nt(d_pre, w_in_ref[...]).astype(BF).astype(F32)
        return normal_back(d_normed, normed, factor) + drows_ref[at, :]

    emb_sum = Scatter(ring(5), demb_ref, emb_land, emb_on, Q)
    demb_ref[rows_of(far), :] = project_back(far).astype(BF)
    emb_sum.first[0].start()
    emb_sum.first[1].start()
    d_right = project_back(right)
    demb_ref[rows_of(right), :] = (
        d_right + jnp.where(iota((Q, 1), 0) == 0, rest_ref[Q : Q + 1, :], 0.0)
    ).astype(BF)
    emb_sum.first[2].start()
    demb_ref[rows_of(left), :] = project_back(left).astype(BF)
    emb_sum.first[3].start()
    rest_ref[0:Q, :] += project_back(tx)
    emb_sum.forward()

    d_win = mm_tn(normed_ref[...], dpre_ref[...]).astype(BF)
    first, second = w_out_sum.finish()
    d_wout = jnp.concatenate([first, second], axis=0) + dout_part[rows_of(tx, DH), :].astype(F32)
    for j in range(4):
        weight_ref[j * D : (j + 1) * D, :] = d_win[:, j * DH : (j + 1) * DH]
        weight_ref[2048 + j * DH : 2048 + (j + 1) * DH, :] = d_wout[
            :, j * DH : (j + 1) * DH
        ].astype(BF)
    own = pl.ds(pl.multiple_of(dp * PIECE, 16), PIECE)

    def out_piece(pd):
        pltpu.make_async_remote_copy(
            src_ref=weight_ref.at[pl.ds(pl.multiple_of(pd * PIECE, 16), PIECE)],
            dst_ref=weight_in.at[own],
            send_sem=all_send.at[5],
            recv_sem=all_recv.at[5],
            device_id=(pd, tx),
            device_id_type=MESH,
        ).start()

    def back_piece(pd):
        pltpu.make_async_remote_copy(
            src_ref=weight_mine,
            dst_ref=weight_sum.at[own],
            send_sem=all_send.at[6],
            recv_sem=all_recv.at[6],
            device_id=(pd, tx),
            device_id_type=MESH,
        ).start()

    each_dp(dp, tx, out_piece)
    weight_in[own] = weight_ref[own]

    wait_rows(neg_back, (OWNERS - 1) * 16, all_recv.at[4])
    gather_chunks(neg_back, picked_ref, 512, CAP_N)

    keeps = [
        pltpu.make_async_copy(
            table_ref.at[pl.ds(i * 512, 512)], table_out.at[pl.ds(i * 512, 512)], keep_sems.at[i]
        )
        for i in range(8)
    ]

    def add_negatives(i):
        total = put_rows(arrived_t_ref, picked_ref, i * 512, 4, 512)
        total = total + put_rows(arrived_t_ref, picked_ref, i * 512, 8, 512)
        table_ref[i * 512 : (i + 1) * 512, :] = total.astype(BF)
        keeps[i].start()

    for i in range(4):
        add_negatives(i)

    first, second = emb_sum.finish()
    d_hist = rest_ref[0:Q, :] + jnp.concatenate([first, second], axis=0)
    wait_rows(hist_out, (OWNERS - 1) * 16, all_send.at[1])
    put_slots(d_hist.astype(BF), slot_h, hist_out, CAP_H)
    spread_all(hist_out, hist_back, 16, all_send.at[3], all_recv.at[3], dp, tx)

    wait_rows(weight_in, (N_DP - 1) * PIECE, all_recv.at[5])
    total = weight_in[0:PIECE, :].astype(F32)
    for i in range(1, N_DP):
        total = total + weight_in[i * PIECE : (i + 1) * PIECE, :].astype(F32)
    weight_mine[...] = total.astype(BF)
    weight_sum[own] = total.astype(BF)
    each_dp(dp, tx, back_piece)

    for i in range(4, 8):
        add_negatives(i)
    wait_rows(hist_back, (OWNERS - 1) * 16, all_recv.at[3])
    gather_chunks(hist_back, picked_ref, 0, CAP_H)
    wait_rows(weight_sum, (N_DP - 1) * PIECE, all_recv.at[6])
    results = [
        pltpu.make_async_copy(arrived_t_ref, ids_out, load_sems.at[0]),
        pltpu.make_async_copy(picked_ref.at[0:512], rows_out, load_sems.at[1]),
        pltpu.make_async_copy(weight_sum, weight_out, load_sems.at[2]),
    ]
    for move in results:
        move.start()
    for move in results + keeps:
        move.wait()
    for c in totals + hist.first + hist.second:
        c.wait_send()
    gates.sent()
    gate_sum.sent()
    wait_rows(request_ref, OWNERS - 1, all_send.at[0])
    wait_rows(hist_out, (OWNERS - 1) * 16, all_send.at[3])
    wait_rows(neg_out, (OWNERS - 1) * 16, all_send.at[4])
    wait_rows(weight_in, (N_DP - 1) * PIECE, all_send.at[5])
    wait_rows(weight_in, (N_DP - 1) * PIECE, all_send.at[6])


def layer(ids, negs, lengths, table, w_in, w_out):
    sem = pltpu.SemaphoreType.DMA
    vm = pltpu.VMEM
    return pl.pallas_call(
        layer_kernel,
        out_shape=[
            jax.ShapeDtypeStruct((128, 128), jnp.int32),
            jax.ShapeDtypeStruct((CAP_H * OWNERS, D), BF),
            jax.ShapeDtypeStruct((2560, 128), BF),
            jax.ShapeDtypeStruct((ROWS, D), BF),
        ],
        in_specs=[VM, VM, SM, HB, HB, HB],
        out_specs=[HB] * 4,
        scratch_shapes=[
            vm((ROWS, D), BF),
            vm((OWNERS, 1, 128), jnp.int32),
            vm((OWNERS, 1, 128), jnp.int32),
            vm((128, 128), jnp.int32),
            vm((OWNERS * 16, 128), BF),
            vm((OWNERS * 16, 256), BF),
            vm((12 * OWNERS, D), BF),
            vm((OWNERS * 16, 128), BF),
            vm((OWNERS * 16, 256), BF),
            vm((OWNERS * 16, 128), BF),
            vm((OWNERS * 16, 256), BF),
            vm((D, D), BF),
            vm((D, D), BF),
            vm((1024, D), BF),
            vm((512, D), BF),
            vm((512, D), BF),
            vm((1024, D), BF),
            vm((1024, D), BF),
            vm((1024, D), F32),
            vm((1024, KEYS), BF),
            vm((1024, KEYS), F32),
            vm((1024, DH), F32),
            vm((1024, DH), F32),
            vm((4096, DH), BF),
            vm((1024, D), F32),
            vm((1024, DH), F32),
            vm((1024, D), BF),
            vm((512, 1024), F32),
            vm((512, 1024), BF),
            vm((4, 1, 1024), F32),
            vm((1, 1024), F32),
            vm((1024, D), F32),
            vm((4096, DH), BF),
            vm((6 * 512, DH), BF),
            vm((2 * 512, DH), BF),
            vm((D, D), BF),
            vm((6 * 64, D), BF),
            vm((2 * 64, D), BF),
            vm((1024, D), BF),
            vm((6 * 128, D), BF),
            vm((2 * 128, D), BF),
            vm((Q + 8, D), F32),
            vm((1024, DH), BF),
            vm((1024, DH), F32),
            vm((1024, DH), BF),
            vm((1024, DH), F32),
            vm((1024, D), BF),
            vm((2560, 128), BF),
            vm((2560, 128), BF),
            vm((PIECE, 128), BF),
            vm((2560, 128), BF),
            pltpu.SemaphoreType.REGULAR,
            sem((6,)),
            sem((7,)),
            sem((7,)),
            sem((6, 6)),
            sem((6, 6)),
            sem((3,)),
            sem((3,)),
            sem((8,)),
        ],
        compiler_params=pltpu.CompilerParams(
            collective_id=0, has_side_effects=True, vmem_limit_bytes=56 * 1024 * 1024
        ),
        name="layer",
    )(ids, negs, lengths, table, w_in, w_out)


def gather_chunks(chunks_ref, rows_ref, at, cap):
    block = 128 // cap
    many = block * 16
    q, r = iota((128, many), 0), iota((128, many), 1)
    fold = one_zero(
        (lax.rem(q, block) == lax.div(r, 16)) & (lax.div(q, block) == lax.rem(r, cap))
    )
    for b in range(cap):
        wide = unfold(chunks_ref[b * many : (b + 1) * many, :], cap, 16 // cap)
        rows = mm(fold, wide).astype(BF)
        for k in range(cap):
            rows_ref[at + k * 128 + b * block : at + k * 128 + (b + 1) * block, :] = rows[
                k * block : (k + 1) * block
            ]


def put_rows(ids_ref, rows_ref, first, slot, tile):
    row = jnp.concatenate([ids_ref[slot + j : slot + j + 1, :] for j in range(4)], axis=1)
    put = one_zero(row == iota((tile, 512), 0) + first)
    return mm(put, rows_ref[slot * 128 : (slot + 4) * 128, :])


TILES = 8


def add_kernel(
    ids_hbm,
    rows_hbm,
    weight_hbm,
    part_hbm,
    out_hbm,
    w_in_hbm,
    w_out_hbm,
    ids_ref,
    rows_ref,
    weight_ref,
    part_ref,
    out_ref,
    w_in_ref,
    w_out_ref,
    in_sems,
    part_sems,
    out_sems,
    w_sems,
):
    tile = ROWS // TILES
    moves = [
        pltpu.make_async_copy(ids_hbm, ids_ref, in_sems.at[0]),
        pltpu.make_async_copy(rows_hbm, rows_ref, in_sems.at[1]),
        pltpu.make_async_copy(weight_hbm, weight_ref, in_sems.at[2]),
    ]
    parts, outs = [], []
    for i in range(TILES):
        at = pl.ds(i * tile, tile)
        parts.append(pltpu.make_async_copy(part_hbm.at[at], part_ref.at[at], part_sems.at[i]))
        outs.append(pltpu.make_async_copy(out_ref.at[at], out_hbm.at[at], out_sems.at[i]))
    for move in moves + parts:
        move.start()
    moves[0].wait()
    moves[1].wait()
    for i in range(TILES):
        at = pl.ds(i * tile, tile)
        parts[i].wait()
        out_ref[at, :] = part_ref[at, :].astype(F32) + put_rows(ids_ref, rows_ref, i * tile, 0, tile)
        outs[i].start()
    moves[2].wait()
    w_in_ref[...] = weight_ref[0:2048, :].astype(F32)
    w_out_ref[...] = jnp.concatenate(
        [weight_ref[2048 + c * 128 : 2048 + (c + 1) * 128, :] for c in range(4)], axis=1
    ).astype(F32)
    weights = [
        pltpu.make_async_copy(w_in_ref, w_in_hbm, w_sems.at[0]),
        pltpu.make_async_copy(w_out_ref, w_out_hbm, w_sems.at[1]),
    ]
    for move in weights:
        move.start()
    for move in outs + weights:
        move.wait()


def add_rows(ids, rows, weight, part):
    anywhere = pl.BlockSpec(memory_space=pl.ANY)
    sem = pltpu.SemaphoreType.DMA
    return pl.pallas_call(
        add_kernel,
        out_shape=[
            jax.ShapeDtypeStruct((ROWS, D), F32),
            jax.ShapeDtypeStruct((2048, DH), F32),
            jax.ShapeDtypeStruct((DH, D), F32),
        ],
        in_specs=[anywhere] * 4,
        out_specs=[anywhere] * 3,
        scratch_shapes=[
            pltpu.VMEM((128, 128), jnp.int32),
            pltpu.VMEM((CAP_H * OWNERS, D), BF),
            pltpu.VMEM((2560, 128), BF),
            pltpu.VMEM((ROWS, D), BF),
            pltpu.VMEM((ROWS, D), F32),
            pltpu.VMEM((2048, DH), F32),
            pltpu.VMEM((DH, D), F32),
            sem((3,)),
            sem((TILES,)),
            sem((TILES,)),
            sem((2,)),
        ],
        compiler_params=pltpu.CompilerParams(vmem_limit_bytes=56 * 1024 * 1024),
        name="add_rows",
    )(ids, rows, weight, part)


def on_device(table, item_ids, negatives, lengths, w_in, w_out):
    ids, rows, weight, part = layer(item_ids.reshape(1, -1), negatives, lengths, table, w_in, w_out)
    grad_table, grad_w_in, grad_w_out = add_rows(ids, rows, weight, part)
    return (grad_table, grad_w_in.reshape(4, D, DH), grad_w_out)


def solution(mesh):
    placed = (
        P(("dp", "table"), None),
        P(("dp", "table")),
        P("dp", "table"),
        P("dp", None),
        P(None, None, "table"),
        P("table", None),
    )
    return jax.shard_map(
        on_device,
        mesh=mesh,
        in_specs=placed,
        out_specs=(P(("dp", "table"), None), P(None, None, "table"), P("table", None)),
        check_vma=False,
    )
```
